128 devices in a mesh: band: 2 (over x_lo), domain: 64 (over z, y, x_hi, core).
Axes of the slice: x: 4 (x_hi: 2, x_lo: 2; x = x_hi * 2 + x_lo), y: 4, z: 4, core: 2. Of those that a mesh axis runs over, the one named last changes fastest.
Arguments:
- orbitals: float32 [32, 512, 32, 128], P('band', 'domain'), may hold values from -6 to 6
- potential: float32 [512, 32, 128], P('domain'), may hold values from -2 to 1
- earlier: float32 [128, 512, 32, 128], P('band', 'domain'), may hold values from -6 to 6
- incoming: float32 [64, 512, 32, 128], P('band', 'domain'), may hold values from -64 to 64
Outputs:
- applied: float32 [32, 512, 32, 128], P('band', 'domain')
- correlations: float32 [128, 64], P('band')
- orthonormal: float32 [64, 512, 32, 128], P('band', 'domain')
The draws below stay inside these ranges and needn't reach their ends.
All inputs are finite; a program needn't handle non-finite values.
Results may differ from the reference program's by a relative error of at most 0.00015.
Values sent between devices are 32-bit elements; how exact they have to be, the bound alone decides.
A program may use at most 128 MiB of HBM per device.

```python
import jax
import jax.numpy as jnp
from jax import lax

CY = 32
CZ = 128
HALF = 6
ORB = 32
NEW = 64
NPREV = 128
NX = 512


def earlier_values(key):
    base = jax.random.normal(key, (NPREV, NX, CY, CZ), jnp.float32)
    return jnp.clip(base, -6.0, 6.0)


def draw_earlier(key, part):
    return earlier_values(key)


def draw_incoming(key, part):
    prev = earlier_values(key)
    key = jax.random.fold_in(key, 7)
    pick = jax.random.randint(jax.random.fold_in(key, 1), (NEW, 2), 0, NPREV)
    weights = jax.random.uniform(jax.random.fold_in(key, 2), (NEW, 2), jnp.float32, 1.0, 3.0)
    signs = jnp.where(jax.random.randint(jax.random.fold_in(key, 3), (NEW, 2), 0, 2) == 0, -1.0, 1.0)
    weights = weights * signs
    noise = jnp.clip(jax.random.normal(jax.random.fold_in(key, 4), (NEW, NX, CY, CZ), jnp.float32), -6.0, 6.0)
    mixed = noise + 0.5 * jnp.roll(noise, 1, axis=0)
    plane = jnp.arange(NX, dtype=jnp.float32)
    profile = 1.0 + 2.0 * plane / max(NX - 1, 1)
    mixed = mixed * profile[None, :, None, None]
    result = weights[:, 0, None, None, None] * prev[pick[:, 0]] + weights[:, 1, None, None, None] * prev[pick[:, 1]] + mixed
    return jnp.clip(result, -64.0, 64.0)


def levels(stream_key, extent, shards, least, high):
    def one(axis_at, blocks):
        draws = jax.random.uniform(jax.random.fold_in(jax.random.fold_in(stream_key, 6), axis_at), (blocks,), jnp.float32, least / len(shards), high / len(shards))
        return jnp.repeat(jnp.exp(draws), extent[axis_at] // blocks).reshape((-1,) + (1,) * (len(extent) - axis_at - 1))

    level = one(*shards[0])
    for cut in shards[1:]:
        level = level * one(*cut)
    return level


def scatter_about(own_key, extent, deviation, reach, shards=(), held_as=jnp.bfloat16):
    level = levels(own_key, extent, shards, -0.22, 0.18) if shards else 1.0
    drawn = jax.random.normal(own_key, extent, jnp.float32) * deviation * level
    return jnp.minimum(jnp.maximum(drawn, -reach), reach).astype(held_as)


def setup_inputs(seed: int = 0) -> dict:
    streams_of = jax.random.split(jax.random.key(seed), 5)
    orbitals = scatter_about(streams_of[0], (ORB, NX, CY, CZ), 1.0, 6.0, ((0, 2), (1, 64)), jnp.float32)
    potential = jnp.clip(-2.0 + 3.0 * jax.random.uniform(streams_of[1], (NX, CY, CZ), jnp.float32) ** levels(streams_of[1], (NX, CY, CZ), ((0, 64),), -0.2, 0.2), -2.0, 1.0)
    earlier = draw_earlier(jax.random.fold_in(streams_of[4], 71), 0)
    incoming = draw_incoming(jax.random.fold_in(streams_of[4], 71), 0)
    return dict(orbitals=orbitals, potential=potential, earlier=earlier, incoming=incoming)


coeffs = (-5369.0 / 1800.0, 12.0 / 7.0, -15.0 / 56.0, 10.0 / 189.0, -1.0 / 112.0, 2.0 / 1925.0, -1.0 / 16632.0)

def laplace(field):
    total = 3.0 * coeffs[0] * field
    padded = jnp.pad(field, ((0, 0), (0, 0), (HALF, HALF), (HALF, HALF)))
    width_y = field.shape[2]
    width_z = field.shape[3]
    for step in range(1, HALF + 1):
        total = total + coeffs[step] * (jnp.roll(field, step, axis=1) + jnp.roll(field, -step, axis=1))
        total = total + coeffs[step] * (padded[:, :, HALF + step:HALF + step + width_y, HALF:HALF + width_z] + padded[:, :, HALF - step:HALF - step + width_y, HALF:HALF + width_z])
        total = total + coeffs[step] * (padded[:, :, HALF:HALF + width_y, HALF + step:HALF + step + width_z] + padded[:, :, HALF:HALF + width_y, HALF - step:HALF - step + width_z])
    return total

def reference(orbitals, potential, earlier, incoming):
    applied = -0.5 * laplace(orbitals) + potential[None] * orbitals
    ncells = NX * CY * CZ
    prev_flat = earlier.reshape(NPREV, -1)
    new_flat = incoming.reshape(NEW, -1)
    high = lax.Precision.HIGHEST
    correlations = jnp.dot(prev_flat.astype(jnp.float32), new_flat.T.astype(jnp.float32), precision=high, preferred_element_type=jnp.float32) / ncells
    cleaned = new_flat - jnp.dot(correlations.T.astype(jnp.float32), prev_flat.astype(jnp.float32), precision=high, preferred_element_type=jnp.float32)
    gram = jnp.dot(cleaned.astype(jnp.float32), cleaned.T.astype(jnp.float32), precision=high, preferred_element_type=jnp.float32) / ncells
    factor = jnp.linalg.cholesky(gram)
    inverse = jax.scipy.linalg.solve_triangular(factor, jnp.eye(NEW, dtype=jnp.float32), lower=True)
    orthonormal = jnp.dot(inverse.astype(jnp.float32), cleaned.astype(jnp.float32), precision=high, preferred_element_type=jnp.float32)
    return (applied, correlations, orthonormal.reshape(NEW, NX, CY, CZ))
```

```python
import jax
import jax.numpy as jnp
from jax import lax
from jax.experimental import pallas as pl
from jax.experimental.pallas import tpu as pltpu
from jax.sharding import PartitionSpec as P

coeffs = (
    -5369.0 / 1800.0,
    12.0 / 7.0,
    -15.0 / 56.0,
    10.0 / 189.0,
    -1.0 / 112.0,
    2.0 / 1925.0,
    -1.0 / 16632.0,
)

MESH = pl.DeviceIdType.MESH
HIGH = lax.Precision.HIGHEST
F32 = jnp.float32
BF16 = jnp.bfloat16

ORB = 16
PREV = 64
NEW = 32
PLANES = 8
KEPT = 4
CY = 32
CZ = 128
DEPTH = 6
ROWS = 2 * PREV + 2 * NEW
CELLS = KEPT * CY * CZ
TOTAL = 512 * CY * CZ

CHUNKS = 16
CHUNK_Y = KEPT * CY // CHUNKS
AHEAD = 2
NEAR = -(-ORB // (CHUNKS - 1))
PIECES = 2
TILES = 16
TILE_Y = KEPT * CY // TILES


def nt(a, b, precision=None):
    return lax.dot_general(
        a, b, (((1,), (1,)), ((), ())), precision=precision, preferred_element_type=F32
    )


def nn(a, b, precision=None):
    return lax.dot_general(
        a, b, (((1,), (0,)), ((), ())), precision=precision, preferred_element_type=F32
    )


def split(a):
    hi = a.astype(BF16)
    return hi, (a - hi.astype(F32)).astype(BF16)


def band_matrix(size, block, diagonal):
    i = lax.broadcasted_iota(jnp.int32, (size, size), 0)
    j = lax.broadcasted_iota(jnp.int32, (size, size), 1)
    gap = jnp.abs(i - j)
    out = jnp.where(gap == 0, diagonal, 0.0).astype(F32)
    for step in range(1, DEPTH + 1):
        out = jnp.where(gap == step, -0.5 * coeffs[step], out)
    if block != size:
        out = jnp.where(i // block == j // block, out, 0.0)
    return out


def kernel(
    orb, pot, earl, inc,
    applied, corr, ortho,
    to_give, rows, high, low, ext, potv, relay, grams, red,
    got_z, sum_z, got_y, part, twin_part, pair, got_x, whole_y, whole, work, factor, outs, band_z, band_y,
    s1, r1, l1, l0,
    s_in, r_in, s_out, r_relay, s_fwd, r_out,
    sz, rz, sy, ry, s_twin, r_twin, sx, rx, sgy, rgy, sgz, rgz,
    s2, r2, go, all_in,
):
    band = lax.axis_index("band")
    domain = lax.axis_index("domain")
    core = domain % 2
    x = ((domain // 2) % 2) * 2 + band
    y = (domain // 4) % 4
    z = domain // 16
    other = 1 - band

    def device(xx, yy, zz, cc):
        return (xx % 2, ((zz * 4 + yy) * 2 + xx // 2) * 2 + cc)

    z_peers = [device(x, y, (z + d) % 4, core) for d in range(1, 4)]
    y_peers = [device(x, (y + d) % 4, z, core) for d in range(1, 4)]
    partner = (other, domain)
    twin = (band, domain + 1 - 2 * core)
    toward = 2 * core - 1
    early = (band + core + 1) % 2
    next_domain = (domain + toward + 64) % 64
    via_y = early * ((next_domain // 4) % 4) + (1 - early) * y
    via_z = early * (next_domain // 16) + (1 - early) * z
    relayer = device((x + toward + 4) % 4, via_y, via_z, 1 - core)
    from_domain = ((z * 4 + y) * 2 + ((x + toward + 4) % 4) // 2) * 2 + 1 - core
    straight = ((z * 4 + y) * 2 + ((x - toward + 4) % 4) // 2) * 2 + core
    to_domain = (early * straight + (1 - early) * (from_domain - toward) + 64) % 64
    forward = (other, to_domain)
    way = 2 * band - 1
    chip = (z * 4 + y) * 2
    to = (chip + x // 2) * 2 + band + way + 64
    to = to % 64
    chip_passer = device(
        (((to // 2) % 2) * 2 + band - way + 4) % 4, (to // 4) % 4, to // 16, 1
    )
    giver_domain = ((chip + ((x - way + 4) % 4) // 2) * 2 + band + way + 64) % 64
    chip_giver = (other, giver_domain - giver_domain % 2 + 1)
    early = early == 1

    def piece(k):
        plane = k // (CY // CHUNK_Y)
        return plane, pl.ds(pl.multiple_of((k % (CY // CHUNK_Y)) * CHUNK_Y, CHUNK_Y), CHUNK_Y)

    def stage(k):
        plane, at = piece(k)
        return (
            pltpu.make_async_copy(
                earl.at[:, KEPT * other + plane, at], to_give.at[0:PREV, plane, at], l1.at[k, 0]
            ),
            pltpu.make_async_copy(
                inc.at[:, KEPT * other + plane, at], to_give.at[PREV:, plane, at], l1.at[k, 1]
            ),
        )

    def stage_all(k, _):
        for copy in stage(k):
            copy.start()
        return 0

    barrier = pltpu.get_barrier_semaphore()
    first, second = core == 0, core == 1

    def greet(peer):
        pl.semaphore_signal(barrier, inc=1, device_id=peer, device_id_type=MESH)

    def tell(semaphore):
        pl.semaphore_signal(semaphore, inc=1, device_id=twin, device_id_type=MESH)

    @pl.when(second)
    def _():
        greet(twin)
        greet((other, domain - 1))

    @pl.when(first)
    def _():
        greet(partner)

    lax.fori_loop(0, CHUNKS, stage_all, 0)

    @pl.when(first)
    def _():
        pl.semaphore_wait(barrier, 3)
        tell(go)

    @pl.when(second)
    def _():
        pl.semaphore_wait(go, 1)

    def remote(src, dst, send, recv, peer):
        return pltpu.make_async_remote_copy(
            src_ref=src, dst_ref=dst, send_sem=send, recv_sem=recv,
            device_id=peer, device_id_type=MESH,
        )

    def give(k):
        plane, at = piece(k)
        return (
            remote(
                to_give.at[0:PREV, plane, at],
                rows.at[pl.ds(PREV * band, PREV), plane, at],
                s1.at[k, 0], r1.at[k, 0], partner,
            ),
            remote(
                to_give.at[PREV:, plane, at],
                rows.at[pl.ds(2 * PREV + NEW * band, NEW), plane, at],
                s1.at[k, 1], r1.at[k, 1], partner,
            ),
        )

    for k in range(AHEAD):
        for copy in stage(k):
            copy.wait()
        for copy in give(k):
            copy.start()

    @pl.when(second)
    def _():
        for d in range(1, 4):
            greet(device(x, y, (z + d) % 4, 1))
            greet(device(x, (y + d) % 4, z, 1))
            greet(device((x + d) % 4, y, z, 1))
        greet(chip_passer)
        greet(chip_giver)

    inner = remote(
        orb.at[:, pl.ds(2 * (1 - core), DEPTH)], ext.at[:, pl.ds(14 * core, DEPTH)],
        s_in, r_in, twin,
    )
    outer, passed = [], []
    for n in range(PIECES):
        some = pl.ds(n * (ORB // PIECES), ORB // PIECES)
        outer.append(
            remote(
                orb.at[some, pl.ds(2 * core, DEPTH)], relay.at[some],
                s_out.at[n], r_relay.at[n], relayer,
            )
        )
        passed.append(
            remote(
                relay.at[some], ext.at[some, pl.ds(14 * core, DEPTH)],
                s_fwd.at[n], r_out.at[n], forward,
            )
        )

    locals_ = [
        pltpu.make_async_copy(orb, ext.at[:, pl.ds(DEPTH, PLANES)], l0.at[0]),
        pltpu.make_async_copy(pot, potv, l0.at[1]),
        pltpu.make_async_copy(
            earl.at[:, pl.ds(KEPT * band, KEPT)], rows.at[pl.ds(PREV * band, PREV)], l0.at[2]
        ),
        pltpu.make_async_copy(
            inc.at[:, pl.ds(KEPT * band, KEPT)],
            rows.at[pl.ds(2 * PREV + NEW * band, NEW)], l0.at[3],
        ),
    ]
    for copy in locals_:
        copy.start()
    inner.start()

    band_z[...] = band_matrix(CZ, CZ, -1.5 * coeffs[0])
    band_y[...] = band_matrix(PLANES * CY, CY, 0.0)
    for copy in locals_:
        copy.wait()

    def near(o, _):
        cells = ext[o, DEPTH : DEPTH + PLANES].reshape(PLANES * CY, CZ)
        field = potv[...].reshape(PLANES * CY, CZ)
        total = field * cells + nn(cells, band_z[...], HIGH) + nn(band_y[...], cells, HIGH)
        applied[o] = total.reshape(PLANES, CY, CZ)
        return 0

    grams[...] = jnp.zeros_like(grams)
    flat_rows = rows.reshape(ROWS * KEPT * CY, CZ)

    def take(k, _):
        for copy in give(k):
            copy.wait_recv()
        for copy in give(k):
            copy.wait_send()

        @pl.when(k + AHEAD < CHUNKS)
        def _():
            for copy in stage(k + AHEAD):
                copy.wait()
            for copy in give(k + AHEAD):
                copy.start()

        @pl.when(jnp.logical_and(k == 2, second))
        def _():
            pl.semaphore_wait(barrier, 11)
            tell(all_in)

        @pl.when(jnp.logical_and(k == 2, first))
        def _():
            pl.semaphore_wait(all_in, 1)

        @pl.when(jnp.logical_and(k == 2, early))
        def _():
            for copy in outer:
                copy.start()

        @pl.when(jnp.logical_and(k == CHUNKS - 1, jnp.logical_not(early)))
        def _():
            for copy in outer:
                copy.start()

        base = pl.multiple_of(k * CHUNK_Y, CHUNK_Y)
        for i in range(CHUNK_Y):
            hi, lo = split(flat_rows[pl.ds(base + i, ROWS, stride=KEPT * CY), :])
            at = pl.ds(pl.multiple_of((base + i) * CZ, CZ), CZ)
            high[:, at] = hi
            low[:, at] = lo
        at = pl.ds(pl.multiple_of(base * CZ, CHUNK_Y * CZ), CHUNK_Y * CZ)
        hi, lo = high[:, at], low[:, at]
        grams[...] += nt(hi, hi) + nt(hi, lo) + nt(lo, hi)

        @pl.when(k < CHUNKS - 1)
        def _():
            lax.fori_loop(k * NEAR, jnp.minimum((k + 1) * NEAR, ORB), near, 0)

        return 0

    lax.fori_loop(0, CHUNKS, take, 0)

    red[0:ROWS, :] = grams[:, 0 : 2 * PREV]
    red[ROWS:, :] = jnp.zeros((2 * NEW, 2 * PREV), F32)
    red[ROWS:, 0 : 2 * NEW] = grams[2 * PREV :, 2 * PREV :]

    sent = []
    def quarter(size, index):
        return pl.ds(pl.multiple_of(size * index, size), size)

    copies = [
        remote(
            red.at[quarter(64, (z + d) % 4)], got_z.at[d - 1],
            sz.at[d - 1], rz.at[d - 1], z_peers[d - 1],
        )
        for d in range(1, 4)
    ]
    for copy in copies:
        copy.start()
    for copy in copies:
        copy.wait_recv()
    sent = sent + copies
    sum_z[...] = red[quarter(64, z)] + got_z[0] + got_z[1] + got_z[2]
    copies = [
        remote(
            sum_z.at[quarter(16, (y + d) % 4)], got_y.at[d - 1],
            sy.at[d - 1], ry.at[d - 1], y_peers[d - 1],
        )
        for d in range(1, 4)
    ]
    for copy in copies:
        copy.start()
    for copy in copies:
        copy.wait_recv()
    sent = sent + copies
    part[...] = sum_z[quarter(16, y)] + got_y[0] + got_y[1] + got_y[2]
    to_twin = remote(part, twin_part, s_twin, r_twin, twin)
    along_x = [
        remote(
            pair, got_x.at[x], sx.at[2 * d + c], rx.at[d],
            device((x + d + 1) % 4, y, z, c),
        )
        for d in range(3)
        for c in range(2)
    ]
    back = remote(pair, got_x.at[x], sx.at[6], rx.at[3], twin)

    @pl.when(jnp.logical_not(early))
    def _():
        to_twin.start()

    @pl.when(early)
    def _():
        to_twin.wait_recv()
        pair[...] = part[...] + twin_part[...]
        for copy in along_x:
            copy.start()
        back.start()
        for n in range(PIECES):
            outer[n].wait_recv()
            passed[n].start()
        got_x[x] = pair[...]

    @pl.when(jnp.logical_not(early))
    def _():
        back.wait_recv()

    for copy in along_x[::2]:
        copy.wait_recv()
    total = got_x[0]
    for d in range(1, 4):
        total = total + got_x[d]
    whole_y[quarter(16, y)] = total * (1.0 / TOTAL)
    copies = [
        remote(
            whole_y.at[quarter(16, y)], whole_y.at[quarter(16, y)],
            sgy.at[d - 1], rgy.at[d - 1], y_peers[d - 1],
        )
        for d in range(1, 4)
    ]
    for copy in copies:
        copy.start()
    for copy in copies:
        copy.wait_recv()
    sent = sent + copies
    whole[quarter(64, z)] = whole_y[...]
    copies = [
        remote(
            whole_y, whole.at[quarter(64, z)], sgz.at[d - 1], rgz.at[d - 1], z_peers[d - 1]
        )
        for d in range(1, 4)
    ]
    for copy in copies:
        copy.start()
    for copy in copies:
        copy.wait_recv()
    sent = sent + copies

    corr_t = whole[2 * PREV : 2 * PREV + 2 * NEW]
    i = lax.broadcasted_iota(jnp.int32, (128, 128), 0)
    j = lax.broadcasted_iota(jnp.int32, (128, 128), 1)
    middle = whole[0 : 2 * PREV] - jnp.where(i == j, 2.0, 0.0)
    gram = whole[ROWS:, 0 : 2 * NEW] + nt(nn(corr_t, middle, HIGH), corr_t, HIGH)
    i = lax.broadcasted_iota(jnp.int32, (64, 128), 0)
    j = lax.broadcasted_iota(jnp.int32, (64, 128), 1)
    factor[...] = jnp.where(j == i + 64, 1.0, 0.0)
    factor[:, 0:64] = gram

    both = factor[...]
    for first in range(0, 64, 4):
        columns = [
            jnp.broadcast_to(both[:, first + n : first + n + 1], (64, 128)) for n in range(4)
        ]
        for n in range(4):
            step = first + n
            pivot = 1.0 / columns[n][step : step + 1]
            below = jnp.where(i > step, columns[n] * pivot, 0.0)
            both = both - below * both[step : step + 1]
            for m in range(n + 1, 4):
                columns[m] = columns[m] - below * columns[m][step : step + 1]
    pivots = jnp.sum(jnp.where(i == j, both, 0.0), axis=1, keepdims=True)
    root = lax.rsqrt(pivots)
    root = root * (1.5 - 0.5 * pivots * root * root)
    factor[...] = both * root
    inverse = factor[:, 64:128]
    inverse_hi, inverse_lo = split(inverse)
    corr_hi, corr_lo = split(corr_t)
    work[0:64] = -(
        nn(inverse_hi, corr_hi) + (nn(inverse_hi, corr_lo) + nn(inverse_lo, corr_hi))
    )
    theirs, own = pl.ds(NEW * other, NEW), pl.ds(NEW * band, NEW)
    prev_hi, prev_lo = split(jnp.concatenate([work[theirs], work[own]], axis=0))
    new_hi, new_lo = split(
        jnp.concatenate([factor[theirs, 64:128], factor[own, 64:128]], axis=0)
    )
    hi = jnp.concatenate([prev_hi, new_hi], axis=1)
    lo = jnp.concatenate([prev_lo, new_lo], axis=1)
    stacked = jnp.concatenate([hi, lo], axis=0)

    flat_outs = outs.reshape(NEW * KEPT * CY, CZ)
    flat_ortho = ortho.reshape(NEW * PLANES * CY, CZ)
    kept = pl.multiple_of(band * (KEPT * CY), KEPT * CY)

    def tile(k):
        return k // (CY // TILE_Y), pl.ds(
            pl.multiple_of((k % (CY // TILE_Y)) * TILE_Y, TILE_Y), TILE_Y
        )

    def send_new(k):
        plane, at = tile(k)
        return remote(
            outs.at[:, plane, at],
            ortho.at[:, KEPT * band + plane, at],
            s2.at[k], r2.at[k], partner,
        )

    def make(k, _):
        base = pl.multiple_of(k * TILE_Y, TILE_Y)
        at = pl.ds(pl.multiple_of(base * CZ, TILE_Y * CZ), TILE_Y * CZ)
        both = nn(stacked, high[:, at])
        total = both[0:64] + both[64:128] + nn(hi, low[:, at])
        for n in range(TILE_Y):
            at = slice(n * CZ, (n + 1) * CZ)
            flat_outs[pl.ds(base + n, NEW, stride=KEPT * CY), :] = total[:NEW, at]
            flat_ortho[pl.ds(kept + base + n, NEW, stride=PLANES * CY), :] = total[NEW:, at]
        send_new(k).start()

        @pl.when(jnp.logical_and(k == 3, jnp.logical_not(early)))
        def _():
            for n in range(PIECES):
                outer[n].wait_recv()
                passed[n].start()

        return 0

    lax.fori_loop(0, TILES, make, 0)

    work[...] = whole[2 * PREV :].T
    corr[...] = work[pl.ds(pl.multiple_of(PREV * band, PREV), PREV), 0 : 2 * NEW]

    inner.wait()
    for copy in passed:
        copy.wait_recv()

    def far(o, _):
        for p in range(PLANES):
            total = applied[o, p]
            for step in range(1, DEPTH + 1):
                total = total - (0.5 * coeffs[step]) * (
                    ext[o, p + DEPTH + step] + ext[o, p + DEPTH - step]
                )
            applied[o, p] = total
        return 0

    lax.fori_loop(0, ORB, far, 0)
    for copy in sent + outer + passed:
        copy.wait_send()

    @pl.when(early)
    def _():
        for copy in along_x + [back]:
            copy.wait_send()

    @pl.when(jnp.logical_not(early))
    def _():
        to_twin.wait_send()


    def finish(k, _):
        send_new(k).wait()
        return 0

    lax.fori_loop(0, TILES, finish, 0)


def hand_over(a, b, c, a_out, b_out, c_out, sems):
    copies = []
    for n in range(2):
        part = pl.ds(n * (ORB // 2), ORB // 2)
        copies.append(pltpu.make_async_copy(a.at[part], a_out.at[part], sems.at[n]))
    for n in range(4):
        part = pl.ds(n * (NEW // 4), NEW // 4)
        copies.append(pltpu.make_async_copy(c.at[part], c_out.at[part], sems.at[2 + n]))
    copies.append(pltpu.make_async_copy(b, b_out, sems.at[6]))
    for copy in copies:
        copy.start()
    for copy in copies:
        copy.wait()


def on_device(orbitals, potential, earlier, incoming):
    dma = pltpu.SemaphoreType.DMA
    any_ = pl.BlockSpec(memory_space=pl.ANY)
    shapes = (
        jax.ShapeDtypeStruct(orbitals.shape, F32),
        jax.ShapeDtypeStruct((PREV, 2 * NEW), F32),
        jax.ShapeDtypeStruct(incoming.shape, F32),
    )
    held = tuple(pltpu.VMEM(shape.shape, shape.dtype) for shape in shapes)
    in_vmem = pl.BlockSpec(memory_space=pltpu.VMEM)
    arguments = [
        pltpu.with_memory_space_constraint(a, pltpu.HBM)
        for a in (orbitals, potential, earlier, incoming)
    ]
    results = pl.pallas_call(
        kernel,
        out_shape=held,
        in_specs=[any_] * 4,
        out_specs=(in_vmem,) * 3,
        scratch_shapes=[
            pltpu.VMEM((PREV + NEW, KEPT, CY, CZ), F32),
            pltpu.VMEM((ROWS, KEPT, CY, CZ), F32),
            pltpu.VMEM((ROWS, CELLS), BF16),
            pltpu.VMEM((ROWS, CELLS), BF16),
            pltpu.VMEM((ORB, PLANES + 2 * DEPTH, CY, CZ), F32),
            pltpu.VMEM((PLANES, CY, CZ), F32),
            pltpu.VMEM((ORB, DEPTH, CY, CZ), F32),
            pltpu.VMEM((ROWS, ROWS), F32),
            pltpu.VMEM((256, 128), F32),
            pltpu.VMEM((3, 64, 128), F32),
            pltpu.VMEM((64, 128), F32),
            pltpu.VMEM((3, 16, 128), F32),
            pltpu.VMEM((16, 128), F32),
            pltpu.VMEM((16, 128), F32),
            pltpu.VMEM((16, 128), F32),
            pltpu.VMEM((4, 16, 128), F32),
            pltpu.VMEM((64, 128), F32),
            pltpu.VMEM((256, 128), F32),
            pltpu.VMEM((128, 128), F32),
            pltpu.VMEM((64, 128), F32),
            pltpu.VMEM((NEW, KEPT, CY, CZ), F32),
            pltpu.VMEM((CZ, CZ), F32),
            pltpu.VMEM((PLANES * CY, PLANES * CY), F32),
            dma((CHUNKS, 2)), dma((CHUNKS, 2)), dma((CHUNKS, 2)), dma((4,)),
            dma, dma, dma((PIECES,)), dma((PIECES,)), dma((PIECES,)), dma((PIECES,)),
            dma((3,)), dma((3,)), dma((3,)), dma((3,)), dma, dma, dma((7,)), dma((4,)),
            dma((3,)), dma((3,)), dma((3,)), dma((3,)),
            dma((TILES,)), dma((TILES,)),
            pltpu.SemaphoreType.REGULAR, pltpu.SemaphoreType.REGULAR,
        ],
        compiler_params=pltpu.CompilerParams(
            collective_id=0, has_side_effects=True, vmem_limit_bytes=50 * 2**20
        ),
        cost_estimate=pl.CostEstimate(
            flops=6 * 10**9, bytes_accessed=22 * 10**6, transcendentals=0
        ),
    )(*arguments)
    return pl.pallas_call(
        hand_over,
        out_shape=shapes,
        in_specs=[any_] * 3,
        out_specs=(any_,) * 3,
        scratch_shapes=[dma((7,))],
        compiler_params=pltpu.CompilerParams(vmem_limit_bytes=50 * 2**20),
        cost_estimate=pl.CostEstimate(flops=0, bytes_accessed=13 * 10**6, transcendentals=0),
    )(*[pltpu.with_memory_space_constraint(a, pltpu.VMEM) for a in results])


def solution(mesh):
    in_specs = (
        P("band", "domain", None, None),
        P("domain", None, None),
        P("band", "domain", None, None),
        P("band", "domain", None, None),
    )
    out_specs = (P("band", "domain", None, None), P("band", None), P("band", "domain", None, None))
    return jax.shard_map(
        on_device, mesh=mesh, in_specs=in_specs, out_specs=out_specs, check_vma=False
    )
```

```python
import jax
import jax.numpy as jnp
from jax import lax
from jax.experimental import pallas as pl
from jax.experimental.pallas import tpu as pltpu
from jax.sharding import PartitionSpec as P

coeffs = (
    -5369.0 / 1800.0,
    12.0 / 7.0,
    -15.0 / 56.0,
    10.0 / 189.0,
    -1.0 / 112.0,
    2.0 / 1925.0,
    -1.0 / 16632.0,
)

MESH = pl.DeviceIdType.MESH
HIGH = lax.Precision.HIGHEST
F32 = jnp.float32
BF16 = jnp.bfloat16

ORB = 16
PREV = 64
NEW = 32
PLANES = 8
KEPT = 4
CY = 32
CZ = 128
DEPTH = 6
ROWS = 2 * PREV + 2 * NEW
HALF_ROWS = PREV + NEW
ORDER = (
    (0, PREV, 0),
    (HALF_ROWS, PREV, PREV),
    (PREV, NEW, 2 * PREV),
    (HALF_ROWS + PREV, NEW, 2 * PREV + NEW),
)
CELLS = KEPT * CY * CZ
TOTAL = 512 * CY * CZ

CHUNKS = 16
CHUNK_Y = KEPT * CY // CHUNKS
AHEAD = 2
NEAR = -(-ORB // (CHUNKS - 1))
PIECES = 2
TILES = 16
TILE_Y = KEPT * CY // TILES


def nt(a, b, precision=None):
    return lax.dot_general(
        a, b, (((1,), (1,)), ((), ())), precision=precision, preferred_element_type=F32
    )


def nn(a, b, precision=None):
    return lax.dot_general(
        a, b, (((1,), (0,)), ((), ())), precision=precision, preferred_element_type=F32
    )


def split(a):
    hi = a.astype(BF16)
    return hi, (a - hi.astype(F32)).astype(BF16)


def band_matrix(size, block, diagonal):
    i = lax.broadcasted_iota(jnp.int32, (size, size), 0)
    j = lax.broadcasted_iota(jnp.int32, (size, size), 1)
    gap = jnp.abs(i - j)
    out = jnp.where(gap == 0, diagonal, 0.0).astype(F32)
    for step in range(1, DEPTH + 1):
        out = jnp.where(gap == step, -0.5 * coeffs[step], out)
    if block != size:
        out = jnp.where(i // block == j // block, out, 0.0)
    return out


def kernel(
    orb, pot, earl, inc,
    applied, corr, ortho,
    to_give, rows, high, low, ext, potv, relay, grams, red,
    got_z, sum_z, got_y, part, twin_part, pair, got_x, whole_y, whole, work, factor, outs, band_z, band_y,
    s1, r1, l1, l2, l0,
    s_in, r_in, s_out, r_relay, s_fwd, r_out,
    sz, rz, sy, ry, s_twin, r_twin, sx, rx, sgy, rgy, sgz, rgz,
    s2, r2, go, all_in,
):
    band = lax.axis_index("band")
    domain = lax.axis_index("domain")
    core = domain % 2
    x = ((domain // 2) % 2) * 2 + band
    y = (domain // 4) % 4
    z = domain // 16
    other = 1 - band

    def device(xx, yy, zz, cc):
        return (xx % 2, ((zz * 4 + yy) * 2 + xx // 2) * 2 + cc)

    z_peers = [device(x, y, (z + d) % 4, core) for d in range(1, 4)]
    y_peers = [device(x, (y + d) % 4, z, core) for d in range(1, 4)]
    partner = (other, domain)
    twin = (band, domain + 1 - 2 * core)
    toward = 2 * core - 1
    early = (band + core + 1) % 2
    next_domain = (domain + toward + 64) % 64
    via_y = early * ((next_domain // 4) % 4) + (1 - early) * y
    via_z = early * (next_domain // 16) + (1 - early) * z
    relayer = device((x + toward + 4) % 4, via_y, via_z, 1 - core)
    from_domain = ((z * 4 + y) * 2 + ((x + toward + 4) % 4) // 2) * 2 + 1 - core
    straight = ((z * 4 + y) * 2 + ((x - toward + 4) % 4) // 2) * 2 + core
    to_domain = (early * straight + (1 - early) * (from_domain - toward) + 64) % 64
    forward = (other, to_domain)
    way = 2 * band - 1
    chip = (z * 4 + y) * 2
    to = (chip + x // 2) * 2 + band + way + 64
    to = to % 64
    chip_passer = device(
        (((to // 2) % 2) * 2 + band - way + 4) % 4, (to // 4) % 4, to // 16, 1
    )
    giver_domain = ((chip + ((x - way + 4) % 4) // 2) * 2 + band + way + 64) % 64
    chip_giver = (other, giver_domain - giver_domain % 2 + 1)
    early = early == 1

    def piece(planes, k):
        plane = planes + k // (CY // CHUNK_Y)
        at = pl.multiple_of((k % (CY // CHUNK_Y)) * CHUNK_Y, CHUNK_Y)
        return plane, pl.ds(at, CHUNK_Y)

    def stage(k):
        plane, at = piece(KEPT * other, k)
        return (
            pltpu.make_async_copy(earl.at[:, plane, at], to_give.at[k, 0:PREV], l1.at[k, 0]),
            pltpu.make_async_copy(inc.at[:, plane, at], to_give.at[k, PREV:], l1.at[k, 1]),
        )

    def own(k):
        plane, at = piece(KEPT * band, k)
        return (
            pltpu.make_async_copy(
                earl.at[:, plane, at], rows.at[k, pl.ds(HALF_ROWS * band, PREV)], l2.at[k, 0]
            ),
            pltpu.make_async_copy(
                inc.at[:, plane, at], rows.at[k, pl.ds(HALF_ROWS * band + PREV, NEW)], l2.at[k, 1]
            ),
        )

    for k in range(AHEAD):
        for copy in stage(k):
            copy.start()

    barrier = pltpu.get_barrier_semaphore()
    first, second = core == 0, core == 1

    def greet(peer):
        pl.semaphore_signal(barrier, inc=1, device_id=peer, device_id_type=MESH)

    def tell(semaphore):
        pl.semaphore_signal(semaphore, inc=1, device_id=twin, device_id_type=MESH)

    @pl.when(second)
    def _():
        greet(twin)
        greet((other, domain - 1))

    @pl.when(first)
    def _():
        greet(partner)

    @pl.when(first)
    def _():
        pl.semaphore_wait(barrier, 3)
        tell(go)

    @pl.when(second)
    def _():
        pl.semaphore_wait(go, 1)

    def remote(src, dst, send, recv, peer):
        return pltpu.make_async_remote_copy(
            src_ref=src, dst_ref=dst, send_sem=send, recv_sem=recv,
            device_id=peer, device_id_type=MESH,
        )

    def give(k):
        return remote(
            to_give.at[k], rows.at[k, pl.ds(HALF_ROWS * band, HALF_ROWS)],
            s1.at[k], r1.at[k], partner,
        )

    for k in range(AHEAD):
        for copy in stage(k):
            copy.wait()
        give(k).start()

    def fetch(k, _):
        for copy in own(k):
            copy.start()

        @pl.when(k + AHEAD < CHUNKS)
        def _():
            for copy in stage(k + AHEAD):
                copy.start()

        return 0

    @pl.when(second)
    def _():
        for d in range(1, 4):
            greet(device(x, y, (z + d) % 4, 1))
            greet(device(x, (y + d) % 4, z, 1))
            greet(device((x + d) % 4, y, z, 1))
        greet(chip_passer)
        greet(chip_giver)

    inner = remote(
        orb.at[:, pl.ds(2 * (1 - core), DEPTH)], ext.at[:, pl.ds(14 * core, DEPTH)],
        s_in, r_in, twin,
    )
    outer, passed = [], []
    for n in range(PIECES):
        some = pl.ds(n * (ORB // PIECES), ORB // PIECES)
        outer.append(
            remote(
                orb.at[some, pl.ds(2 * core, DEPTH)], relay.at[some],
                s_out.at[n], r_relay.at[n], relayer,
            )
        )
        passed.append(
            remote(
                relay.at[some], ext.at[some, pl.ds(14 * core, DEPTH)],
                s_fwd.at[n], r_out.at[n], forward,
            )
        )

    locals_ = [
        pltpu.make_async_copy(orb, ext.at[:, pl.ds(DEPTH, PLANES)], l0.at[0]),
        pltpu.make_async_copy(pot, potv, l0.at[1]),
    ]
    for copy in locals_:
        copy.start()
    lax.fori_loop(0, CHUNKS, fetch, 0)
    inner.start()

    band_z[...] = band_matrix(CZ, CZ, -1.5 * coeffs[0])
    band_y[...] = band_matrix(PLANES * CY, CY, 0.0)
    for copy in locals_:
        copy.wait()

    def near(o, _):
        cells = ext[o, DEPTH : DEPTH + PLANES].reshape(PLANES * CY, CZ)
        field = potv[...].reshape(PLANES * CY, CZ)
        total = field * cells + nn(cells, band_z[...], HIGH) + nn(band_y[...], cells, HIGH)
        applied[o] = total.reshape(PLANES, CY, CZ)
        return 0

    grams[...] = jnp.zeros_like(grams)
    flat_rows = rows.reshape(CHUNKS * ROWS * CHUNK_Y, CZ)

    def take(k, _):
        give(k).wait_recv()
        give(k).wait_send()

        @pl.when(k + AHEAD < CHUNKS)
        def _():
            for copy in stage(k + AHEAD):
                copy.wait()
            give(k + AHEAD).start()

        for copy in own(k):
            copy.wait()

        @pl.when(jnp.logical_and(k == 2, second))
        def _():
            pl.semaphore_wait(barrier, 11)
            tell(all_in)

        @pl.when(jnp.logical_and(k == 2, first))
        def _():
            pl.semaphore_wait(all_in, 1)

        @pl.when(jnp.logical_and(k == 2, early))
        def _():
            for copy in outer:
                copy.start()

        @pl.when(jnp.logical_and(k == CHUNKS - 1, jnp.logical_not(early)))
        def _():
            for copy in outer:
                copy.start()

        base = pl.multiple_of(k * CHUNK_Y, CHUNK_Y)
        start = pl.multiple_of(k * (ROWS * CHUNK_Y), ROWS * CHUNK_Y)
        for i in range(CHUNK_Y):
            at = pl.ds(pl.multiple_of((base + i) * CZ, CZ), CZ)
            for row, count, to in ORDER:
                hi, lo = split(
                    flat_rows[pl.ds(start + row * CHUNK_Y + i, count, stride=CHUNK_Y), :]
                )
                high[to : to + count, at] = hi
                low[to : to + count, at] = lo
        at = pl.ds(pl.multiple_of(base * CZ, CHUNK_Y * CZ), CHUNK_Y * CZ)
        hi, lo = high[:, at], low[:, at]
        grams[...] += nt(hi, hi) + nt(hi, lo) + nt(lo, hi)

        @pl.when(k < CHUNKS - 1)
        def _():
            lax.fori_loop(k * NEAR, jnp.minimum((k + 1) * NEAR, ORB), near, 0)

        return 0

    lax.fori_loop(0, CHUNKS, take, 0)

    red[0:ROWS, :] = grams[:, 0 : 2 * PREV]
    red[ROWS:, :] = jnp.zeros((2 * NEW, 2 * PREV), F32)
    red[ROWS:, 0 : 2 * NEW] = grams[2 * PREV :, 2 * PREV :]

    sent = []
    def quarter(size, index):
        return pl.ds(pl.multiple_of(size * index, size), size)

    copies = [
        remote(
            red.at[quarter(64, (z + d) % 4)], got_z.at[d - 1],
            sz.at[d - 1], rz.at[d - 1], z_peers[d - 1],
        )
        for d in range(1, 4)
    ]
    for copy in copies:
        copy.start()
    for copy in copies:
        copy.wait_recv()
    sent = sent + copies
    sum_z[...] = red[quarter(64, z)] + got_z[0] + got_z[1] + got_z[2]
    copies = [
        remote(
            sum_z.at[quarter(16, (y + d) % 4)], got_y.at[d - 1],
            sy.at[d - 1], ry.at[d - 1], y_peers[d - 1],
        )
        for d in range(1, 4)
    ]
    for copy in copies:
        copy.start()
    for copy in copies:
        copy.wait_recv()
    sent = sent + copies
    part[...] = sum_z[quarter(16, y)] + got_y[0] + got_y[1] + got_y[2]
    to_twin = remote(part, twin_part, s_twin, r_twin, twin)
    along_x = [
        remote(
            pair, got_x.at[x], sx.at[2 * d + c], rx.at[d],
            device((x + d + 1) % 4, y, z, c),
        )
        for d in range(3)
        for c in range(2)
    ]
    back = remote(pair, got_x.at[x], sx.at[6], rx.at[3], twin)

    @pl.when(jnp.logical_not(early))
    def _():
        to_twin.start()

    @pl.when(early)
    def _():
        to_twin.wait_recv()
        pair[...] = part[...] + twin_part[...]
        for copy in along_x:
            copy.start()
        back.start()
        for n in range(PIECES):
            outer[n].wait_recv()
            passed[n].start()
        got_x[x] = pair[...]

    @pl.when(jnp.logical_not(early))
    def _():
        back.wait_recv()

    for copy in along_x[::2]:
        copy.wait_recv()
    total = got_x[0]
    for d in range(1, 4):
        total = total + got_x[d]
    whole_y[quarter(16, y)] = total * (1.0 / TOTAL)
    copies = [
        remote(
            whole_y.at[quarter(16, y)], whole_y.at[quarter(16, y)],
            sgy.at[d - 1], rgy.at[d - 1], y_peers[d - 1],
        )
        for d in range(1, 4)
    ]
    for copy in copies:
        copy.start()
    for copy in copies:
        copy.wait_recv()
    sent = sent + copies
    whole[quarter(64, z)] = whole_y[...]
    copies = [
        remote(
            whole_y, whole.at[quarter(64, z)], sgz.at[d - 1], rgz.at[d - 1], z_peers[d - 1]
        )
        for d in range(1, 4)
    ]
    for copy in copies:
        copy.start()
    for copy in copies:
        copy.wait_recv()
    sent = sent + copies

    corr_t = whole[2 * PREV : 2 * PREV + 2 * NEW]
    i = lax.broadcasted_iota(jnp.int32, (128, 128), 0)
    j = lax.broadcasted_iota(jnp.int32, (128, 128), 1)
    middle = whole[0 : 2 * PREV] - jnp.where(i == j, 2.0, 0.0)
    gram = whole[ROWS:, 0 : 2 * NEW] + nt(nn(corr_t, middle, HIGH), corr_t, HIGH)
    i = lax.broadcasted_iota(jnp.int32, (64, 128), 0)
    j = lax.broadcasted_iota(jnp.int32, (64, 128), 1)
    factor[...] = jnp.where(j == i + 64, 1.0, 0.0)
    factor[:, 0:64] = gram

    both = factor[...]
    for first in range(0, 64, 4):
        columns = [
            jnp.broadcast_to(both[:, first + n : first + n + 1], (64, 128)) for n in range(4)
        ]
        for n in range(4):
            step = first + n
            pivot = 1.0 / columns[n][step : step + 1]
            below = jnp.where(i > step, columns[n] * pivot, 0.0)
            both = both - below * both[step : step + 1]
            for m in range(n + 1, 4):
                columns[m] = columns[m] - below * columns[m][step : step + 1]
    pivots = jnp.sum(jnp.where(i == j, both, 0.0), axis=1, keepdims=True)
    root = lax.rsqrt(pivots)
    root = root * (1.5 - 0.5 * pivots * root * root)
    factor[...] = both * root
    inverse = factor[:, 64:128]
    inverse_hi, inverse_lo = split(inverse)
    corr_hi, corr_lo = split(corr_t)
    work[0:64] = -(
        nn(inverse_hi, corr_hi) + (nn(inverse_hi, corr_lo) + nn(inverse_lo, corr_hi))
    )
    theirs, own = pl.ds(NEW * other, NEW), pl.ds(NEW * band, NEW)
    prev_hi, prev_lo = split(jnp.concatenate([work[theirs], work[own]], axis=0))
    new_hi, new_lo = split(
        jnp.concatenate([factor[theirs, 64:128], factor[own, 64:128]], axis=0)
    )
    hi = jnp.concatenate([prev_hi, new_hi], axis=1)
    lo = jnp.concatenate([prev_lo, new_lo], axis=1)
    stacked = jnp.concatenate([hi, lo], axis=0)

    flat_outs = outs.reshape(NEW * KEPT * CY, CZ)
    flat_ortho = ortho.reshape(NEW * PLANES * CY, CZ)
    kept = pl.multiple_of(band * (KEPT * CY), KEPT * CY)

    def tile(k):
        return k // (CY // TILE_Y), pl.ds(
            pl.multiple_of((k % (CY // TILE_Y)) * TILE_Y, TILE_Y), TILE_Y
        )

    def send_new(k):
        plane, at = tile(k)
        return remote(
            outs.at[:, plane, at],
            ortho.at[:, KEPT * band + plane, at],
            s2.at[k], r2.at[k], partner,
        )

    def make(k, _):
        base = pl.multiple_of(k * TILE_Y, TILE_Y)
        at = pl.ds(pl.multiple_of(base * CZ, TILE_Y * CZ), TILE_Y * CZ)
        both = nn(stacked, high[:, at])
        total = both[0:64] + both[64:128] + nn(hi, low[:, at])
        for n in range(TILE_Y):
            at = slice(n * CZ, (n + 1) * CZ)
            flat_outs[pl.ds(base + n, NEW, stride=KEPT * CY), :] = total[:NEW, at]
            flat_ortho[pl.ds(kept + base + n, NEW, stride=PLANES * CY), :] = total[NEW:, at]
        send_new(k).start()

        @pl.when(jnp.logical_and(k == 3, jnp.logical_not(early)))
        def _():
            for n in range(PIECES):
                outer[n].wait_recv()
                passed[n].start()

        return 0

    lax.fori_loop(0, TILES, make, 0)

    work[...] = whole[2 * PREV :].T
    corr[...] = work[pl.ds(pl.multiple_of(PREV * band, PREV), PREV), 0 : 2 * NEW]

    inner.wait()
    for copy in passed:
        copy.wait_recv()

    def far(o, _):
        for p in range(PLANES):
            total = applied[o, p]
            for step in range(1, DEPTH + 1):
                total = total - (0.5 * coeffs[step]) * (
                    ext[o, p + DEPTH + step] + ext[o, p + DEPTH - step]
                )
            applied[o, p] = total
        return 0

    lax.fori_loop(0, ORB, far, 0)
    for copy in sent + outer + passed:
        copy.wait_send()

    @pl.when(early)
    def _():
        for copy in along_x + [back]:
            copy.wait_send()

    @pl.when(jnp.logical_not(early))
    def _():
        to_twin.wait_send()


    def finish(k, _):
        send_new(k).wait()
        return 0

    lax.fori_loop(0, TILES, finish, 0)


def hand_over(a, b, c, a_out, b_out, c_out, sems):
    copies = []
    for n in range(2):
        part = pl.ds(n * (ORB // 2), ORB // 2)
        copies.append(pltpu.make_async_copy(a.at[part], a_out.at[part], sems.at[n]))
    for n in range(4):
        part = pl.ds(n * (NEW // 4), NEW // 4)
        copies.append(pltpu.make_async_copy(c.at[part], c_out.at[part], sems.at[2 + n]))
    copies.append(pltpu.make_async_copy(b, b_out, sems.at[6]))
    for copy in copies:
        copy.start()
    for copy in copies:
        copy.wait()


def on_device(orbitals, potential, earlier, incoming):
    dma = pltpu.SemaphoreType.DMA
    any_ = pl.BlockSpec(memory_space=pl.ANY)
    shapes = (
        jax.ShapeDtypeStruct(orbitals.shape, F32),
        jax.ShapeDtypeStruct((PREV, 2 * NEW), F32),
        jax.ShapeDtypeStruct(incoming.shape, F32),
    )
    held = tuple(pltpu.VMEM(shape.shape, shape.dtype) for shape in shapes)
    in_vmem = pl.BlockSpec(memory_space=pltpu.VMEM)
    arguments = [
        pltpu.with_memory_space_constraint(a, pltpu.HBM)
        for a in (orbitals, potential, earlier, incoming)
    ]
    results = pl.pallas_call(
        kernel,
        out_shape=held,
        in_specs=[any_] * 4,
        out_specs=(in_vmem,) * 3,
        scratch_shapes=[
            pltpu.VMEM((CHUNKS, HALF_ROWS, CHUNK_Y, CZ), F32),
            pltpu.VMEM((CHUNKS, ROWS, CHUNK_Y, CZ), F32),
            pltpu.VMEM((ROWS, CELLS), BF16),
            pltpu.VMEM((ROWS, CELLS), BF16),
            pltpu.VMEM((ORB, PLANES + 2 * DEPTH, CY, CZ), F32),
            pltpu.VMEM((PLANES, CY, CZ), F32),
            pltpu.VMEM((ORB, DEPTH, CY, CZ), F32),
            pltpu.VMEM((ROWS, ROWS), F32),
            pltpu.VMEM((256, 128), F32),
            pltpu.VMEM((3, 64, 128), F32),
            pltpu.VMEM((64, 128), F32),
            pltpu.VMEM((3, 16, 128), F32),
            pltpu.VMEM((16, 128), F32),
            pltpu.VMEM((16, 128), F32),
            pltpu.VMEM((16, 128), F32),
            pltpu.VMEM((4, 16, 128), F32),
            pltpu.VMEM((64, 128), F32),
            pltpu.VMEM((256, 128), F32),
            pltpu.VMEM((128, 128), F32),
            pltpu.VMEM((64, 128), F32),
            pltpu.VMEM((NEW, KEPT, CY, CZ), F32),
            pltpu.VMEM((CZ, CZ), F32),
            pltpu.VMEM((PLANES * CY, PLANES * CY), F32),
            dma((CHUNKS,)), dma((CHUNKS,)), dma((CHUNKS, 2)), dma((CHUNKS, 2)), dma((2,)),
            dma, dma, dma((PIECES,)), dma((PIECES,)), dma((PIECES,)), dma((PIECES,)),
            dma((3,)), dma((3,)), dma((3,)), dma((3,)), dma, dma, dma((7,)), dma((4,)),
            dma((3,)), dma((3,)), dma((3,)), dma((3,)),
            dma((TILES,)), dma((TILES,)),
            pltpu.SemaphoreType.REGULAR, pltpu.SemaphoreType.REGULAR,
        ],
        compiler_params=pltpu.CompilerParams(
            collective_id=0, has_side_effects=True, vmem_limit_bytes=50 * 2**20
        ),
        cost_estimate=pl.CostEstimate(
            flops=6 * 10**9, bytes_accessed=22 * 10**6, transcendentals=0
        ),
    )(*arguments)
    return pl.pallas_call(
        hand_over,
        out_shape=shapes,
        in_specs=[any_] * 3,
        out_specs=(any_,) * 3,
        scratch_shapes=[dma((7,))],
        compiler_params=pltpu.CompilerParams(vmem_limit_bytes=50 * 2**20),
        cost_estimate=pl.CostEstimate(flops=0, bytes_accessed=13 * 10**6, transcendentals=0),
    )(*[pltpu.with_memory_space_constraint(a, pltpu.VMEM) for a in results])


def solution(mesh):
    in_specs = (
        P("band", "domain", None, None),
        P("domain", None, None),
        P("band", "domain", None, None),
        P("band", "domain", None, None),
    )
    out_specs = (P("band", "domain", None, None), P("band", None), P("band", "domain", None, None))
    return jax.shard_map(
        on_device, mesh=mesh, in_specs=in_specs, out_specs=out_specs, check_vma=False
    )
```

```python
import jax
import jax.numpy as jnp
from jax import lax
from jax.experimental import pallas as pl
from jax.experimental.pallas import tpu as pltpu
from jax.sharding import PartitionSpec as P

coeffs = (
    -5369.0 / 1800.0,
    12.0 / 7.0,
    -15.0 / 56.0,
    10.0 / 189.0,
    -1.0 / 112.0,
    2.0 / 1925.0,
    -1.0 / 16632.0,
)

MESH = pl.DeviceIdType.MESH
HIGH = lax.Precision.HIGHEST
F32 = jnp.float32
BF16 = jnp.bfloat16

ORB = 16
PREV = 64
NEW = 32
PLANES = 8
KEPT = 4
CY = 32
CZ = 128
DEPTH = 6
ROWS = 2 * PREV + 2 * NEW
HALF_ROWS = PREV + NEW
ORDER = (
    (0, PREV, 0),
    (HALF_ROWS, PREV, PREV),
    (PREV, NEW, 2 * PREV),
    (HALF_ROWS + PREV, NEW, 2 * PREV + NEW),
)
CELLS = KEPT * CY * CZ
TOTAL = 512 * CY * CZ

CHUNKS = 16
CHUNK_Y = KEPT * CY // CHUNKS
AHEAD = 2
NEAR = -(-ORB // (CHUNKS - 1))
PIECES = 2
TILES = 16
TILE_Y = KEPT * CY // TILES


def nt(a, b, precision=None):
    return lax.dot_general(
        a, b, (((1,), (1,)), ((), ())), precision=precision, preferred_element_type=F32
    )


def nn(a, b, precision=None):
    return lax.dot_general(
        a, b, (((1,), (0,)), ((), ())), precision=precision, preferred_element_type=F32
    )


def split(a):
    hi = a.astype(BF16)
    return hi, (a - hi.astype(F32)).astype(BF16)


def band_matrix(size, block, diagonal):
    i = lax.broadcasted_iota(jnp.int32, (size, size), 0)
    j = lax.broadcasted_iota(jnp.int32, (size, size), 1)
    gap = jnp.abs(i - j)
    out = jnp.where(gap == 0, diagonal, 0.0).astype(F32)
    for step in range(1, DEPTH + 1):
        out = jnp.where(gap == step, -0.5 * coeffs[step], out)
    if block != size:
        out = jnp.where(i // block == j // block, out, 0.0)
    return out


def kernel(
    orb, pot, earl, inc,
    applied, corr, ortho,
    to_give, rows, high, low, ext, potv, relay, grams, red,
    got_z, sum_z, got_y, part, twin_part, pair, got_x, whole_y, whole, work, factor, outs, band_z, band_y,
    s1, r1, l1, l2, l0,
    s_in, r_in, s_out, r_relay, s_fwd, r_out,
    sz, rz, sy, ry, s_twin, r_twin, sx, rx, sgy, rgy, sgz, rgz,
    s2, r2, go, all_in,
):
    band = lax.axis_index("band")
    domain = lax.axis_index("domain")
    core = domain % 2
    x = ((domain // 2) % 2) * 2 + band
    y = (domain // 4) % 4
    z = domain // 16
    other = 1 - band

    def device(xx, yy, zz, cc):
        return (xx % 2, ((zz * 4 + yy) * 2 + xx // 2) * 2 + cc)

    z_peers = [device(x, y, (z + d) % 4, core) for d in range(1, 4)]
    y_peers = [device(x, (y + d) % 4, z, core) for d in range(1, 4)]
    partner = (other, domain)
    twin = (band, domain + 1 - 2 * core)
    toward = 2 * core - 1
    early = (band + core + 1) % 2
    next_domain = (domain + toward + 64) % 64
    via_y = early * ((next_domain // 4) % 4) + (1 - early) * y
    via_z = early * (next_domain // 16) + (1 - early) * z
    relayer = device((x + toward + 4) % 4, via_y, via_z, 1 - core)
    from_domain = ((z * 4 + y) * 2 + ((x + toward + 4) % 4) // 2) * 2 + 1 - core
    straight = ((z * 4 + y) * 2 + ((x - toward + 4) % 4) // 2) * 2 + core
    to_domain = (early * straight + (1 - early) * (from_domain - toward) + 64) % 64
    forward = (other, to_domain)
    way = 2 * band - 1
    chip = (z * 4 + y) * 2
    to = (chip + x // 2) * 2 + band + way + 64
    to = to % 64
    chip_passer = device(
        (((to // 2) % 2) * 2 + band - way + 4) % 4, (to // 4) % 4, to // 16, 0
    )
    giver_domain = ((chip + ((x - way + 4) % 4) // 2) * 2 + band + way + 64) % 64
    chip_giver = (other, giver_domain - giver_domain % 2)
    early = early == 1

    def piece(planes, k):
        plane = planes + k // (CY // CHUNK_Y)
        at = pl.multiple_of((k % (CY // CHUNK_Y)) * CHUNK_Y, CHUNK_Y)
        return plane, pl.ds(at, CHUNK_Y)

    def stage(k):
        plane, at = piece(KEPT * other, k)
        return (
            pltpu.make_async_copy(earl.at[:, plane, at], to_give.at[k, 0:PREV], l1.at[k, 0]),
            pltpu.make_async_copy(inc.at[:, plane, at], to_give.at[k, PREV:], l1.at[k, 1]),
        )

    def own(k):
        plane, at = piece(KEPT * band, k)
        return (
            pltpu.make_async_copy(
                earl.at[:, plane, at], rows.at[k, pl.ds(HALF_ROWS * band, PREV)], l2.at[k, 0]
            ),
            pltpu.make_async_copy(
                inc.at[:, plane, at], rows.at[k, pl.ds(HALF_ROWS * band + PREV, NEW)], l2.at[k, 1]
            ),
        )

    for k in range(AHEAD):
        for copy in stage(k):
            copy.start()

    barrier = pltpu.get_barrier_semaphore()
    first, second = core == 1, core == 0

    def greet(peer):
        pl.semaphore_signal(barrier, inc=1, device_id=peer, device_id_type=MESH)

    def tell(semaphore):
        pl.semaphore_signal(semaphore, inc=1, device_id=twin, device_id_type=MESH)

    @pl.when(second)
    def _():
        greet(twin)
        greet((other, domain + 1))

    @pl.when(first)
    def _():
        greet(partner)

    @pl.when(first)
    def _():
        pl.semaphore_wait(barrier, 3)
        tell(go)

    @pl.when(second)
    def _():
        pl.semaphore_wait(go, 1)

    def remote(src, dst, send, recv, peer):
        return pltpu.make_async_remote_copy(
            src_ref=src, dst_ref=dst, send_sem=send, recv_sem=recv,
            device_id=peer, device_id_type=MESH,
        )

    def give(k):
        return remote(
            to_give.at[k], rows.at[k, pl.ds(HALF_ROWS * band, HALF_ROWS)],
            s1.at[k], r1.at[k], partner,
        )

    for k in range(AHEAD):
        for copy in stage(k):
            copy.wait()
        give(k).start()

    def fetch(k, _):
        for copy in own(k):
            copy.start()

        @pl.when(k + AHEAD < CHUNKS)
        def _():
            for copy in stage(k + AHEAD):
                copy.start()

        return 0

    @pl.when(second)
    def _():
        for d in range(1, 4):
            greet(device(x, y, (z + d) % 4, 0))
            greet(device(x, (y + d) % 4, z, 0))
            greet(device((x + d) % 4, y, z, 0))
        greet(chip_passer)
        greet(chip_giver)

    inner = remote(
        orb.at[:, pl.ds(2 * (1 - core), DEPTH)], ext.at[:, pl.ds(14 * core, DEPTH)],
        s_in, r_in, twin,
    )
    outer, passed = [], []
    for n in range(PIECES):
        some = pl.ds(n * (ORB // PIECES), ORB // PIECES)
        outer.append(
            remote(
                orb.at[some, pl.ds(2 * core, DEPTH)], relay.at[some],
                s_out.at[n], r_relay.at[n], relayer,
            )
        )
        passed.append(
            remote(
                relay.at[some], ext.at[some, pl.ds(14 * core, DEPTH)],
                s_fwd.at[n], r_out.at[n], forward,
            )
        )

    locals_ = [
        pltpu.make_async_copy(orb, ext.at[:, pl.ds(DEPTH, PLANES)], l0.at[0]),
        pltpu.make_async_copy(pot, potv, l0.at[1]),
    ]
    for copy in locals_:
        copy.start()
    lax.fori_loop(0, CHUNKS, fetch, 0)
    inner.start()

    band_z[...] = band_matrix(CZ, CZ, -1.5 * coeffs[0])
    band_y[...] = band_matrix(PLANES * CY, CY, 0.0)
    for copy in locals_:
        copy.wait()

    def near(o, _):
        cells = ext[o, DEPTH : DEPTH + PLANES].reshape(PLANES * CY, CZ)
        field = potv[...].reshape(PLANES * CY, CZ)
        total = field * cells + nn(cells, band_z[...], HIGH) + nn(band_y[...], cells, HIGH)
        applied[o] = total.reshape(PLANES, CY, CZ)
        return 0

    grams[...] = jnp.zeros_like(grams)
    flat_rows = rows.reshape(CHUNKS * ROWS * CHUNK_Y, CZ)

    def take(k, _):
        give(k).wait_recv()
        give(k).wait_send()

        @pl.when(k + AHEAD < CHUNKS)
        def _():
            for copy in stage(k + AHEAD):
                copy.wait()
            give(k + AHEAD).start()

        for copy in own(k):
            copy.wait()

        @pl.when(jnp.logical_and(k == 2, second))
        def _():
            pl.semaphore_wait(barrier, 11)
            tell(all_in)

        @pl.when(jnp.logical_and(k == 2, first))
        def _():
            pl.semaphore_wait(all_in, 1)

        @pl.when(jnp.logical_and(k == 2, early))
        def _():
            for copy in outer:
                copy.start()

        @pl.when(jnp.logical_and(k == CHUNKS - 1, jnp.logical_not(early)))
        def _():
            for copy in outer:
                copy.start()

        base = pl.multiple_of(k * CHUNK_Y, CHUNK_Y)
        start = pl.multiple_of(k * (ROWS * CHUNK_Y), ROWS * CHUNK_Y)
        for i in range(CHUNK_Y):
            at = pl.ds(pl.multiple_of((base + i) * CZ, CZ), CZ)
            for row, count, to in ORDER:
                hi, lo = split(
                    flat_rows[pl.ds(start + row * CHUNK_Y + i, count, stride=CHUNK_Y), :]
                )
                high[to : to + count, at] = hi
                low[to : to + count, at] = lo
        at = pl.ds(pl.multiple_of(base * CZ, CHUNK_Y * CZ), CHUNK_Y * CZ)
        hi, lo = high[:, at], low[:, at]
        grams[...] += nt(hi, hi) + nt(hi, lo) + nt(lo, hi)

        @pl.when(k < CHUNKS - 1)
        def _():
            lax.fori_loop(k * NEAR, jnp.minimum((k + 1) * NEAR, ORB), near, 0)

        return 0

    lax.fori_loop(0, CHUNKS, take, 0)

    red[0:ROWS, :] = grams[:, 0 : 2 * PREV]
    red[ROWS:, :] = jnp.zeros((2 * NEW, 2 * PREV), F32)
    red[ROWS:, 0 : 2 * NEW] = grams[2 * PREV :, 2 * PREV :]

    sent = []
    def quarter(size, index):
        return pl.ds(pl.multiple_of(size * index, size), size)

    copies = [
        remote(
            red.at[quarter(64, (z + d) % 4)], got_z.at[d - 1],
            sz.at[d - 1], rz.at[d - 1], z_peers[d - 1],
        )
        for d in range(1, 4)
    ]
    for copy in copies:
        copy.start()
    for copy in copies:
        copy.wait_recv()
    sent = sent + copies
    sum_z[...] = red[quarter(64, z)] + got_z[0] + got_z[1] + got_z[2]
    copies = [
        remote(
            sum_z.at[quarter(16, (y + d) % 4)], got_y.at[d - 1],
            sy.at[d - 1], ry.at[d - 1], y_peers[d - 1],
        )
        for d in range(1, 4)
    ]
    for copy in copies:
        copy.start()
    for copy in copies:
        copy.wait_recv()
    sent = sent + copies
    part[...] = sum_z[quarter(16, y)] + got_y[0] + got_y[1] + got_y[2]
    to_twin = remote(part, twin_part, s_twin, r_twin, twin)
    along_x = [
        remote(
            pair, got_x.at[x], sx.at[2 * d + c], rx.at[d],
            device((x + d + 1) % 4, y, z, c),
        )
        for d in range(3)
        for c in range(2)
    ]
    back = remote(pair, got_x.at[x], sx.at[6], rx.at[3], twin)

    @pl.when(jnp.logical_not(early))
    def _():
        to_twin.start()

    @pl.when(early)
    def _():
        to_twin.wait_recv()
        pair[...] = part[...] + twin_part[...]
        for copy in along_x:
            copy.start()
        back.start()
        for n in range(PIECES):
            outer[n].wait_recv()
            passed[n].start()
        got_x[x] = pair[...]

    @pl.when(jnp.logical_not(early))
    def _():
        back.wait_recv()

    for copy in along_x[::2]:
        copy.wait_recv()
    total = got_x[0]
    for d in range(1, 4):
        total = total + got_x[d]
    whole_y[quarter(16, y)] = total * (1.0 / TOTAL)
    copies = [
        remote(
            whole_y.at[quarter(16, y)], whole_y.at[quarter(16, y)],
            sgy.at[d - 1], rgy.at[d - 1], y_peers[d - 1],
        )
        for d in range(1, 4)
    ]
    for copy in copies:
        copy.start()
    for copy in copies:
        copy.wait_recv()
    sent = sent + copies
    whole[quarter(64, z)] = whole_y[...]
    copies = [
        remote(
            whole_y, whole.at[quarter(64, z)], sgz.at[d - 1], rgz.at[d - 1], z_peers[d - 1]
        )
        for d in range(1, 4)
    ]
    for copy in copies:
        copy.start()
    for copy in copies:
        copy.wait_recv()
    sent = sent + copies

    corr_t = whole[2 * PREV : 2 * PREV + 2 * NEW]
    i = lax.broadcasted_iota(jnp.int32, (128, 128), 0)
    j = lax.broadcasted_iota(jnp.int32, (128, 128), 1)
    middle = whole[0 : 2 * PREV] - jnp.where(i == j, 2.0, 0.0)
    gram = whole[ROWS:, 0 : 2 * NEW] + nt(nn(corr_t, middle, HIGH), corr_t, HIGH)
    i = lax.broadcasted_iota(jnp.int32, (64, 128), 0)
    j = lax.broadcasted_iota(jnp.int32, (64, 128), 1)
    factor[...] = jnp.where(j == i + 64, 1.0, 0.0)
    factor[:, 0:64] = gram

    both = factor[...]
    for first in range(0, 64, 4):
        columns = [
            jnp.broadcast_to(both[:, first + n : first + n + 1], (64, 128)) for n in range(4)
        ]
        for n in range(4):
            step = first + n
            pivot = 1.0 / columns[n][step : step + 1]
            below = jnp.where(i > step, columns[n] * pivot, 0.0)
            both = both - below * both[step : step + 1]
            for m in range(n + 1, 4):
                columns[m] = columns[m] - below * columns[m][step : step + 1]
    pivots = jnp.sum(jnp.where(i == j, both, 0.0), axis=1, keepdims=True)
    root = lax.rsqrt(pivots)
    root = root * (1.5 - 0.5 * pivots * root * root)
    factor[...] = both * root
    inverse = factor[:, 64:128]
    inverse_hi, inverse_lo = split(inverse)
    corr_hi, corr_lo = split(corr_t)
    work[0:64] = -(
        nn(inverse_hi, corr_hi) + (nn(inverse_hi, corr_lo) + nn(inverse_lo, corr_hi))
    )
    theirs, own = pl.ds(NEW * other, NEW), pl.ds(NEW * band, NEW)
    prev_hi, prev_lo = split(jnp.concatenate([work[theirs], work[own]], axis=0))
    new_hi, new_lo = split(
        jnp.concatenate([factor[theirs, 64:128], factor[own, 64:128]], axis=0)
    )
    hi = jnp.concatenate([prev_hi, new_hi], axis=1)
    lo = jnp.concatenate([prev_lo, new_lo], axis=1)
    stacked = jnp.concatenate([hi, lo], axis=0)

    flat_outs = outs.reshape(NEW * KEPT * CY, CZ)
    flat_ortho = ortho.reshape(NEW * PLANES * CY, CZ)
    kept = pl.multiple_of(band * (KEPT * CY), KEPT * CY)

    def tile(k):
        return k // (CY // TILE_Y), pl.ds(
            pl.multiple_of((k % (CY // TILE_Y)) * TILE_Y, TILE_Y), TILE_Y
        )

    def send_new(k):
        plane, at = tile(k)
        return remote(
            outs.at[:, plane, at],
            ortho.at[:, KEPT * band + plane, at],
            s2.at[k], r2.at[k], partner,
        )

    def make(k, _):
        base = pl.multiple_of(k * TILE_Y, TILE_Y)
        at = pl.ds(pl.multiple_of(base * CZ, TILE_Y * CZ), TILE_Y * CZ)
        both = nn(stacked, high[:, at])
        total = both[0:64] + both[64:128] + nn(hi, low[:, at])
        for n in range(TILE_Y):
            at = slice(n * CZ, (n + 1) * CZ)
            flat_outs[pl.ds(base + n, NEW, stride=KEPT * CY), :] = total[:NEW, at]
            flat_ortho[pl.ds(kept + base + n, NEW, stride=PLANES * CY), :] = total[NEW:, at]
        send_new(k).start()

        @pl.when(jnp.logical_and(k == 3, jnp.logical_not(early)))
        def _():
            for n in range(PIECES):
                outer[n].wait_recv()
                passed[n].start()

        return 0

    lax.fori_loop(0, TILES, make, 0)

    work[...] = whole[2 * PREV :].T
    corr[...] = work[pl.ds(pl.multiple_of(PREV * band, PREV), PREV), 0 : 2 * NEW]

    inner.wait()
    for copy in passed:
        copy.wait_recv()

    def far(o, _):
        for p in range(PLANES):
            total = applied[o, p]
            for step in range(1, DEPTH + 1):
                total = total - (0.5 * coeffs[step]) * (
                    ext[o, p + DEPTH + step] + ext[o, p + DEPTH - step]
                )
            applied[o, p] = total
        return 0

    lax.fori_loop(0, ORB, far, 0)
    for copy in sent + outer + passed:
        copy.wait_send()

    @pl.when(early)
    def _():
        for copy in along_x + [back]:
            copy.wait_send()

    @pl.when(jnp.logical_not(early))
    def _():
        to_twin.wait_send()


    def finish(k, _):
        send_new(k).wait()
        return 0

    lax.fori_loop(0, TILES, finish, 0)


def hand_over(a, b, c, a_out, b_out, c_out, sems):
    copies = []
    for n in range(2):
        part = pl.ds(n * (ORB // 2), ORB // 2)
        copies.append(pltpu.make_async_copy(a.at[part], a_out.at[part], sems.at[n]))
    for n in range(4):
        part = pl.ds(n * (NEW // 4), NEW // 4)
        copies.append(pltpu.make_async_copy(c.at[part], c_out.at[part], sems.at[2 + n]))
    copies.append(pltpu.make_async_copy(b, b_out, sems.at[6]))
    for copy in copies:
        copy.start()
    for copy in copies:
        copy.wait()


def on_device(orbitals, potential, earlier, incoming):
    dma = pltpu.SemaphoreType.DMA
    any_ = pl.BlockSpec(memory_space=pl.ANY)
    shapes = (
        jax.ShapeDtypeStruct(orbitals.shape, F32),
        jax.ShapeDtypeStruct((PREV, 2 * NEW), F32),
        jax.ShapeDtypeStruct(incoming.shape, F32),
    )
    held = tuple(pltpu.VMEM(shape.shape, shape.dtype) for shape in shapes)
    in_vmem = pl.BlockSpec(memory_space=pltpu.VMEM)
    arguments = [
        pltpu.with_memory_space_constraint(a, pltpu.HBM)
        for a in (orbitals, potential, earlier, incoming)
    ]
    results = pl.pallas_call(
        kernel,
        out_shape=held,
        in_specs=[any_] * 4,
        out_specs=(in_vmem,) * 3,
        scratch_shapes=[
            pltpu.VMEM((CHUNKS, HALF_ROWS, CHUNK_Y, CZ), F32),
            pltpu.VMEM((CHUNKS, ROWS, CHUNK_Y, CZ), F32),
            pltpu.VMEM((ROWS, CELLS), BF16),
            pltpu.VMEM((ROWS, CELLS), BF16),
            pltpu.VMEM((ORB, PLANES + 2 * DEPTH, CY, CZ), F32),
            pltpu.VMEM((PLANES, CY, CZ), F32),
            pltpu.VMEM((ORB, DEPTH, CY, CZ), F32),
            pltpu.VMEM((ROWS, ROWS), F32),
            pltpu.VMEM((256, 128), F32),
            pltpu.VMEM((3, 64, 128), F32),
            pltpu.VMEM((64, 128), F32),
            pltpu.VMEM((3, 16, 128), F32),
            pltpu.VMEM((16, 128), F32),
            pltpu.VMEM((16, 128), F32),
            pltpu.VMEM((16, 128), F32),
            pltpu.VMEM((4, 16, 128), F32),
            pltpu.VMEM((64, 128), F32),
            pltpu.VMEM((256, 128), F32),
            pltpu.VMEM((128, 128), F32),
            pltpu.VMEM((64, 128), F32),
            pltpu.VMEM((NEW, KEPT, CY, CZ), F32),
            pltpu.VMEM((CZ, CZ), F32),
            pltpu.VMEM((PLANES * CY, PLANES * CY), F32),
            dma((CHUNKS,)), dma((CHUNKS,)), dma((CHUNKS, 2)), dma((CHUNKS, 2)), dma((2,)),
            dma, dma, dma((PIECES,)), dma((PIECES,)), dma((PIECES,)), dma((PIECES,)),
            dma((3,)), dma((3,)), dma((3,)), dma((3,)), dma, dma, dma((7,)), dma((4,)),
            dma((3,)), dma((3,)), dma((3,)), dma((3,)),
            dma((TILES,)), dma((TILES,)),
            pltpu.SemaphoreType.REGULAR, pltpu.SemaphoreType.REGULAR,
        ],
        compiler_params=pltpu.CompilerParams(
            collective_id=0, has_side_effects=True, vmem_limit_bytes=50 * 2**20
        ),
        cost_estimate=pl.CostEstimate(
            flops=6 * 10**9, bytes_accessed=22 * 10**6, transcendentals=0
        ),
    )(*arguments)
    return pl.pallas_call(
        hand_over,
        out_shape=shapes,
        in_specs=[any_] * 3,
        out_specs=(any_,) * 3,
        scratch_shapes=[dma((7,))],
        compiler_params=pltpu.CompilerParams(vmem_limit_bytes=50 * 2**20),
        cost_estimate=pl.CostEstimate(flops=0, bytes_accessed=13 * 10**6, transcendentals=0),
    )(*[pltpu.with_memory_space_constraint(a, pltpu.VMEM) for a in results])


def solution(mesh):
    in_specs = (
        P("band", "domain", None, None),
        P("domain", None, None),
        P("band", "domain", None, None),
        P("band", "domain", None, None),
    )
    out_specs = (P("band", "domain", None, None), P("band", None), P("band", "domain", None, None))
    return jax.shard_map(
        on_device, mesh=mesh, in_specs=in_specs, out_specs=out_specs, check_vma=False
    )
```

```python
import jax
import jax.numpy as jnp
from jax import lax
from jax.experimental import pallas as pl
from jax.experimental.pallas import tpu as pltpu
from jax.sharding import PartitionSpec as P

coeffs = (
    -5369.0 / 1800.0,
    12.0 / 7.0,
    -15.0 / 56.0,
    10.0 / 189.0,
    -1.0 / 112.0,
    2.0 / 1925.0,
    -1.0 / 16632.0,
)

MESH = pl.DeviceIdType.MESH
HIGH = lax.Precision.HIGHEST
F32 = jnp.float32
BF16 = jnp.bfloat16

ORB = 16
PREV = 64
NEW = 32
PLANES = 8
KEPT = 4
CY = 32
CZ = 128
DEPTH = 6
ROWS = 2 * PREV + 2 * NEW
HALF_ROWS = PREV + NEW
ORDER = (
    (0, PREV, 0),
    (HALF_ROWS, PREV, PREV),
    (PREV, NEW, 2 * PREV),
    (HALF_ROWS + PREV, NEW, 2 * PREV + NEW),
)
CELLS = KEPT * CY * CZ
TOTAL = 512 * CY * CZ

CHUNKS = 16
CHUNK_Y = KEPT * CY // CHUNKS
AHEAD = 2
NEAR = -(-ORB // (CHUNKS - 1))
PIECES = 2
TILES = 16
LAG = 2
TILE_Y = KEPT * CY // TILES


def nt(a, b, precision=None):
    return lax.dot_general(
        a, b, (((1,), (1,)), ((), ())), precision=precision, preferred_element_type=F32
    )


def nn(a, b, precision=None):
    return lax.dot_general(
        a, b, (((1,), (0,)), ((), ())), precision=precision, preferred_element_type=F32
    )


def split(a):
    hi = a.astype(BF16)
    return hi, (a - hi.astype(F32)).astype(BF16)


def band_matrix(size, block, diagonal):
    i = lax.broadcasted_iota(jnp.int32, (size, size), 0)
    j = lax.broadcasted_iota(jnp.int32, (size, size), 1)
    gap = jnp.abs(i - j)
    out = jnp.where(gap == 0, diagonal, 0.0).astype(F32)
    for step in range(1, DEPTH + 1):
        out = jnp.where(gap == step, -0.5 * coeffs[step], out)
    if block != size:
        out = jnp.where(i // block == j // block, out, 0.0)
    return out


def kernel(
    orb, pot, earl, inc,
    applied, corr, ortho,
    to_give, rows, high, low, ext, potv, relay, grams, red,
    got_z, sum_z, got_y, part, twin_part, pair, got_x, whole_y, whole, work, factor, outs, band_z, band_y,
    s1, r1, l1, l2, l0,
    s_in, r_in, s_out, r_relay, s_fwd, r_out,
    sz, rz, sy, ry, s_twin, r_twin, sx, rx, sgy, rgy, sgz, rgz,
    s2, r2, go, all_in,
):
    band = lax.axis_index("band")
    domain = lax.axis_index("domain")
    core = domain % 2
    x = ((domain // 2) % 2) * 2 + band
    y = (domain // 4) % 4
    z = domain // 16
    other = 1 - band

    def device(xx, yy, zz, cc):
        return (xx % 2, ((zz * 4 + yy) * 2 + xx // 2) * 2 + cc)

    z_peers = [device(x, y, (z + d) % 4, core) for d in range(1, 4)]
    y_peers = [device(x, (y + d) % 4, z, core) for d in range(1, 4)]
    partner = (other, domain)
    twin = (band, domain + 1 - 2 * core)
    toward = 2 * core - 1
    early = (band + core + 1) % 2
    next_domain = (domain + toward + 64) % 64
    via_y = early * ((next_domain // 4) % 4) + (1 - early) * y
    via_z = early * (next_domain // 16) + (1 - early) * z
    relayer = device((x + toward + 4) % 4, via_y, via_z, 1 - core)
    from_domain = ((z * 4 + y) * 2 + ((x + toward + 4) % 4) // 2) * 2 + 1 - core
    straight = ((z * 4 + y) * 2 + ((x - toward + 4) % 4) // 2) * 2 + core
    to_domain = (early * straight + (1 - early) * (from_domain - toward) + 64) % 64
    forward = (other, to_domain)
    way = 2 * band - 1
    chip = (z * 4 + y) * 2
    to = (chip + x // 2) * 2 + band + way + 64
    to = to % 64
    chip_passer = device(
        (((to // 2) % 2) * 2 + band - way + 4) % 4, (to // 4) % 4, to // 16, 1
    )
    giver_domain = ((chip + ((x - way + 4) % 4) // 2) * 2 + band + way + 64) % 64
    chip_giver = (other, giver_domain - giver_domain % 2 + 1)
    early = early == 1

    def piece(planes, k):
        plane = planes + k // (CY // CHUNK_Y)
        at = pl.multiple_of((k % (CY // CHUNK_Y)) * CHUNK_Y, CHUNK_Y)
        return plane, pl.ds(at, CHUNK_Y)

    def stage(k):
        plane, at = piece(KEPT * other, k)
        return (
            pltpu.make_async_copy(earl.at[:, plane, at], to_give.at[k, 0:PREV], l1.at[k, 0]),
            pltpu.make_async_copy(inc.at[:, plane, at], to_give.at[k, PREV:], l1.at[k, 1]),
        )

    def own(k):
        plane, at = piece(KEPT * band, k)
        return (
            pltpu.make_async_copy(
                earl.at[:, plane, at], rows.at[k, pl.ds(HALF_ROWS * band, PREV)], l2.at[k, 0]
            ),
            pltpu.make_async_copy(
                inc.at[:, plane, at], rows.at[k, pl.ds(HALF_ROWS * band + PREV, NEW)], l2.at[k, 1]
            ),
        )

    for k in range(AHEAD):
        for copy in stage(k):
            copy.start()

    barrier = pltpu.get_barrier_semaphore()
    first, second = core == 0, core == 1

    def greet(peer):
        pl.semaphore_signal(barrier, inc=1, device_id=peer, device_id_type=MESH)

    def tell(semaphore):
        pl.semaphore_signal(semaphore, inc=1, device_id=twin, device_id_type=MESH)

    @pl.when(second)
    def _():
        greet(twin)
        greet((other, domain - 1))

    @pl.when(first)
    def _():
        greet(partner)

    @pl.when(first)
    def _():
        pl.semaphore_wait(barrier, 3)
        tell(go)

    @pl.when(second)
    def _():
        pl.semaphore_wait(go, 1)

    def remote(src, dst, send, recv, peer):
        return pltpu.make_async_remote_copy(
            src_ref=src, dst_ref=dst, send_sem=send, recv_sem=recv,
            device_id=peer, device_id_type=MESH,
        )

    def give(k):
        return remote(
            to_give.at[k], rows.at[k, pl.ds(HALF_ROWS * band, HALF_ROWS)],
            s1.at[k], r1.at[k], partner,
        )

    for k in range(AHEAD):
        for copy in stage(k):
            copy.wait()
        give(k).start()

    def fetch(k, _):
        for copy in own(k):
            copy.start()

        @pl.when(k + AHEAD < CHUNKS)
        def _():
            for copy in stage(k + AHEAD):
                copy.start()

        return 0

    @pl.when(second)
    def _():
        for d in range(1, 4):
            greet(device(x, y, (z + d) % 4, 1))
            greet(device(x, (y + d) % 4, z, 1))
            greet(device((x + d) % 4, y, z, 1))
        greet(chip_passer)
        greet(chip_giver)

    inner = remote(
        orb.at[:, pl.ds(2 * (1 - core), DEPTH)], ext.at[:, pl.ds(14 * core, DEPTH)],
        s_in, r_in, twin,
    )
    outer, passed = [], []
    for n in range(PIECES):
        some = pl.ds(n * (ORB // PIECES), ORB // PIECES)
        outer.append(
            remote(
                orb.at[some, pl.ds(2 * core, DEPTH)], relay.at[some],
                s_out.at[n], r_relay.at[n], relayer,
            )
        )
        passed.append(
            remote(
                relay.at[some], ext.at[some, pl.ds(14 * core, DEPTH)],
                s_fwd.at[n], r_out.at[n], forward,
            )
        )

    locals_ = [
        pltpu.make_async_copy(orb, ext.at[:, pl.ds(DEPTH, PLANES)], l0.at[0]),
        pltpu.make_async_copy(pot, potv, l0.at[1]),
    ]
    for copy in locals_:
        copy.start()
    lax.fori_loop(0, CHUNKS, fetch, 0)
    inner.start()

    band_z[...] = band_matrix(CZ, CZ, -1.5 * coeffs[0])
    band_y[...] = band_matrix(PLANES * CY, CY, 0.0)
    for copy in locals_:
        copy.wait()

    def near(o, _):
        cells = ext[o, DEPTH : DEPTH + PLANES].reshape(PLANES * CY, CZ)
        field = potv[...].reshape(PLANES * CY, CZ)
        total = field * cells + nn(cells, band_z[...], HIGH) + nn(band_y[...], cells, HIGH)
        applied[o] = total.reshape(PLANES, CY, CZ)
        return 0

    grams[...] = jnp.zeros_like(grams)
    flat_rows = rows.reshape(CHUNKS * ROWS * CHUNK_Y, CZ)

    def take(k, _):
        give(k).wait_recv()
        give(k).wait_send()

        @pl.when(k + AHEAD < CHUNKS)
        def _():
            for copy in stage(k + AHEAD):
                copy.wait()
            give(k + AHEAD).start()

        for copy in own(k):
            copy.wait()

        @pl.when(jnp.logical_and(k == 2, second))
        def _():
            pl.semaphore_wait(barrier, 11)
            tell(all_in)

        @pl.when(jnp.logical_and(k == 2, first))
        def _():
            pl.semaphore_wait(all_in, 1)

        @pl.when(jnp.logical_and(k == 2, early))
        def _():
            for copy in outer:
                copy.start()

        @pl.when(jnp.logical_and(k == CHUNKS - 1, jnp.logical_not(early)))
        def _():
            for copy in outer:
                copy.start()

        base = pl.multiple_of(k * CHUNK_Y, CHUNK_Y)
        start = pl.multiple_of(k * (ROWS * CHUNK_Y), ROWS * CHUNK_Y)
        for i in range(CHUNK_Y):
            at = pl.ds(pl.multiple_of((base + i) * CZ, CZ), CZ)
            for row, count, to in ORDER:
                hi, lo = split(
                    flat_rows[pl.ds(start + row * CHUNK_Y + i, count, stride=CHUNK_Y), :]
                )
                high[to : to + count, at] = hi
                low[to : to + count, at] = lo
        at = pl.ds(pl.multiple_of(base * CZ, CHUNK_Y * CZ), CHUNK_Y * CZ)
        hi, lo = high[:, at], low[:, at]
        grams[...] += nt(hi, hi) + nt(hi, lo) + nt(lo, hi)

        @pl.when(k < CHUNKS - 1)
        def _():
            lax.fori_loop(k * NEAR, jnp.minimum((k + 1) * NEAR, ORB), near, 0)

        return 0

    lax.fori_loop(0, CHUNKS, take, 0)

    red[0:ROWS, :] = grams[:, 0 : 2 * PREV]
    red[ROWS:, :] = jnp.zeros((2 * NEW, 2 * PREV), F32)
    red[ROWS:, 0 : 2 * NEW] = grams[2 * PREV :, 2 * PREV :]

    sent = []
    def quarter(size, index):
        return pl.ds(pl.multiple_of(size * index, size), size)

    copies = [
        remote(
            red.at[quarter(64, (z + d) % 4)], got_z.at[d - 1],
            sz.at[d - 1], rz.at[d - 1], z_peers[d - 1],
        )
        for d in range(1, 4)
    ]
    for copy in copies:
        copy.start()
    for copy in copies:
        copy.wait_recv()
    sent = sent + copies
    sum_z[...] = red[quarter(64, z)] + got_z[0] + got_z[1] + got_z[2]
    copies = [
        remote(
            sum_z.at[quarter(16, (y + d) % 4)], got_y.at[d - 1],
            sy.at[d - 1], ry.at[d - 1], y_peers[d - 1],
        )
        for d in range(1, 4)
    ]
    for copy in copies:
        copy.start()
    for copy in copies:
        copy.wait_recv()
    sent = sent + copies
    part[...] = sum_z[quarter(16, y)] + got_y[0] + got_y[1] + got_y[2]
    to_twin = remote(part, twin_part, s_twin, r_twin, twin)
    along_x = [
        remote(
            pair, got_x.at[x], sx.at[2 * d + c], rx.at[d],
            device((x + d + 1) % 4, y, z, c),
        )
        for d in range(3)
        for c in range(2)
    ]
    back = remote(pair, got_x.at[x], sx.at[6], rx.at[3], twin)

    @pl.when(jnp.logical_not(early))
    def _():
        to_twin.start()

    @pl.when(early)
    def _():
        to_twin.wait_recv()
        pair[...] = part[...] + twin_part[...]
        for copy in along_x:
            copy.start()
        back.start()
        for n in range(PIECES):
            outer[n].wait_recv()
            passed[n].start()
        got_x[x] = pair[...]

    @pl.when(jnp.logical_not(early))
    def _():
        back.wait_recv()

    for copy in along_x[::2]:
        copy.wait_recv()
    total = got_x[0]
    for d in range(1, 4):
        total = total + got_x[d]
    whole_y[quarter(16, y)] = total * (1.0 / TOTAL)
    copies = [
        remote(
            whole_y.at[quarter(16, y)], whole_y.at[quarter(16, y)],
            sgy.at[d - 1], rgy.at[d - 1], y_peers[d - 1],
        )
        for d in range(1, 4)
    ]
    for copy in copies:
        copy.start()
    for copy in copies:
        copy.wait_recv()
    sent = sent + copies
    whole[quarter(64, z)] = whole_y[...]
    copies = [
        remote(
            whole_y, whole.at[quarter(64, z)], sgz.at[d - 1], rgz.at[d - 1], z_peers[d - 1]
        )
        for d in range(1, 4)
    ]
    for copy in copies:
        copy.start()
    for copy in copies:
        copy.wait_recv()
    sent = sent + copies

    corr_t = whole[2 * PREV : 2 * PREV + 2 * NEW]
    i = lax.broadcasted_iota(jnp.int32, (128, 128), 0)
    j = lax.broadcasted_iota(jnp.int32, (128, 128), 1)
    middle = whole[0 : 2 * PREV] - jnp.where(i == j, 2.0, 0.0)
    gram = whole[ROWS:, 0 : 2 * NEW] + nt(nn(corr_t, middle, HIGH), corr_t, HIGH)
    i = lax.broadcasted_iota(jnp.int32, (64, 128), 0)
    j = lax.broadcasted_iota(jnp.int32, (64, 128), 1)
    factor[...] = jnp.where(j == i + 64, 1.0, 0.0)
    factor[:, 0:64] = gram

    both = factor[...]
    for first in range(0, 64, 4):
        columns = [
            jnp.broadcast_to(both[:, first + n : first + n + 1], (64, 128)) for n in range(4)
        ]
        for n in range(4):
            step = first + n
            pivot = 1.0 / columns[n][step : step + 1]
            below = jnp.where(i > step, columns[n] * pivot, 0.0)
            both = both - below * both[step : step + 1]
            for m in range(n + 1, 4):
                columns[m] = columns[m] - below * columns[m][step : step + 1]
    pivots = jnp.sum(jnp.where(i == j, both, 0.0), axis=1, keepdims=True)
    root = lax.rsqrt(pivots)
    root = root * (1.5 - 0.5 * pivots * root * root)
    factor[...] = both * root
    inverse = factor[:, 64:128]
    inverse_hi, inverse_lo = split(inverse)
    corr_hi, corr_lo = split(corr_t)
    work[0:64] = -(
        nn(inverse_hi, corr_hi) + (nn(inverse_hi, corr_lo) + nn(inverse_lo, corr_hi))
    )
    theirs, own = pl.ds(NEW * other, NEW), pl.ds(NEW * band, NEW)
    prev_hi, prev_lo = split(jnp.concatenate([work[theirs], work[own]], axis=0))
    new_hi, new_lo = split(
        jnp.concatenate([factor[theirs, 64:128], factor[own, 64:128]], axis=0)
    )
    hi = jnp.concatenate([prev_hi, new_hi], axis=1)
    lo = jnp.concatenate([prev_lo, new_lo], axis=1)
    stacked = jnp.concatenate([hi, lo], axis=0)

    flat_outs = outs.reshape(NEW * KEPT * CY, CZ)
    flat_ortho = ortho.reshape(NEW * PLANES * CY, CZ)
    kept = pl.multiple_of(band * (KEPT * CY), KEPT * CY)

    def tile(k):
        return k // (CY // TILE_Y), pl.ds(
            pl.multiple_of((k % (CY // TILE_Y)) * TILE_Y, TILE_Y), TILE_Y
        )

    def send_new(k):
        plane, at = tile(k)
        return remote(
            outs.at[:, plane, at],
            ortho.at[:, KEPT * band + plane, at],
            s2.at[k], r2.at[k], partner,
        )

    def make(k, _):
        base = pl.multiple_of(k * TILE_Y, TILE_Y)
        at = pl.ds(pl.multiple_of(base * CZ, TILE_Y * CZ), TILE_Y * CZ)
        both = nn(stacked, high[:, at])
        total = both[0:64] + both[64:128] + nn(hi, low[:, at])
        for n in range(TILE_Y):
            at = slice(n * CZ, (n + 1) * CZ)
            flat_outs[pl.ds(base + n, NEW, stride=KEPT * CY), :] = total[:NEW, at]
            flat_ortho[pl.ds(kept + base + n, NEW, stride=PLANES * CY), :] = total[NEW:, at]
        ready = k - LAG * (1 - core)

        @pl.when(ready >= 0)
        def _():
            send_new(ready).start()

        @pl.when(jnp.logical_and(k == 3, jnp.logical_not(early)))
        def _():
            for n in range(PIECES):
                outer[n].wait_recv()
                passed[n].start()

        return 0

    lax.fori_loop(0, TILES, make, 0)

    @pl.when(core == 0)
    def _():
        for k in range(TILES - LAG, TILES):
            send_new(k).start()


    work[...] = whole[2 * PREV :].T
    corr[...] = work[pl.ds(pl.multiple_of(PREV * band, PREV), PREV), 0 : 2 * NEW]

    inner.wait()
    for copy in passed:
        copy.wait_recv()

    def far(o, _):
        for p in range(PLANES):
            total = applied[o, p]
            for step in range(1, DEPTH + 1):
                total = total - (0.5 * coeffs[step]) * (
                    ext[o, p + DEPTH + step] + ext[o, p + DEPTH - step]
                )
            applied[o, p] = total
        return 0

    lax.fori_loop(0, ORB, far, 0)
    for copy in sent + outer + passed:
        copy.wait_send()

    @pl.when(early)
    def _():
        for copy in along_x + [back]:
            copy.wait_send()

    @pl.when(jnp.logical_not(early))
    def _():
        to_twin.wait_send()


    def finish(k, _):
        send_new(k).wait()
        return 0

    lax.fori_loop(0, TILES, finish, 0)


def hand_over(a, b, c, a_out, b_out, c_out, sems):
    copies = []
    for n in range(2):
        part = pl.ds(n * (ORB // 2), ORB // 2)
        copies.append(pltpu.make_async_copy(a.at[part], a_out.at[part], sems.at[n]))
    for n in range(4):
        part = pl.ds(n * (NEW // 4), NEW // 4)
        copies.append(pltpu.make_async_copy(c.at[part], c_out.at[part], sems.at[2 + n]))
    copies.append(pltpu.make_async_copy(b, b_out, sems.at[6]))
    for copy in copies:
        copy.start()
    for copy in copies:
        copy.wait()


def on_device(orbitals, potential, earlier, incoming):
    dma = pltpu.SemaphoreType.DMA
    any_ = pl.BlockSpec(memory_space=pl.ANY)
    shapes = (
        jax.ShapeDtypeStruct(orbitals.shape, F32),
        jax.ShapeDtypeStruct((PREV, 2 * NEW), F32),
        jax.ShapeDtypeStruct(incoming.shape, F32),
    )
    held = tuple(pltpu.VMEM(shape.shape, shape.dtype) for shape in shapes)
    in_vmem = pl.BlockSpec(memory_space=pltpu.VMEM)
    arguments = [
        pltpu.with_memory_space_constraint(a, pltpu.HBM)
        for a in (orbitals, potential, earlier, incoming)
    ]
    results = pl.pallas_call(
        kernel,
        out_shape=held,
        in_specs=[any_] * 4,
        out_specs=(in_vmem,) * 3,
        scratch_shapes=[
            pltpu.VMEM((CHUNKS, HALF_ROWS, CHUNK_Y, CZ), F32),
            pltpu.VMEM((CHUNKS, ROWS, CHUNK_Y, CZ), F32),
            pltpu.VMEM((ROWS, CELLS), BF16),
            pltpu.VMEM((ROWS, CELLS), BF16),
            pltpu.VMEM((ORB, PLANES + 2 * DEPTH, CY, CZ), F32),
            pltpu.VMEM((PLANES, CY, CZ), F32),
            pltpu.VMEM((ORB, DEPTH, CY, CZ), F32),
            pltpu.VMEM((ROWS, ROWS), F32),
            pltpu.VMEM((256, 128), F32),
            pltpu.VMEM((3, 64, 128), F32),
            pltpu.VMEM((64, 128), F32),
            pltpu.VMEM((3, 16, 128), F32),
            pltpu.VMEM((16, 128), F32),
            pltpu.VMEM((16, 128), F32),
            pltpu.VMEM((16, 128), F32),
            pltpu.VMEM((4, 16, 128), F32),
            pltpu.VMEM((64, 128), F32),
            pltpu.VMEM((256, 128), F32),
            pltpu.VMEM((128, 128), F32),
            pltpu.VMEM((64, 128), F32),
            pltpu.VMEM((NEW, KEPT, CY, CZ), F32),
            pltpu.VMEM((CZ, CZ), F32),
            pltpu.VMEM((PLANES * CY, PLANES * CY), F32),
            dma((CHUNKS,)), dma((CHUNKS,)), dma((CHUNKS, 2)), dma((CHUNKS, 2)), dma((2,)),
            dma, dma, dma((PIECES,)), dma((PIECES,)), dma((PIECES,)), dma((PIECES,)),
            dma((3,)), dma((3,)), dma((3,)), dma((3,)), dma, dma, dma((7,)), dma((4,)),
            dma((3,)), dma((3,)), dma((3,)), dma((3,)),
            dma((TILES,)), dma((TILES,)),
            pltpu.SemaphoreType.REGULAR, pltpu.SemaphoreType.REGULAR,
        ],
        compiler_params=pltpu.CompilerParams(
            collective_id=0, has_side_effects=True, vmem_limit_bytes=50 * 2**20
        ),
        cost_estimate=pl.CostEstimate(
            flops=6 * 10**9, bytes_accessed=22 * 10**6, transcendentals=0
        ),
    )(*arguments)
    return pl.pallas_call(
        hand_over,
        out_shape=shapes,
        in_specs=[any_] * 3,
        out_specs=(any_,) * 3,
        scratch_shapes=[dma((7,))],
        compiler_params=pltpu.CompilerParams(vmem_limit_bytes=50 * 2**20),
        cost_estimate=pl.CostEstimate(flops=0, bytes_accessed=13 * 10**6, transcendentals=0),
    )(*[pltpu.with_memory_space_constraint(a, pltpu.VMEM) for a in results])


def solution(mesh):
    in_specs = (
        P("band", "domain", None, None),
        P("domain", None, None),
        P("band", "domain", None, None),
        P("band", "domain", None, None),
    )
    out_specs = (P("band", "domain", None, None), P("band", None), P("band", "domain", None, None))
    return jax.shard_map(
        on_device, mesh=mesh, in_specs=in_specs, out_specs=out_specs, check_vma=False
    )
```

```python
import jax
import jax.numpy as jnp
from jax import lax
from jax.experimental import pallas as pl
from jax.experimental.pallas import tpu as pltpu
from jax.sharding import PartitionSpec as P

coeffs = (
    -5369.0 / 1800.0,
    12.0 / 7.0,
    -15.0 / 56.0,
    10.0 / 189.0,
    -1.0 / 112.0,
    2.0 / 1925.0,
    -1.0 / 16632.0,
)

MESH = pl.DeviceIdType.MESH
HIGH = lax.Precision.HIGHEST
F32 = jnp.float32
BF16 = jnp.bfloat16

ORB = 16
PREV = 64
NEW = 32
PLANES = 8
KEPT = 4
CY = 32
CZ = 128
DEPTH = 6
ROWS = 2 * PREV + 2 * NEW
HALF_ROWS = PREV + NEW
ORDER = (
    (0, PREV, 0),
    (HALF_ROWS, PREV, PREV),
    (PREV, NEW, 2 * PREV),
    (HALF_ROWS + PREV, NEW, 2 * PREV + NEW),
)
CELLS = KEPT * CY * CZ
TOTAL = 512 * CY * CZ

CHUNKS = 16
CHUNK_Y = KEPT * CY // CHUNKS
AHEAD = 2
NEAR = -(-ORB // (CHUNKS - 1))
PIECES = 4
TILES = 16
TILE_Y = KEPT * CY // TILES


def nt(a, b, precision=None):
    return lax.dot_general(
        a, b, (((1,), (1,)), ((), ())), precision=precision, preferred_element_type=F32
    )


def nn(a, b, precision=None):
    return lax.dot_general(
        a, b, (((1,), (0,)), ((), ())), precision=precision, preferred_element_type=F32
    )


def split(a):
    hi = a.astype(BF16)
    return hi, (a - hi.astype(F32)).astype(BF16)


def band_matrix(size, block, diagonal):
    i = lax.broadcasted_iota(jnp.int32, (size, size), 0)
    j = lax.broadcasted_iota(jnp.int32, (size, size), 1)
    gap = jnp.abs(i - j)
    out = jnp.where(gap == 0, diagonal, 0.0).astype(F32)
    for step in range(1, DEPTH + 1):
        out = jnp.where(gap == step, -0.5 * coeffs[step], out)
    if block != size:
        out = jnp.where(i // block == j // block, out, 0.0)
    return out


def kernel(
    orb, pot, earl, inc,
    applied, corr, ortho,
    to_give, rows, high, low, ext, potv, relay, grams, red,
    got_z, sum_z, got_y, part, twin_part, pair, got_x, whole_y, whole, work, factor, outs, band_z, band_y,
    s1, r1, l1, l2, l0,
    s_in, r_in, s_out, r_relay, s_fwd, r_out,
    sz, rz, sy, ry, s_twin, r_twin, sx, rx, sgy, rgy, sgz, rgz,
    s2, r2, go, all_in,
):
    band = lax.axis_index("band")
    domain = lax.axis_index("domain")
    core = domain % 2
    x = ((domain // 2) % 2) * 2 + band
    y = (domain // 4) % 4
    z = domain // 16
    other = 1 - band

    def device(xx, yy, zz, cc):
        return (xx % 2, ((zz * 4 + yy) * 2 + xx // 2) * 2 + cc)

    z_peers = [device(x, y, (z + d) % 4, core) for d in range(1, 4)]
    y_peers = [device(x, (y + d) % 4, z, core) for d in range(1, 4)]
    partner = (other, domain)
    twin = (band, domain + 1 - 2 * core)
    toward = 2 * core - 1
    early = (band + core + 1) % 2
    next_domain = (domain + toward + 64) % 64
    via_y = early * ((next_domain // 4) % 4) + (1 - early) * y
    via_z = early * (next_domain // 16) + (1 - early) * z
    relayer = device((x + toward + 4) % 4, via_y, via_z, 1 - core)
    from_domain = ((z * 4 + y) * 2 + ((x + toward + 4) % 4) // 2) * 2 + 1 - core
    straight = ((z * 4 + y) * 2 + ((x - toward + 4) % 4) // 2) * 2 + core
    to_domain = (early * straight + (1 - early) * (from_domain - toward) + 64) % 64
    forward = (other, to_domain)
    way = 2 * band - 1
    chip = (z * 4 + y) * 2
    to = (chip + x // 2) * 2 + band + way + 64
    to = to % 64
    chip_passer = device(
        (((to // 2) % 2) * 2 + band - way + 4) % 4, (to // 4) % 4, to // 16, 1
    )
    giver_domain = ((chip + ((x - way + 4) % 4) // 2) * 2 + band + way + 64) % 64
    chip_giver = (other, giver_domain - giver_domain % 2 + 1)
    early = early == 1

    def piece(planes, k):
        plane = planes + k // (CY // CHUNK_Y)
        at = pl.multiple_of((k % (CY // CHUNK_Y)) * CHUNK_Y, CHUNK_Y)
        return plane, pl.ds(at, CHUNK_Y)

    def stage(k):
        plane, at = piece(KEPT * other, k)
        return (
            pltpu.make_async_copy(earl.at[:, plane, at], to_give.at[k, 0:PREV], l1.at[k, 0]),
            pltpu.make_async_copy(inc.at[:, plane, at], to_give.at[k, PREV:], l1.at[k, 1]),
        )

    def own(k):
        plane, at = piece(KEPT * band, k)
        return (
            pltpu.make_async_copy(
                earl.at[:, plane, at], rows.at[k, pl.ds(HALF_ROWS * band, PREV)], l2.at[k, 0]
            ),
            pltpu.make_async_copy(
                inc.at[:, plane, at], rows.at[k, pl.ds(HALF_ROWS * band + PREV, NEW)], l2.at[k, 1]
            ),
        )

    for k in range(AHEAD):
        for copy in stage(k):
            copy.start()

    barrier = pltpu.get_barrier_semaphore()
    first, second = core == 0, core == 1

    def greet(peer):
        pl.semaphore_signal(barrier, inc=1, device_id=peer, device_id_type=MESH)

    def tell(semaphore):
        pl.semaphore_signal(semaphore, inc=1, device_id=twin, device_id_type=MESH)

    @pl.when(second)
    def _():
        greet(twin)
        greet((other, domain - 1))

    @pl.when(first)
    def _():
        greet(partner)

    @pl.when(first)
    def _():
        pl.semaphore_wait(barrier, 3)
        tell(go)

    @pl.when(second)
    def _():
        pl.semaphore_wait(go, 1)

    def remote(src, dst, send, recv, peer):
        return pltpu.make_async_remote_copy(
            src_ref=src, dst_ref=dst, send_sem=send, recv_sem=recv,
            device_id=peer, device_id_type=MESH,
        )

    def give(k):
        return remote(
            to_give.at[k], rows.at[k, pl.ds(HALF_ROWS * band, HALF_ROWS)],
            s1.at[k], r1.at[k], partner,
        )

    for k in range(AHEAD):
        for copy in stage(k):
            copy.wait()
        give(k).start()

    def fetch(k, _):
        for copy in own(k):
            copy.start()

        @pl.when(k + AHEAD < CHUNKS)
        def _():
            for copy in stage(k + AHEAD):
                copy.start()

        return 0

    @pl.when(second)
    def _():
        for d in range(1, 4):
            greet(device(x, y, (z + d) % 4, 1))
            greet(device(x, (y + d) % 4, z, 1))
            greet(device((x + d) % 4, y, z, 1))
        greet(chip_passer)
        greet(chip_giver)

    inner = remote(
        orb.at[:, pl.ds(2 * (1 - core), DEPTH)], ext.at[:, pl.ds(14 * core, DEPTH)],
        s_in, r_in, twin,
    )
    outer, passed = [], []
    for n in range(PIECES):
        some = pl.ds(n * (ORB // PIECES), ORB // PIECES)
        outer.append(
            remote(
                orb.at[some, pl.ds(2 * core, DEPTH)], relay.at[some],
                s_out.at[n], r_relay.at[n], relayer,
            )
        )
        passed.append(
            remote(
                relay.at[some], ext.at[some, pl.ds(14 * core, DEPTH)],
                s_fwd.at[n], r_out.at[n], forward,
            )
        )

    locals_ = [
        pltpu.make_async_copy(orb, ext.at[:, pl.ds(DEPTH, PLANES)], l0.at[0]),
        pltpu.make_async_copy(pot, potv, l0.at[1]),
    ]
    for copy in locals_:
        copy.start()
    lax.fori_loop(0, CHUNKS, fetch, 0)
    inner.start()

    band_z[...] = band_matrix(CZ, CZ, -1.5 * coeffs[0])
    band_y[...] = band_matrix(PLANES * CY, CY, 0.0)
    for copy in locals_:
        copy.wait()

    def near(o, _):
        cells = ext[o, DEPTH : DEPTH + PLANES].reshape(PLANES * CY, CZ)
        field = potv[...].reshape(PLANES * CY, CZ)
        total = field * cells + nn(cells, band_z[...], HIGH) + nn(band_y[...], cells, HIGH)
        applied[o] = total.reshape(PLANES, CY, CZ)
        return 0

    grams[...] = jnp.zeros_like(grams)
    flat_rows = rows.reshape(CHUNKS * ROWS * CHUNK_Y, CZ)

    def take(k, _):
        give(k).wait_recv()
        give(k).wait_send()

        @pl.when(k + AHEAD < CHUNKS)
        def _():
            for copy in stage(k + AHEAD):
                copy.wait()
            give(k + AHEAD).start()

        for copy in own(k):
            copy.wait()

        @pl.when(jnp.logical_and(k == 2, second))
        def _():
            pl.semaphore_wait(barrier, 11)
            tell(all_in)

        @pl.when(jnp.logical_and(k == 2, first))
        def _():
            pl.semaphore_wait(all_in, 1)

        @pl.when(jnp.logical_and(k == 2, early))
        def _():
            for copy in outer:
                copy.start()

        @pl.when(jnp.logical_and(k == CHUNKS - 1, jnp.logical_not(early)))
        def _():
            for copy in outer:
                copy.start()

        @pl.when(jnp.logical_and(k == CHUNKS - 1, early))
        def _():
            outer[0].wait_recv()
            passed[0].start()

        base = pl.multiple_of(k * CHUNK_Y, CHUNK_Y)
        start = pl.multiple_of(k * (ROWS * CHUNK_Y), ROWS * CHUNK_Y)
        for i in range(CHUNK_Y):
            at = pl.ds(pl.multiple_of((base + i) * CZ, CZ), CZ)
            for row, count, to in ORDER:
                hi, lo = split(
                    flat_rows[pl.ds(start + row * CHUNK_Y + i, count, stride=CHUNK_Y), :]
                )
                high[to : to + count, at] = hi
                low[to : to + count, at] = lo
        at = pl.ds(pl.multiple_of(base * CZ, CHUNK_Y * CZ), CHUNK_Y * CZ)
        hi, lo = high[:, at], low[:, at]
        grams[...] += nt(hi, hi) + nt(hi, lo) + nt(lo, hi)

        @pl.when(k < CHUNKS - 1)
        def _():
            lax.fori_loop(k * NEAR, jnp.minimum((k + 1) * NEAR, ORB), near, 0)

        return 0

    lax.fori_loop(0, CHUNKS, take, 0)

    red[0:ROWS, :] = grams[:, 0 : 2 * PREV]
    red[ROWS:, :] = jnp.zeros((2 * NEW, 2 * PREV), F32)
    red[ROWS:, 0 : 2 * NEW] = grams[2 * PREV :, 2 * PREV :]

    sent = []
    def quarter(size, index):
        return pl.ds(pl.multiple_of(size * index, size), size)

    copies = [
        remote(
            red.at[quarter(64, (z + d) % 4)], got_z.at[d - 1],
            sz.at[d - 1], rz.at[d - 1], z_peers[d - 1],
        )
        for d in range(1, 4)
    ]
    for copy in copies:
        copy.start()
    for copy in copies:
        copy.wait_recv()
    sent = sent + copies
    sum_z[...] = red[quarter(64, z)] + got_z[0] + got_z[1] + got_z[2]
    copies = [
        remote(
            sum_z.at[quarter(16, (y + d) % 4)], got_y.at[d - 1],
            sy.at[d - 1], ry.at[d - 1], y_peers[d - 1],
        )
        for d in range(1, 4)
    ]
    for copy in copies:
        copy.start()
    for copy in copies:
        copy.wait_recv()
    sent = sent + copies
    part[...] = sum_z[quarter(16, y)] + got_y[0] + got_y[1] + got_y[2]
    to_twin = remote(part, twin_part, s_twin, r_twin, twin)
    along_x = [
        remote(
            pair, got_x.at[x], sx.at[2 * d + c], rx.at[d],
            device((x + d + 1) % 4, y, z, c),
        )
        for d in range(3)
        for c in range(2)
    ]
    back = remote(pair, got_x.at[x], sx.at[6], rx.at[3], twin)

    @pl.when(jnp.logical_not(early))
    def _():
        to_twin.start()

    @pl.when(early)
    def _():
        to_twin.wait_recv()
        pair[...] = part[...] + twin_part[...]
        for copy in along_x:
            copy.start()
        back.start()
        for n in range(1, PIECES):
            outer[n].wait_recv()
            passed[n].start()
        got_x[x] = pair[...]

    @pl.when(jnp.logical_not(early))
    def _():
        back.wait_recv()

    for copy in along_x[::2]:
        copy.wait_recv()
    total = got_x[0]
    for d in range(1, 4):
        total = total + got_x[d]
    whole_y[quarter(16, y)] = total * (1.0 / TOTAL)
    copies = [
        remote(
            whole_y.at[quarter(16, y)], whole_y.at[quarter(16, y)],
            sgy.at[d - 1], rgy.at[d - 1], y_peers[d - 1],
        )
        for d in range(1, 4)
    ]
    for copy in copies:
        copy.start()
    for copy in copies:
        copy.wait_recv()
    sent = sent + copies
    whole[quarter(64, z)] = whole_y[...]
    copies = [
        remote(
            whole_y, whole.at[quarter(64, z)], sgz.at[d - 1], rgz.at[d - 1], z_peers[d - 1]
        )
        for d in range(1, 4)
    ]
    for copy in copies:
        copy.start()
    for copy in copies:
        copy.wait_recv()
    sent = sent + copies

    corr_t = whole[2 * PREV : 2 * PREV + 2 * NEW]
    i = lax.broadcasted_iota(jnp.int32, (128, 128), 0)
    j = lax.broadcasted_iota(jnp.int32, (128, 128), 1)
    middle = whole[0 : 2 * PREV] - jnp.where(i == j, 2.0, 0.0)
    gram = whole[ROWS:, 0 : 2 * NEW] + nt(nn(corr_t, middle, HIGH), corr_t, HIGH)
    i = lax.broadcasted_iota(jnp.int32, (64, 128), 0)
    j = lax.broadcasted_iota(jnp.int32, (64, 128), 1)
    factor[...] = jnp.where(j == i + 64, 1.0, 0.0)
    factor[:, 0:64] = gram

    both = factor[...]
    for first in range(0, 64, 4):
        columns = [
            jnp.broadcast_to(both[:, first + n : first + n + 1], (64, 128)) for n in range(4)
        ]
        for n in range(4):
            step = first + n
            pivot = 1.0 / columns[n][step : step + 1]
            below = jnp.where(i > step, columns[n] * pivot, 0.0)
            both = both - below * both[step : step + 1]
            for m in range(n + 1, 4):
                columns[m] = columns[m] - below * columns[m][step : step + 1]
    pivots = jnp.sum(jnp.where(i == j, both, 0.0), axis=1, keepdims=True)
    root = lax.rsqrt(pivots)
    root = root * (1.5 - 0.5 * pivots * root * root)
    factor[...] = both * root
    inverse = factor[:, 64:128]
    inverse_hi, inverse_lo = split(inverse)
    corr_hi, corr_lo = split(corr_t)
    work[0:64] = -(
        nn(inverse_hi, corr_hi) + (nn(inverse_hi, corr_lo) + nn(inverse_lo, corr_hi))
    )
    theirs, own = pl.ds(NEW * other, NEW), pl.ds(NEW * band, NEW)
    prev_hi, prev_lo = split(jnp.concatenate([work[theirs], work[own]], axis=0))
    new_hi, new_lo = split(
        jnp.concatenate([factor[theirs, 64:128], factor[own, 64:128]], axis=0)
    )
    hi = jnp.concatenate([prev_hi, new_hi], axis=1)
    lo = jnp.concatenate([prev_lo, new_lo], axis=1)
    stacked = jnp.concatenate([hi, lo], axis=0)

    flat_outs = outs.reshape(NEW * KEPT * CY, CZ)
    flat_ortho = ortho.reshape(NEW * PLANES * CY, CZ)
    kept = pl.multiple_of(band * (KEPT * CY), KEPT * CY)

    def tile(k):
        return k // (CY // TILE_Y), pl.ds(
            pl.multiple_of((k % (CY // TILE_Y)) * TILE_Y, TILE_Y), TILE_Y
        )

    def send_new(k):
        plane, at = tile(k)
        return remote(
            outs.at[:, plane, at],
            ortho.at[:, KEPT * band + plane, at],
            s2.at[k], r2.at[k], partner,
        )

    def make(k, _):
        base = pl.multiple_of(k * TILE_Y, TILE_Y)
        at = pl.ds(pl.multiple_of(base * CZ, TILE_Y * CZ), TILE_Y * CZ)
        both = nn(stacked, high[:, at])
        total = both[0:64] + both[64:128] + nn(hi, low[:, at])
        for n in range(TILE_Y):
            at = slice(n * CZ, (n + 1) * CZ)
            flat_outs[pl.ds(base + n, NEW, stride=KEPT * CY), :] = total[:NEW, at]
            flat_ortho[pl.ds(kept + base + n, NEW, stride=PLANES * CY), :] = total[NEW:, at]
        send_new(k).start()

        @pl.when(jnp.logical_and(k == 3, jnp.logical_not(early)))
        def _():
            for n in range(PIECES):
                outer[n].wait_recv()
                passed[n].start()

        return 0

    lax.fori_loop(0, TILES, make, 0)

    work[...] = whole[2 * PREV :].T
    corr[...] = work[pl.ds(pl.multiple_of(PREV * band, PREV), PREV), 0 : 2 * NEW]

    inner.wait()
    for copy in passed:
        copy.wait_recv()

    def far(o, _):
        for p in range(PLANES):
            total = applied[o, p]
            for step in range(1, DEPTH + 1):
                total = total - (0.5 * coeffs[step]) * (
                    ext[o, p + DEPTH + step] + ext[o, p + DEPTH - step]
                )
            applied[o, p] = total
        return 0

    lax.fori_loop(0, ORB, far, 0)
    for copy in sent + outer + passed:
        copy.wait_send()

    @pl.when(early)
    def _():
        for copy in along_x + [back]:
            copy.wait_send()

    @pl.when(jnp.logical_not(early))
    def _():
        to_twin.wait_send()


    def finish(k, _):
        send_new(k).wait()
        return 0

    lax.fori_loop(0, TILES, finish, 0)


def hand_over(a, b, c, a_out, b_out, c_out, sems):
    copies = []
    for n in range(2):
        part = pl.ds(n * (ORB // 2), ORB // 2)
        copies.append(pltpu.make_async_copy(a.at[part], a_out.at[part], sems.at[n]))
    for n in range(4):
        part = pl.ds(n * (NEW // 4), NEW // 4)
        copies.append(pltpu.make_async_copy(c.at[part], c_out.at[part], sems.at[2 + n]))
    copies.append(pltpu.make_async_copy(b, b_out, sems.at[6]))
    for copy in copies:
        copy.start()
    for copy in copies:
        copy.wait()


def on_device(orbitals, potential, earlier, incoming):
    dma = pltpu.SemaphoreType.DMA
    any_ = pl.BlockSpec(memory_space=pl.ANY)
    shapes = (
        jax.ShapeDtypeStruct(orbitals.shape, F32),
        jax.ShapeDtypeStruct((PREV, 2 * NEW), F32),
        jax.ShapeDtypeStruct(incoming.shape, F32),
    )
    held = tuple(pltpu.VMEM(shape.shape, shape.dtype) for shape in shapes)
    in_vmem = pl.BlockSpec(memory_space=pltpu.VMEM)
    arguments = [
        pltpu.with_memory_space_constraint(a, pltpu.HBM)
        for a in (orbitals, potential, earlier, incoming)
    ]
    results = pl.pallas_call(
        kernel,
        out_shape=held,
        in_specs=[any_] * 4,
        out_specs=(in_vmem,) * 3,
        scratch_shapes=[
            pltpu.VMEM((CHUNKS, HALF_ROWS, CHUNK_Y, CZ), F32),
            pltpu.VMEM((CHUNKS, ROWS, CHUNK_Y, CZ), F32),
            pltpu.VMEM((ROWS, CELLS), BF16),
            pltpu.VMEM((ROWS, CELLS), BF16),
            pltpu.VMEM((ORB, PLANES + 2 * DEPTH, CY, CZ), F32),
            pltpu.VMEM((PLANES, CY, CZ), F32),
            pltpu.VMEM((ORB, DEPTH, CY, CZ), F32),
            pltpu.VMEM((ROWS, ROWS), F32),
            pltpu.VMEM((256, 128), F32),
            pltpu.VMEM((3, 64, 128), F32),
            pltpu.VMEM((64, 128), F32),
            pltpu.VMEM((3, 16, 128), F32),
            pltpu.VMEM((16, 128), F32),
            pltpu.VMEM((16, 128), F32),
            pltpu.VMEM((16, 128), F32),
            pltpu.VMEM((4, 16, 128), F32),
            pltpu.VMEM((64, 128), F32),
            pltpu.VMEM((256, 128), F32),
            pltpu.VMEM((128, 128), F32),
            pltpu.VMEM((64, 128), F32),
            pltpu.VMEM((NEW, KEPT, CY, CZ), F32),
            pltpu.VMEM((CZ, CZ), F32),
            pltpu.VMEM((PLANES * CY, PLANES * CY), F32),
            dma((CHUNKS,)), dma((CHUNKS,)), dma((CHUNKS, 2)), dma((CHUNKS, 2)), dma((2,)),
            dma, dma, dma((PIECES,)), dma((PIECES,)), dma((PIECES,)), dma((PIECES,)),
            dma((3,)), dma((3,)), dma((3,)), dma((3,)), dma, dma, dma((7,)), dma((4,)),
            dma((3,)), dma((3,)), dma((3,)), dma((3,)),
            dma((TILES,)), dma((TILES,)),
            pltpu.SemaphoreType.REGULAR, pltpu.SemaphoreType.REGULAR,
        ],
        compiler_params=pltpu.CompilerParams(
            collective_id=0, has_side_effects=True, vmem_limit_bytes=50 * 2**20
        ),
        cost_estimate=pl.CostEstimate(
            flops=6 * 10**9, bytes_accessed=22 * 10**6, transcendentals=0
        ),
    )(*arguments)
    return pl.pallas_call(
        hand_over,
        out_shape=shapes,
        in_specs=[any_] * 3,
        out_specs=(any_,) * 3,
        scratch_shapes=[dma((7,))],
        compiler_params=pltpu.CompilerParams(vmem_limit_bytes=50 * 2**20),
        cost_estimate=pl.CostEstimate(flops=0, bytes_accessed=13 * 10**6, transcendentals=0),
    )(*[pltpu.with_memory_space_constraint(a, pltpu.VMEM) for a in results])


def solution(mesh):
    in_specs = (
        P("band", "domain", None, None),
        P("domain", None, None),
        P("band", "domain", None, None),
        P("band", "domain", None, None),
    )
    out_specs = (P("band", "domain", None, None), P("band", None), P("band", "domain", None, None))
    return jax.shard_map(
        on_device, mesh=mesh, in_specs=in_specs, out_specs=out_specs, check_vma=False
    )
```

```python
import jax
import jax.numpy as jnp
from jax import lax
from jax.experimental import pallas as pl
from jax.experimental.pallas import tpu as pltpu
from jax.sharding import PartitionSpec as P

coeffs = (
    -5369.0 / 1800.0,
    12.0 / 7.0,
    -15.0 / 56.0,
    10.0 / 189.0,
    -1.0 / 112.0,
    2.0 / 1925.0,
    -1.0 / 16632.0,
)

MESH = pl.DeviceIdType.MESH
HIGH = lax.Precision.HIGHEST
F32 = jnp.float32
BF16 = jnp.bfloat16

ORB = 16
PREV = 64
NEW = 32
PLANES = 8
KEPT = 4
CY = 32
CZ = 128
DEPTH = 6
ROWS = 2 * PREV + 2 * NEW
HALF_ROWS = PREV + NEW
ORDER = (
    (0, PREV, 0),
    (HALF_ROWS, PREV, PREV),
    (PREV, NEW, 2 * PREV),
    (HALF_ROWS + PREV, NEW, 2 * PREV + NEW),
)
CELLS = KEPT * CY * CZ
TOTAL = 512 * CY * CZ

CHUNKS = 16
CHUNK_Y = KEPT * CY // CHUNKS
AHEAD = 2
NEAR = -(-ORB // (CHUNKS - 1))
PIECES = 4
TILES = 16
TILE_Y = KEPT * CY // TILES


def nt(a, b, precision=None):
    return lax.dot_general(
        a, b, (((1,), (1,)), ((), ())), precision=precision, preferred_element_type=F32
    )


def nn(a, b, precision=None):
    return lax.dot_general(
        a, b, (((1,), (0,)), ((), ())), precision=precision, preferred_element_type=F32
    )


def split(a):
    hi = a.astype(BF16)
    return hi, (a - hi.astype(F32)).astype(BF16)


def band_matrix(size, block, diagonal):
    i = lax.broadcasted_iota(jnp.int32, (size, size), 0)
    j = lax.broadcasted_iota(jnp.int32, (size, size), 1)
    gap = jnp.abs(i - j)
    out = jnp.where(gap == 0, diagonal, 0.0).astype(F32)
    for step in range(1, DEPTH + 1):
        out = jnp.where(gap == step, -0.5 * coeffs[step], out)
    if block != size:
        out = jnp.where(i // block == j // block, out, 0.0)
    return out


def kernel(
    orb, pot, earl, inc,
    applied, corr, ortho,
    to_give, rows, high, low, ext, potv, relay, grams, red,
    got_z, sum_z, got_y, part, twin_part, pair, got_x, whole_y, whole, work, factor, outs, band_z, band_y,
    s1, r1, l1, l2, l0,
    s_in, r_in, s_out, r_relay, s_fwd, r_out,
    sz, rz, sy, ry, s_twin, r_twin, sx, rx, sgy, rgy, sgz, rgz,
    s2, r2, go, all_in,
):
    band = lax.axis_index("band")
    domain = lax.axis_index("domain")
    core = domain % 2
    x = ((domain // 2) % 2) * 2 + band
    y = (domain // 4) % 4
    z = domain // 16
    other = 1 - band

    def device(xx, yy, zz, cc):
        return (xx % 2, ((zz * 4 + yy) * 2 + xx // 2) * 2 + cc)

    z_peers = [device(x, y, (z + d) % 4, core) for d in range(1, 4)]
    y_peers = [device(x, (y + d) % 4, z, core) for d in range(1, 4)]
    partner = (other, domain)
    twin = (band, domain + 1 - 2 * core)
    toward = 2 * core - 1
    early = (band + core + 1) % 2
    next_domain = (domain + toward + 64) % 64
    via_y = early * ((next_domain // 4) % 4) + (1 - early) * y
    via_z = early * (next_domain // 16) + (1 - early) * z
    relayer = device((x + toward + 4) % 4, via_y, via_z, 1 - core)
    from_domain = ((z * 4 + y) * 2 + ((x + toward + 4) % 4) // 2) * 2 + 1 - core
    straight = ((z * 4 + y) * 2 + ((x - toward + 4) % 4) // 2) * 2 + core
    to_domain = (early * straight + (1 - early) * (from_domain - toward) + 64) % 64
    forward = (other, to_domain)
    way = 2 * band - 1
    chip = (z * 4 + y) * 2
    to = (chip + x // 2) * 2 + band + way + 64
    to = to % 64
    chip_passer = device(
        (((to // 2) % 2) * 2 + band - way + 4) % 4, (to // 4) % 4, to // 16, 1
    )
    giver_domain = ((chip + ((x - way + 4) % 4) // 2) * 2 + band + way + 64) % 64
    chip_giver = (other, giver_domain - giver_domain % 2 + 1)
    early = early == 1

    def piece(planes, k):
        plane = planes + k // (CY // CHUNK_Y)
        at = pl.multiple_of((k % (CY // CHUNK_Y)) * CHUNK_Y, CHUNK_Y)
        return plane, pl.ds(at, CHUNK_Y)

    def stage(k):
        plane, at = piece(KEPT * other, k)
        return (
            pltpu.make_async_copy(earl.at[:, plane, at], to_give.at[k, 0:PREV], l1.at[k, 0]),
            pltpu.make_async_copy(inc.at[:, plane, at], to_give.at[k, PREV:], l1.at[k, 1]),
        )

    def own(k):
        plane, at = piece(KEPT * band, k)
        return (
            pltpu.make_async_copy(
                earl.at[:, plane, at], rows.at[k, pl.ds(HALF_ROWS * band, PREV)], l2.at[k, 0]
            ),
            pltpu.make_async_copy(
                inc.at[:, plane, at], rows.at[k, pl.ds(HALF_ROWS * band + PREV, NEW)], l2.at[k, 1]
            ),
        )

    for k in range(AHEAD):
        for copy in stage(k):
            copy.start()

    barrier = pltpu.get_barrier_semaphore()
    first, second = core == 0, core == 1

    def greet(peer):
        pl.semaphore_signal(barrier, inc=1, device_id=peer, device_id_type=MESH)

    def tell(semaphore):
        pl.semaphore_signal(semaphore, inc=1, device_id=twin, device_id_type=MESH)

    @pl.when(second)
    def _():
        greet(twin)
        greet((other, domain - 1))

    @pl.when(first)
    def _():
        greet(partner)

    @pl.when(first)
    def _():
        pl.semaphore_wait(barrier, 3)
        tell(go)

    @pl.when(second)
    def _():
        pl.semaphore_wait(go, 1)

    def remote(src, dst, send, recv, peer):
        return pltpu.make_async_remote_copy(
            src_ref=src, dst_ref=dst, send_sem=send, recv_sem=recv,
            device_id=peer, device_id_type=MESH,
        )

    def give(k):
        return remote(
            to_give.at[k], rows.at[k, pl.ds(HALF_ROWS * band, HALF_ROWS)],
            s1.at[k], r1.at[k], partner,
        )

    for k in range(AHEAD):
        for copy in stage(k):
            copy.wait()
        give(k).start()

    def fetch(k, _):
        for copy in own(k):
            copy.start()

        @pl.when(k + AHEAD < CHUNKS)
        def _():
            for copy in stage(k + AHEAD):
                copy.start()

        return 0

    @pl.when(second)
    def _():
        for d in range(1, 4):
            greet(device(x, y, (z + d) % 4, 1))
            greet(device(x, (y + d) % 4, z, 1))
            greet(device((x + d) % 4, y, z, 1))
        greet(chip_passer)
        greet(chip_giver)

    inner = remote(
        orb.at[:, pl.ds(2 * (1 - core), DEPTH)], ext.at[:, pl.ds(14 * core, DEPTH)],
        s_in, r_in, twin,
    )
    outer, passed = [], []
    for n in range(PIECES):
        some = pl.ds(n * (ORB // PIECES), ORB // PIECES)
        outer.append(
            remote(
                orb.at[some, pl.ds(2 * core, DEPTH)], relay.at[some],
                s_out.at[n], r_relay.at[n], relayer,
            )
        )
        passed.append(
            remote(
                relay.at[some], ext.at[some, pl.ds(14 * core, DEPTH)],
                s_fwd.at[n], r_out.at[n], forward,
            )
        )

    locals_ = [
        pltpu.make_async_copy(orb, ext.at[:, pl.ds(DEPTH, PLANES)], l0.at[0]),
        pltpu.make_async_copy(pot, potv, l0.at[1]),
    ]
    for copy in locals_:
        copy.start()
    lax.fori_loop(0, CHUNKS, fetch, 0)
    inner.start()

    band_z[...] = band_matrix(CZ, CZ, -1.5 * coeffs[0])
    band_y[...] = band_matrix(PLANES * CY, CY, 0.0)
    for copy in locals_:
        copy.wait()

    def near(o, _):
        cells = ext[o, DEPTH : DEPTH + PLANES].reshape(PLANES * CY, CZ)
        field = potv[...].reshape(PLANES * CY, CZ)
        total = field * cells + nn(cells, band_z[...], HIGH) + nn(band_y[...], cells, HIGH)
        applied[o] = total.reshape(PLANES, CY, CZ)
        return 0

    grams[...] = jnp.zeros_like(grams)
    flat_rows = rows.reshape(CHUNKS * ROWS * CHUNK_Y, CZ)

    def take(k, _):
        give(k).wait_recv()
        give(k).wait_send()

        @pl.when(k + AHEAD < CHUNKS)
        def _():
            for copy in stage(k + AHEAD):
                copy.wait()
            give(k + AHEAD).start()

        for copy in own(k):
            copy.wait()

        @pl.when(jnp.logical_and(k == 2, second))
        def _():
            pl.semaphore_wait(barrier, 11)
            tell(all_in)

        @pl.when(jnp.logical_and(k == 2, first))
        def _():
            pl.semaphore_wait(all_in, 1)

        @pl.when(jnp.logical_and(k == 2, early))
        def _():
            for copy in outer:
                copy.start()

        @pl.when(jnp.logical_and(k == CHUNKS - 1, early))
        def _():
            outer[0].wait_recv()
            passed[0].start()

        base = pl.multiple_of(k * CHUNK_Y, CHUNK_Y)
        start = pl.multiple_of(k * (ROWS * CHUNK_Y), ROWS * CHUNK_Y)
        for i in range(CHUNK_Y):
            at = pl.ds(pl.multiple_of((base + i) * CZ, CZ), CZ)
            for row, count, to in ORDER:
                hi, lo = split(
                    flat_rows[pl.ds(start + row * CHUNK_Y + i, count, stride=CHUNK_Y), :]
                )
                high[to : to + count, at] = hi
                low[to : to + count, at] = lo
        at = pl.ds(pl.multiple_of(base * CZ, CHUNK_Y * CZ), CHUNK_Y * CZ)
        hi, lo = high[:, at], low[:, at]
        grams[...] += nt(hi, hi) + nt(hi, lo) + nt(lo, hi)

        @pl.when(jnp.logical_and(k == CHUNKS - 2, jnp.logical_not(early)))
        def _():
            for copy in outer:
                copy.start()

        @pl.when(k < CHUNKS - 1)
        def _():
            lax.fori_loop(k * NEAR, jnp.minimum((k + 1) * NEAR, ORB), near, 0)

        return 0

    lax.fori_loop(0, CHUNKS, take, 0)

    red[0:ROWS, :] = grams[:, 0 : 2 * PREV]
    red[ROWS:, :] = jnp.zeros((2 * NEW, 2 * PREV), F32)
    red[ROWS:, 0 : 2 * NEW] = grams[2 * PREV :, 2 * PREV :]

    sent = []
    def quarter(size, index):
        return pl.ds(pl.multiple_of(size * index, size), size)

    copies = [
        remote(
            red.at[quarter(64, (z + d) % 4)], got_z.at[d - 1],
            sz.at[d - 1], rz.at[d - 1], z_peers[d - 1],
        )
        for d in range(1, 4)
    ]
    for copy in copies:
        copy.start()
    for copy in copies:
        copy.wait_recv()
    sent = sent + copies
    sum_z[...] = red[quarter(64, z)] + got_z[0] + got_z[1] + got_z[2]
    copies = [
        remote(
            sum_z.at[quarter(16, (y + d) % 4)], got_y.at[d - 1],
            sy.at[d - 1], ry.at[d - 1], y_peers[d - 1],
        )
        for d in range(1, 4)
    ]
    for copy in copies:
        copy.start()
    for copy in copies:
        copy.wait_recv()
    sent = sent + copies
    part[...] = sum_z[quarter(16, y)] + got_y[0] + got_y[1] + got_y[2]
    to_twin = remote(part, twin_part, s_twin, r_twin, twin)
    along_x = [
        remote(
            pair, got_x.at[x], sx.at[2 * d + c], rx.at[d],
            device((x + d + 1) % 4, y, z, c),
        )
        for d in range(3)
        for c in range(2)
    ]
    back = remote(pair, got_x.at[x], sx.at[6], rx.at[3], twin)

    @pl.when(jnp.logical_not(early))
    def _():
        to_twin.start()

    @pl.when(early)
    def _():
        to_twin.wait_recv()
        pair[...] = part[...] + twin_part[...]
        for copy in along_x:
            copy.start()
        back.start()
        for n in range(1, PIECES):
            outer[n].wait_recv()
            passed[n].start()
        got_x[x] = pair[...]

    @pl.when(jnp.logical_not(early))
    def _():
        back.wait_recv()

    for copy in along_x[::2]:
        copy.wait_recv()
    total = got_x[0]
    for d in range(1, 4):
        total = total + got_x[d]
    whole_y[quarter(16, y)] = total * (1.0 / TOTAL)
    copies = [
        remote(
            whole_y.at[quarter(16, y)], whole_y.at[quarter(16, y)],
            sgy.at[d - 1], rgy.at[d - 1], y_peers[d - 1],
        )
        for d in range(1, 4)
    ]
    for copy in copies:
        copy.start()
    for copy in copies:
        copy.wait_recv()
    sent = sent + copies
    whole[quarter(64, z)] = whole_y[...]
    copies = [
        remote(
            whole_y, whole.at[quarter(64, z)], sgz.at[d - 1], rgz.at[d - 1], z_peers[d - 1]
        )
        for d in range(1, 4)
    ]
    for copy in copies:
        copy.start()
    for copy in copies:
        copy.wait_recv()
    sent = sent + copies

    corr_t = whole[2 * PREV : 2 * PREV + 2 * NEW]
    i = lax.broadcasted_iota(jnp.int32, (128, 128), 0)
    j = lax.broadcasted_iota(jnp.int32, (128, 128), 1)
    middle = whole[0 : 2 * PREV] - jnp.where(i == j, 2.0, 0.0)
    gram = whole[ROWS:, 0 : 2 * NEW] + nt(nn(corr_t, middle, HIGH), corr_t, HIGH)
    i = lax.broadcasted_iota(jnp.int32, (64, 128), 0)
    j = lax.broadcasted_iota(jnp.int32, (64, 128), 1)
    factor[...] = jnp.where(j == i + 64, 1.0, 0.0)
    factor[:, 0:64] = gram

    both = factor[...]
    for first in range(0, 64, 4):
        columns = [
            jnp.broadcast_to(both[:, first + n : first + n + 1], (64, 128)) for n in range(4)
        ]
        for n in range(4):
            step = first + n
            pivot = 1.0 / columns[n][step : step + 1]
            below = jnp.where(i > step, columns[n] * pivot, 0.0)
            both = both - below * both[step : step + 1]
            for m in range(n + 1, 4):
                columns[m] = columns[m] - below * columns[m][step : step + 1]
    pivots = jnp.sum(jnp.where(i == j, both, 0.0), axis=1, keepdims=True)
    root = lax.rsqrt(pivots)
    root = root * (1.5 - 0.5 * pivots * root * root)
    factor[...] = both * root
    inverse = factor[:, 64:128]
    inverse_hi, inverse_lo = split(inverse)
    corr_hi, corr_lo = split(corr_t)
    work[0:64] = -(
        nn(inverse_hi, corr_hi) + (nn(inverse_hi, corr_lo) + nn(inverse_lo, corr_hi))
    )
    theirs, own = pl.ds(NEW * other, NEW), pl.ds(NEW * band, NEW)
    prev_hi, prev_lo = split(jnp.concatenate([work[theirs], work[own]], axis=0))
    new_hi, new_lo = split(
        jnp.concatenate([factor[theirs, 64:128], factor[own, 64:128]], axis=0)
    )
    hi = jnp.concatenate([prev_hi, new_hi], axis=1)
    lo = jnp.concatenate([prev_lo, new_lo], axis=1)
    stacked = jnp.concatenate([hi, lo], axis=0)

    flat_outs = outs.reshape(NEW * KEPT * CY, CZ)
    flat_ortho = ortho.reshape(NEW * PLANES * CY, CZ)
    kept = pl.multiple_of(band * (KEPT * CY), KEPT * CY)

    def tile(k):
        return k // (CY // TILE_Y), pl.ds(
            pl.multiple_of((k % (CY // TILE_Y)) * TILE_Y, TILE_Y), TILE_Y
        )

    def send_new(k):
        plane, at = tile(k)
        return remote(
            outs.at[:, plane, at],
            ortho.at[:, KEPT * band + plane, at],
            s2.at[k], r2.at[k], partner,
        )

    def make(k, _):
        base = pl.multiple_of(k * TILE_Y, TILE_Y)
        at = pl.ds(pl.multiple_of(base * CZ, TILE_Y * CZ), TILE_Y * CZ)
        both = nn(stacked, high[:, at])
        total = both[0:64] + both[64:128] + nn(hi, low[:, at])
        for n in range(TILE_Y):
            at = slice(n * CZ, (n + 1) * CZ)
            flat_outs[pl.ds(base + n, NEW, stride=KEPT * CY), :] = total[:NEW, at]
            flat_ortho[pl.ds(kept + base + n, NEW, stride=PLANES * CY), :] = total[NEW:, at]
        send_new(k).start()

        @pl.when(jnp.logical_and(k == 3, jnp.logical_not(early)))
        def _():
            for n in range(PIECES):
                outer[n].wait_recv()
                passed[n].start()

        return 0

    lax.fori_loop(0, TILES, make, 0)

    work[...] = whole[2 * PREV :].T
    corr[...] = work[pl.ds(pl.multiple_of(PREV * band, PREV), PREV), 0 : 2 * NEW]

    inner.wait()
    for copy in passed:
        copy.wait_recv()

    def far(o, _):
        for p in range(PLANES):
            total = applied[o, p]
            for step in range(1, DEPTH + 1):
                total = total - (0.5 * coeffs[step]) * (
                    ext[o, p + DEPTH + step] + ext[o, p + DEPTH - step]
                )
            applied[o, p] = total
        return 0

    lax.fori_loop(0, ORB, far, 0)
    for copy in sent + outer + passed:
        copy.wait_send()

    @pl.when(early)
    def _():
        for copy in along_x + [back]:
            copy.wait_send()

    @pl.when(jnp.logical_not(early))
    def _():
        to_twin.wait_send()


    def finish(k, _):
        send_new(k).wait()
        return 0

    lax.fori_loop(0, TILES, finish, 0)


def hand_over(a, b, c, a_out, b_out, c_out, sems):
    copies = []
    for n in range(2):
        part = pl.ds(n * (ORB // 2), ORB // 2)
        copies.append(pltpu.make_async_copy(a.at[part], a_out.at[part], sems.at[n]))
    for n in range(4):
        part = pl.ds(n * (NEW // 4), NEW // 4)
        copies.append(pltpu.make_async_copy(c.at[part], c_out.at[part], sems.at[2 + n]))
    copies.append(pltpu.make_async_copy(b, b_out, sems.at[6]))
    for copy in copies:
        copy.start()
    for copy in copies:
        copy.wait()


def on_device(orbitals, potential, earlier, incoming):
    dma = pltpu.SemaphoreType.DMA
    any_ = pl.BlockSpec(memory_space=pl.ANY)
    shapes = (
        jax.ShapeDtypeStruct(orbitals.shape, F32),
        jax.ShapeDtypeStruct((PREV, 2 * NEW), F32),
        jax.ShapeDtypeStruct(incoming.shape, F32),
    )
    held = tuple(pltpu.VMEM(shape.shape, shape.dtype) for shape in shapes)
    in_vmem = pl.BlockSpec(memory_space=pltpu.VMEM)
    arguments = [
        pltpu.with_memory_space_constraint(a, pltpu.HBM)
        for a in (orbitals, potential, earlier, incoming)
    ]
    results = pl.pallas_call(
        kernel,
        out_shape=held,
        in_specs=[any_] * 4,
        out_specs=(in_vmem,) * 3,
        scratch_shapes=[
            pltpu.VMEM((CHUNKS, HALF_ROWS, CHUNK_Y, CZ), F32),
            pltpu.VMEM((CHUNKS, ROWS, CHUNK_Y, CZ), F32),
            pltpu.VMEM((ROWS, CELLS), BF16),
            pltpu.VMEM((ROWS, CELLS), BF16),
            pltpu.VMEM((ORB, PLANES + 2 * DEPTH, CY, CZ), F32),
            pltpu.VMEM((PLANES, CY, CZ), F32),
            pltpu.VMEM((ORB, DEPTH, CY, CZ), F32),
            pltpu.VMEM((ROWS, ROWS), F32),
            pltpu.VMEM((256, 128), F32),
            pltpu.VMEM((3, 64, 128), F32),
            pltpu.VMEM((64, 128), F32),
            pltpu.VMEM((3, 16, 128), F32),
            pltpu.VMEM((16, 128), F32),
            pltpu.VMEM((16, 128), F32),
            pltpu.VMEM((16, 128), F32),
            pltpu.VMEM((4, 16, 128), F32),
            pltpu.VMEM((64, 128), F32),
            pltpu.VMEM((256, 128), F32),
            pltpu.VMEM((128, 128), F32),
            pltpu.VMEM((64, 128), F32),
            pltpu.VMEM((NEW, KEPT, CY, CZ), F32),
            pltpu.VMEM((CZ, CZ), F32),
            pltpu.VMEM((PLANES * CY, PLANES * CY), F32),
            dma((CHUNKS,)), dma((CHUNKS,)), dma((CHUNKS, 2)), dma((CHUNKS, 2)), dma((2,)),
            dma, dma, dma((PIECES,)), dma((PIECES,)), dma((PIECES,)), dma((PIECES,)),
            dma((3,)), dma((3,)), dma((3,)), dma((3,)), dma, dma, dma((7,)), dma((4,)),
            dma((3,)), dma((3,)), dma((3,)), dma((3,)),
            dma((TILES,)), dma((TILES,)),
            pltpu.SemaphoreType.REGULAR, pltpu.SemaphoreType.REGULAR,
        ],
        compiler_params=pltpu.CompilerParams(
            collective_id=0, has_side_effects=True, vmem_limit_bytes=50 * 2**20
        ),
        cost_estimate=pl.CostEstimate(
            flops=6 * 10**9, bytes_accessed=22 * 10**6, transcendentals=0
        ),
    )(*arguments)
    return pl.pallas_call(
        hand_over,
        out_shape=shapes,
        in_specs=[any_] * 3,
        out_specs=(any_,) * 3,
        scratch_shapes=[dma((7,))],
        compiler_params=pltpu.CompilerParams(vmem_limit_bytes=50 * 2**20),
        cost_estimate=pl.CostEstimate(flops=0, bytes_accessed=13 * 10**6, transcendentals=0),
    )(*[pltpu.with_memory_space_constraint(a, pltpu.VMEM) for a in results])


def solution(mesh):
    in_specs = (
        P("band", "domain", None, None),
        P("domain", None, None),
        P("band", "domain", None, None),
        P("band", "domain", None, None),
    )
    out_specs = (P("band", "domain", None, None), P("band", None), P("band", "domain", None, None))
    return jax.shard_map(
        on_device, mesh=mesh, in_specs=in_specs, out_specs=out_specs, check_vma=False
    )
```

```python
import jax
import jax.numpy as jnp
from jax import lax
from jax.experimental import pallas as pl
from jax.experimental.pallas import tpu as pltpu
from jax.sharding import PartitionSpec as P

coeffs = (
    -5369.0 / 1800.0,
    12.0 / 7.0,
    -15.0 / 56.0,
    10.0 / 189.0,
    -1.0 / 112.0,
    2.0 / 1925.0,
    -1.0 / 16632.0,
)

MESH = pl.DeviceIdType.MESH
HIGH = lax.Precision.HIGHEST
F32 = jnp.float32
BF16 = jnp.bfloat16

ORB = 16
PREV = 64
NEW = 32
PLANES = 8
KEPT = 4
CY = 32
CZ = 128
DEPTH = 6
ROWS = 2 * PREV + 2 * NEW
HALF_ROWS = PREV + NEW
CELLS = KEPT * CY * CZ
TOTAL = 512 * CY * CZ

CHUNKS = 16
CHUNK_Y = KEPT * CY // CHUNKS
AHEAD = 2
NEAR = -(-ORB // (CHUNKS - 1))
PIECES = 4
TILES = 16
TILE_Y = KEPT * CY // TILES


def nt(a, b, precision=None):
    return lax.dot_general(
        a, b, (((1,), (1,)), ((), ())), precision=precision, preferred_element_type=F32
    )


def nn(a, b, precision=None):
    return lax.dot_general(
        a, b, (((1,), (0,)), ((), ())), precision=precision, preferred_element_type=F32
    )


def split(a):
    hi = a.astype(BF16)
    return hi, (a - hi.astype(F32)).astype(BF16)


def band_matrix(size, block, diagonal):
    i = lax.broadcasted_iota(jnp.int32, (size, size), 0)
    j = lax.broadcasted_iota(jnp.int32, (size, size), 1)
    gap = jnp.abs(i - j)
    out = jnp.where(gap == 0, diagonal, 0.0).astype(F32)
    for step in range(1, DEPTH + 1):
        out = jnp.where(gap == step, -0.5 * coeffs[step], out)
    if block != size:
        out = jnp.where(i // block == j // block, out, 0.0)
    return out


def kernel(
    orb, pot, earl, inc,
    applied, corr, ortho,
    to_give, rows, high, low, ext, potv, relay, grams, red,
    got_z, sum_z, got_y, part, twin_part, pair, got_x, whole_y, whole, work, factor, outs, band_z, band_y,
    s1, r1, l1, l2, l0,
    s_in, r_in, s_out, r_relay, s_fwd, r_out,
    sz, rz, sy, ry, s_twin, r_twin, sx, rx, sgy, rgy, sgz, rgz,
    s2, r2, go, all_in,
):
    band = lax.axis_index("band")
    domain = lax.axis_index("domain")
    core = domain % 2
    x = ((domain // 2) % 2) * 2 + band
    y = (domain // 4) % 4
    z = domain // 16
    other = 1 - band

    def device(xx, yy, zz, cc):
        return (xx % 2, ((zz * 4 + yy) * 2 + xx // 2) * 2 + cc)

    z_peers = [device(x, y, (z + d) % 4, core) for d in range(1, 4)]
    y_peers = [device(x, (y + d) % 4, z, core) for d in range(1, 4)]
    partner = (other, domain)
    twin = (band, domain + 1 - 2 * core)
    toward = 2 * core - 1
    early = (band + core + 1) % 2
    next_domain = (domain + toward + 64) % 64
    via_y = early * ((next_domain // 4) % 4) + (1 - early) * y
    via_z = early * (next_domain // 16) + (1 - early) * z
    relayer = device((x + toward + 4) % 4, via_y, via_z, 1 - core)
    from_domain = ((z * 4 + y) * 2 + ((x + toward + 4) % 4) // 2) * 2 + 1 - core
    straight = ((z * 4 + y) * 2 + ((x - toward + 4) % 4) // 2) * 2 + core
    to_domain = (early * straight + (1 - early) * (from_domain - toward) + 64) % 64
    forward = (other, to_domain)
    way = 2 * band - 1
    chip = (z * 4 + y) * 2
    to = (chip + x // 2) * 2 + band + way + 64
    to = to % 64
    chip_passer = device(
        (((to // 2) % 2) * 2 + band - way + 4) % 4, (to // 4) % 4, to // 16, 1
    )
    giver_domain = ((chip + ((x - way + 4) % 4) // 2) * 2 + band + way + 64) % 64
    chip_giver = (other, giver_domain - giver_domain % 2 + 1)
    early = early == 1

    def piece(planes, k):
        plane = planes + k // (CY // CHUNK_Y)
        at = pl.multiple_of((k % (CY // CHUNK_Y)) * CHUNK_Y, CHUNK_Y)
        return plane, pl.ds(at, CHUNK_Y)

    def stage(k):
        plane, at = piece(KEPT * other, k)
        return (
            pltpu.make_async_copy(earl.at[:, plane, at], to_give.at[k, 0:PREV], l1.at[k, 0]),
            pltpu.make_async_copy(inc.at[:, plane, at], to_give.at[k, PREV:], l1.at[k, 1]),
        )

    def own(k):
        plane, at = piece(KEPT * band, k)
        return (
            pltpu.make_async_copy(
                earl.at[:, plane, at], rows.at[k, pl.ds(HALF_ROWS * band, PREV)], l2.at[k, 0]
            ),
            pltpu.make_async_copy(
                inc.at[:, plane, at], rows.at[k, pl.ds(HALF_ROWS * band + PREV, NEW)], l2.at[k, 1]
            ),
        )

    for k in range(AHEAD):
        for copy in stage(k):
            copy.start()

    barrier = pltpu.get_barrier_semaphore()
    first, second = core == 0, core == 1

    def greet(peer):
        pl.semaphore_signal(barrier, inc=1, device_id=peer, device_id_type=MESH)

    def tell(semaphore):
        pl.semaphore_signal(semaphore, inc=1, device_id=twin, device_id_type=MESH)

    @pl.when(second)
    def _():
        greet(twin)
        greet((other, domain - 1))

    @pl.when(first)
    def _():
        greet(partner)

    @pl.when(first)
    def _():
        pl.semaphore_wait(barrier, 3)
        tell(go)

    @pl.when(second)
    def _():
        pl.semaphore_wait(go, 1)

    def remote(src, dst, send, recv, peer):
        return pltpu.make_async_remote_copy(
            src_ref=src, dst_ref=dst, send_sem=send, recv_sem=recv,
            device_id=peer, device_id_type=MESH,
        )

    def give(k):
        return remote(
            to_give.at[k], rows.at[k, pl.ds(HALF_ROWS * band, HALF_ROWS)],
            s1.at[k], r1.at[k], partner,
        )

    for k in range(AHEAD):
        for copy in stage(k):
            copy.wait()
        give(k).start()

    def fetch(k, _):
        for copy in own(k):
            copy.start()

        @pl.when(k + AHEAD < CHUNKS)
        def _():
            for copy in stage(k + AHEAD):
                copy.start()

        return 0

    @pl.when(second)
    def _():
        for d in range(1, 4):
            greet(device(x, y, (z + d) % 4, 1))
            greet(device(x, (y + d) % 4, z, 1))
            greet(device((x + d) % 4, y, z, 1))
        greet(chip_passer)
        greet(chip_giver)

    inner = remote(
        orb.at[:, pl.ds(2 * (1 - core), DEPTH)], ext.at[:, pl.ds(14 * core, DEPTH)],
        s_in, r_in, twin,
    )
    outer, passed = [], []
    for n in range(PIECES):
        some = pl.ds(n * (ORB // PIECES), ORB // PIECES)
        outer.append(
            remote(
                orb.at[some, pl.ds(2 * core, DEPTH)], relay.at[some],
                s_out.at[n], r_relay.at[n], relayer,
            )
        )
        passed.append(
            remote(
                relay.at[some], ext.at[some, pl.ds(14 * core, DEPTH)],
                s_fwd.at[n], r_out.at[n], forward,
            )
        )

    locals_ = [
        pltpu.make_async_copy(orb, ext.at[:, pl.ds(DEPTH, PLANES)], l0.at[0]),
        pltpu.make_async_copy(pot, potv, l0.at[1]),
    ]
    for copy in locals_:
        copy.start()
    lax.fori_loop(0, CHUNKS, fetch, 0)
    inner.start()

    band_z[...] = band_matrix(CZ, CZ, -1.5 * coeffs[0])
    band_y[...] = band_matrix(PLANES * CY, CY, 0.0)
    for copy in locals_:
        copy.wait()

    def near(o, _):
        cells = ext[o, DEPTH : DEPTH + PLANES].reshape(PLANES * CY, CZ)
        field = potv[...].reshape(PLANES * CY, CZ)
        total = field * cells + nn(cells, band_z[...], HIGH) + nn(band_y[...], cells, HIGH)
        applied[o] = total.reshape(PLANES, CY, CZ)
        return 0

    grams[...] = jnp.zeros_like(grams)
    flat_rows = rows.reshape(CHUNKS * ROWS * CHUNK_Y, CZ)

    def spread(k, side):
        base = pl.multiple_of(k * CHUNK_Y, CHUNK_Y)
        start = pl.multiple_of((k * 2 + side) * (HALF_ROWS * CHUNK_Y), HALF_ROWS * CHUNK_Y)
        places = ((0, PREV, PREV * side), (PREV, NEW, 2 * PREV + NEW * side))
        for i in range(CHUNK_Y):
            at = pl.ds(pl.multiple_of((base + i) * CZ, CZ), CZ)
            for row, count, to in places:
                hi, lo = split(
                    flat_rows[pl.ds(start + row * CHUNK_Y + i, count, stride=CHUNK_Y), :]
                )
                to = pl.ds(pl.multiple_of(to, NEW), count)
                high[to, at] = hi
                low[to, at] = lo

    def spread_own(k):
        for copy in own(k):
            copy.wait()
        spread(k, band)

    spread_own(0)

    def take(k, _):
        give(k).wait_recv()
        give(k).wait_send()

        @pl.when(k + AHEAD < CHUNKS)
        def _():
            for copy in stage(k + AHEAD):
                copy.wait()
            give(k + AHEAD).start()

        @pl.when(jnp.logical_and(k == 2, second))
        def _():
            pl.semaphore_wait(barrier, 11)
            tell(all_in)

        @pl.when(jnp.logical_and(k == 2, first))
        def _():
            pl.semaphore_wait(all_in, 1)

        @pl.when(jnp.logical_and(k == 2, early))
        def _():
            for copy in outer:
                copy.start()

        @pl.when(jnp.logical_and(k == CHUNKS - 1, early))
        def _():
            outer[0].wait_recv()
            passed[0].start()

        base = pl.multiple_of(k * CHUNK_Y, CHUNK_Y)
        spread(k, other)
        at = pl.ds(pl.multiple_of(base * CZ, CHUNK_Y * CZ), CHUNK_Y * CZ)
        hi, lo = high[:, at], low[:, at]
        grams[...] += nt(hi, hi) + nt(hi, lo) + nt(lo, hi)

        @pl.when(jnp.logical_and(k == CHUNKS - 2, jnp.logical_not(early)))
        def _():
            for copy in outer:
                copy.start()

        @pl.when(k < CHUNKS - 1)
        def _():
            spread_own(k + 1)
            lax.fori_loop(k * NEAR, jnp.minimum((k + 1) * NEAR, ORB), near, 0)

        return 0

    lax.fori_loop(0, CHUNKS, take, 0)

    red[0:ROWS, :] = grams[:, 0 : 2 * PREV]
    red[ROWS:, :] = jnp.zeros((2 * NEW, 2 * PREV), F32)
    red[ROWS:, 0 : 2 * NEW] = grams[2 * PREV :, 2 * PREV :]

    sent = []
    def quarter(size, index):
        return pl.ds(pl.multiple_of(size * index, size), size)

    copies = [
        remote(
            red.at[quarter(64, (z + d) % 4)], got_z.at[d - 1],
            sz.at[d - 1], rz.at[d - 1], z_peers[d - 1],
        )
        for d in range(1, 4)
    ]
    for copy in copies:
        copy.start()
    for copy in copies:
        copy.wait_recv()
    sent = sent + copies
    sum_z[...] = red[quarter(64, z)] + got_z[0] + got_z[1] + got_z[2]
    copies = [
        remote(
            sum_z.at[quarter(16, (y + d) % 4)], got_y.at[d - 1],
            sy.at[d - 1], ry.at[d - 1], y_peers[d - 1],
        )
        for d in range(1, 4)
    ]
    for copy in copies:
        copy.start()
    for copy in copies:
        copy.wait_recv()
    sent = sent + copies
    part[...] = sum_z[quarter(16, y)] + got_y[0] + got_y[1] + got_y[2]
    to_twin = remote(part, twin_part, s_twin, r_twin, twin)
    along_x = [
        remote(
            pair, got_x.at[x], sx.at[2 * d + c], rx.at[d],
            device((x + d + 1) % 4, y, z, c),
        )
        for d in range(3)
        for c in range(2)
    ]
    back = remote(pair, got_x.at[x], sx.at[6], rx.at[3], twin)

    @pl.when(jnp.logical_not(early))
    def _():
        to_twin.start()

    @pl.when(early)
    def _():
        to_twin.wait_recv()
        pair[...] = part[...] + twin_part[...]
        for copy in along_x:
            copy.start()
        back.start()
        for n in range(1, PIECES):
            outer[n].wait_recv()
            passed[n].start()
        got_x[x] = pair[...]

    @pl.when(jnp.logical_not(early))
    def _():
        back.wait_recv()

    for copy in along_x[::2]:
        copy.wait_recv()
    total = got_x[0]
    for d in range(1, 4):
        total = total + got_x[d]
    whole_y[quarter(16, y)] = total * (1.0 / TOTAL)
    copies = [
        remote(
            whole_y.at[quarter(16, y)], whole_y.at[quarter(16, y)],
            sgy.at[d - 1], rgy.at[d - 1], y_peers[d - 1],
        )
        for d in range(1, 4)
    ]
    for copy in copies:
        copy.start()
    for copy in copies:
        copy.wait_recv()
    sent = sent + copies
    whole[quarter(64, z)] = whole_y[...]
    copies = [
        remote(
            whole_y, whole.at[quarter(64, z)], sgz.at[d - 1], rgz.at[d - 1], z_peers[d - 1]
        )
        for d in range(1, 4)
    ]
    for copy in copies:
        copy.start()
    for copy in copies:
        copy.wait_recv()
    sent = sent + copies

    corr_t = whole[2 * PREV : 2 * PREV + 2 * NEW]
    i = lax.broadcasted_iota(jnp.int32, (128, 128), 0)
    j = lax.broadcasted_iota(jnp.int32, (128, 128), 1)
    middle = whole[0 : 2 * PREV] - jnp.where(i == j, 2.0, 0.0)
    gram = whole[ROWS:, 0 : 2 * NEW] + nt(nn(corr_t, middle, HIGH), corr_t, HIGH)
    i = lax.broadcasted_iota(jnp.int32, (64, 128), 0)
    j = lax.broadcasted_iota(jnp.int32, (64, 128), 1)
    factor[...] = jnp.where(j == i + 64, 1.0, 0.0)
    factor[:, 0:64] = gram

    both = factor[...]
    for first in range(0, 64, 4):
        columns = [
            jnp.broadcast_to(both[:, first + n : first + n + 1], (64, 128)) for n in range(4)
        ]
        for n in range(4):
            step = first + n
            pivot = 1.0 / columns[n][step : step + 1]
            below = jnp.where(i > step, columns[n] * pivot, 0.0)
            both = both - below * both[step : step + 1]
            for m in range(n + 1, 4):
                columns[m] = columns[m] - below * columns[m][step : step + 1]
    pivots = jnp.sum(jnp.where(i == j, both, 0.0), axis=1, keepdims=True)
    root = lax.rsqrt(pivots)
    root = root * (1.5 - 0.5 * pivots * root * root)
    factor[...] = both * root
    inverse = factor[:, 64:128]
    inverse_hi, inverse_lo = split(inverse)
    corr_hi, corr_lo = split(corr_t)
    work[0:64] = -(
        nn(inverse_hi, corr_hi) + (nn(inverse_hi, corr_lo) + nn(inverse_lo, corr_hi))
    )
    theirs, own = pl.ds(NEW * other, NEW), pl.ds(NEW * band, NEW)
    prev_hi, prev_lo = split(jnp.concatenate([work[theirs], work[own]], axis=0))
    new_hi, new_lo = split(
        jnp.concatenate([factor[theirs, 64:128], factor[own, 64:128]], axis=0)
    )
    hi = jnp.concatenate([prev_hi, new_hi], axis=1)
    lo = jnp.concatenate([prev_lo, new_lo], axis=1)
    stacked = jnp.concatenate([hi, lo], axis=0)

    flat_outs = outs.reshape(NEW * KEPT * CY, CZ)
    flat_ortho = ortho.reshape(NEW * PLANES * CY, CZ)
    kept = pl.multiple_of(band * (KEPT * CY), KEPT * CY)

    def tile(k):
        return k // (CY // TILE_Y), pl.ds(
            pl.multiple_of((k % (CY // TILE_Y)) * TILE_Y, TILE_Y), TILE_Y
        )

    def send_new(k):
        plane, at = tile(k)
        return remote(
            outs.at[:, plane, at],
            ortho.at[:, KEPT * band + plane, at],
            s2.at[k], r2.at[k], partner,
        )

    def make(k, _):
        base = pl.multiple_of(k * TILE_Y, TILE_Y)
        at = pl.ds(pl.multiple_of(base * CZ, TILE_Y * CZ), TILE_Y * CZ)
        both = nn(stacked, high[:, at])
        total = both[0:64] + both[64:128] + nn(hi, low[:, at])
        for n in range(TILE_Y):
            at = slice(n * CZ, (n + 1) * CZ)
            flat_outs[pl.ds(base + n, NEW, stride=KEPT * CY), :] = total[:NEW, at]
            flat_ortho[pl.ds(kept + base + n, NEW, stride=PLANES * CY), :] = total[NEW:, at]
        send_new(k).start()

        @pl.when(jnp.logical_and(k == 3, jnp.logical_not(early)))
        def _():
            for n in range(PIECES):
                outer[n].wait_recv()
                passed[n].start()

        return 0

    lax.fori_loop(0, TILES, make, 0)

    work[...] = whole[2 * PREV :].T
    corr[...] = work[pl.ds(pl.multiple_of(PREV * band, PREV), PREV), 0 : 2 * NEW]

    inner.wait()
    for copy in passed:
        copy.wait_recv()

    def far(o, _):
        for p in range(PLANES):
            total = applied[o, p]
            for step in range(1, DEPTH + 1):
                total = total - (0.5 * coeffs[step]) * (
                    ext[o, p + DEPTH + step] + ext[o, p + DEPTH - step]
                )
            applied[o, p] = total
        return 0

    lax.fori_loop(0, ORB, far, 0)
    for copy in sent + outer + passed:
        copy.wait_send()

    @pl.when(early)
    def _():
        for copy in along_x + [back]:
            copy.wait_send()

    @pl.when(jnp.logical_not(early))
    def _():
        to_twin.wait_send()


    def finish(k, _):
        send_new(k).wait()
        return 0

    lax.fori_loop(0, TILES, finish, 0)


def hand_over(a, b, c, a_out, b_out, c_out, sems):
    copies = []
    for n in range(2):
        part = pl.ds(n * (ORB // 2), ORB // 2)
        copies.append(pltpu.make_async_copy(a.at[part], a_out.at[part], sems.at[n]))
    for n in range(4):
        part = pl.ds(n * (NEW // 4), NEW // 4)
        copies.append(pltpu.make_async_copy(c.at[part], c_out.at[part], sems.at[2 + n]))
    copies.append(pltpu.make_async_copy(b, b_out, sems.at[6]))
    for copy in copies:
        copy.start()
    for copy in copies:
        copy.wait()


def on_device(orbitals, potential, earlier, incoming):
    dma = pltpu.SemaphoreType.DMA
    any_ = pl.BlockSpec(memory_space=pl.ANY)
    shapes = (
        jax.ShapeDtypeStruct(orbitals.shape, F32),
        jax.ShapeDtypeStruct((PREV, 2 * NEW), F32),
        jax.ShapeDtypeStruct(incoming.shape, F32),
    )
    held = tuple(pltpu.VMEM(shape.shape, shape.dtype) for shape in shapes)
    in_vmem = pl.BlockSpec(memory_space=pltpu.VMEM)
    arguments = [
        pltpu.with_memory_space_constraint(a, pltpu.HBM)
        for a in (orbitals, potential, earlier, incoming)
    ]
    results = pl.pallas_call(
        kernel,
        out_shape=held,
        in_specs=[any_] * 4,
        out_specs=(in_vmem,) * 3,
        scratch_shapes=[
            pltpu.VMEM((CHUNKS, HALF_ROWS, CHUNK_Y, CZ), F32),
            pltpu.VMEM((CHUNKS, ROWS, CHUNK_Y, CZ), F32),
            pltpu.VMEM((ROWS, CELLS), BF16),
            pltpu.VMEM((ROWS, CELLS), BF16),
            pltpu.VMEM((ORB, PLANES + 2 * DEPTH, CY, CZ), F32),
            pltpu.VMEM((PLANES, CY, CZ), F32),
            pltpu.VMEM((ORB, DEPTH, CY, CZ), F32),
            pltpu.VMEM((ROWS, ROWS), F32),
            pltpu.VMEM((256, 128), F32),
            pltpu.VMEM((3, 64, 128), F32),
            pltpu.VMEM((64, 128), F32),
            pltpu.VMEM((3, 16, 128), F32),
            pltpu.VMEM((16, 128), F32),
            pltpu.VMEM((16, 128), F32),
            pltpu.VMEM((16, 128), F32),
            pltpu.VMEM((4, 16, 128), F32),
            pltpu.VMEM((64, 128), F32),
            pltpu.VMEM((256, 128), F32),
            pltpu.VMEM((128, 128), F32),
            pltpu.VMEM((64, 128), F32),
            pltpu.VMEM((NEW, KEPT, CY, CZ), F32),
            pltpu.VMEM((CZ, CZ), F32),
            pltpu.VMEM((PLANES * CY, PLANES * CY), F32),
            dma((CHUNKS,)), dma((CHUNKS,)), dma((CHUNKS, 2)), dma((CHUNKS, 2)), dma((2,)),
            dma, dma, dma((PIECES,)), dma((PIECES,)), dma((PIECES,)), dma((PIECES,)),
            dma((3,)), dma((3,)), dma((3,)), dma((3,)), dma, dma, dma((7,)), dma((4,)),
            dma((3,)), dma((3,)), dma((3,)), dma((3,)),
            dma((TILES,)), dma((TILES,)),
            pltpu.SemaphoreType.REGULAR, pltpu.SemaphoreType.REGULAR,
        ],
        compiler_params=pltpu.CompilerParams(
            collective_id=0, has_side_effects=True, vmem_limit_bytes=50 * 2**20
        ),
        cost_estimate=pl.CostEstimate(
            flops=6 * 10**9, bytes_accessed=22 * 10**6, transcendentals=0
        ),
    )(*arguments)
    return pl.pallas_call(
        hand_over,
        out_shape=shapes,
        in_specs=[any_] * 3,
        out_specs=(any_,) * 3,
        scratch_shapes=[dma((7,))],
        compiler_params=pltpu.CompilerParams(vmem_limit_bytes=50 * 2**20),
        cost_estimate=pl.CostEstimate(flops=0, bytes_accessed=13 * 10**6, transcendentals=0),
    )(*[pltpu.with_memory_space_constraint(a, pltpu.VMEM) for a in results])


def solution(mesh):
    in_specs = (
        P("band", "domain", None, None),
        P("domain", None, None),
        P("band", "domain", None, None),
        P("band", "domain", None, None),
    )
    out_specs = (P("band", "domain", None, None), P("band", None), P("band", "domain", None, None))
    return jax.shard_map(
        on_device, mesh=mesh, in_specs=in_specs, out_specs=out_specs, check_vma=False
    )
```

```python
import jax
import jax.numpy as jnp
from jax import lax
from jax.experimental import pallas as pl
from jax.experimental.pallas import tpu as pltpu
from jax.sharding import PartitionSpec as P

coeffs = (
    -5369.0 / 1800.0,
    12.0 / 7.0,
    -15.0 / 56.0,
    10.0 / 189.0,
    -1.0 / 112.0,
    2.0 / 1925.0,
    -1.0 / 16632.0,
)

MESH = pl.DeviceIdType.MESH
HIGH = lax.Precision.HIGHEST
F32 = jnp.float32
BF16 = jnp.bfloat16

ORB = 16
PREV = 64
NEW = 32
PLANES = 8
KEPT = 4
CY = 32
CZ = 128
DEPTH = 6
ROWS = 2 * PREV + 2 * NEW
HALF_ROWS = PREV + NEW
ORDER = (
    (0, PREV, 0),
    (HALF_ROWS, PREV, PREV),
    (PREV, NEW, 2 * PREV),
    (HALF_ROWS + PREV, NEW, 2 * PREV + NEW),
)
CELLS = KEPT * CY * CZ
TOTAL = 512 * CY * CZ

CHUNKS = 16
CHUNK_Y = KEPT * CY // CHUNKS
AHEAD = 2
NEAR = -(-ORB // (CHUNKS - 1))
PIECES = 4
TILES = 16
TILE_Y = KEPT * CY // TILES


def nt(a, b, precision=None):
    return lax.dot_general(
        a, b, (((1,), (1,)), ((), ())), precision=precision, preferred_element_type=F32
    )


def nn(a, b, precision=None):
    return lax.dot_general(
        a, b, (((1,), (0,)), ((), ())), precision=precision, preferred_element_type=F32
    )


def split(a):
    hi = a.astype(BF16)
    return hi, (a - hi.astype(F32)).astype(BF16)


def band_matrix(size, block, diagonal):
    i = lax.broadcasted_iota(jnp.int32, (size, size), 0)
    j = lax.broadcasted_iota(jnp.int32, (size, size), 1)
    gap = jnp.abs(i - j)
    out = jnp.where(gap == 0, diagonal, 0.0).astype(F32)
    for step in range(1, DEPTH + 1):
        out = jnp.where(gap == step, -0.5 * coeffs[step], out)
    if block != size:
        out = jnp.where(i // block == j // block, out, 0.0)
    return out


def kernel(
    orb, pot, earl, inc,
    applied, corr, ortho,
    to_give, rows, high, low, ext, potv, relay, grams, red,
    got_z, sum_z, got_y, part, twin_part, pair, got_x, whole_y, whole, work, factor, outs, band_z, band_y,
    s1, r1, l1, l2, l0,
    s_in, r_in, s_out, r_relay, s_fwd, r_out,
    sz, rz, sy, ry, s_twin, r_twin, sx, rx, sgy, rgy, sgz, rgz,
    s2, r2, go, all_in,
):
    band = lax.axis_index("band")
    domain = lax.axis_index("domain")
    core = domain % 2
    x = ((domain // 2) % 2) * 2 + band
    y = (domain // 4) % 4
    z = domain // 16
    other = 1 - band

    def device(xx, yy, zz, cc):
        return (xx % 2, ((zz * 4 + yy) * 2 + xx // 2) * 2 + cc)

    z_peers = [device(x, y, (z + d) % 4, core) for d in range(1, 4)]
    y_peers = [device(x, (y + d) % 4, z, core) for d in range(1, 4)]
    partner = (other, domain)
    twin = (band, domain + 1 - 2 * core)
    toward = 2 * core - 1
    early = (band + core + 1) % 2
    next_domain = (domain + toward + 64) % 64
    via_y = early * ((next_domain // 4) % 4) + (1 - early) * y
    via_z = early * (next_domain // 16) + (1 - early) * z
    relayer = device((x + toward + 4) % 4, via_y, via_z, 1 - core)
    from_domain = ((z * 4 + y) * 2 + ((x + toward + 4) % 4) // 2) * 2 + 1 - core
    straight = ((z * 4 + y) * 2 + ((x - toward + 4) % 4) // 2) * 2 + core
    to_domain = (early * straight + (1 - early) * (from_domain - toward) + 64) % 64
    forward = (other, to_domain)
    way = 2 * band - 1
    chip = (z * 4 + y) * 2
    to = (chip + x // 2) * 2 + band + way + 64
    to = to % 64
    chip_passer = device(
        (((to // 2) % 2) * 2 + band - way + 4) % 4, (to // 4) % 4, to // 16, 1
    )
    giver_domain = ((chip + ((x - way + 4) % 4) // 2) * 2 + band + way + 64) % 64
    chip_giver = (other, giver_domain - giver_domain % 2 + 1)
    early = early == 1

    def piece(planes, k):
        plane = planes + k // (CY // CHUNK_Y)
        at = pl.multiple_of((k % (CY // CHUNK_Y)) * CHUNK_Y, CHUNK_Y)
        return plane, pl.ds(at, CHUNK_Y)

    def stage(k):
        plane, at = piece(KEPT * other, k)
        return (
            pltpu.make_async_copy(earl.at[:, plane, at], to_give.at[k, 0:PREV], l1.at[k, 0]),
            pltpu.make_async_copy(inc.at[:, plane, at], to_give.at[k, PREV:], l1.at[k, 1]),
        )

    def own(k):
        plane, at = piece(KEPT * band, k)
        return (
            pltpu.make_async_copy(
                earl.at[:, plane, at], rows.at[k, pl.ds(HALF_ROWS * band, PREV)], l2.at[k, 0]
            ),
            pltpu.make_async_copy(
                inc.at[:, plane, at], rows.at[k, pl.ds(HALF_ROWS * band + PREV, NEW)], l2.at[k, 1]
            ),
        )

    for k in range(AHEAD):
        for copy in stage(k):
            copy.start()

    barrier = pltpu.get_barrier_semaphore()
    first, second = core == 0, core == 1

    def greet(peer):
        pl.semaphore_signal(barrier, inc=1, device_id=peer, device_id_type=MESH)

    def tell(semaphore):
        pl.semaphore_signal(semaphore, inc=1, device_id=twin, device_id_type=MESH)

    @pl.when(second)
    def _():
        greet(twin)
        greet((other, domain - 1))

    @pl.when(first)
    def _():
        greet(partner)

    @pl.when(first)
    def _():
        pl.semaphore_wait(barrier, 3)
        tell(go)

    @pl.when(second)
    def _():
        pl.semaphore_wait(go, 1)

    def remote(src, dst, send, recv, peer):
        return pltpu.make_async_remote_copy(
            src_ref=src, dst_ref=dst, send_sem=send, recv_sem=recv,
            device_id=peer, device_id_type=MESH,
        )

    def give(k):
        return remote(
            to_give.at[k], rows.at[k, pl.ds(HALF_ROWS * band, HALF_ROWS)],
            s1.at[k], r1.at[k], partner,
        )

    for k in range(AHEAD):
        for copy in stage(k):
            copy.wait()
        give(k).start()

    def fetch(k, _):
        for copy in own(k):
            copy.start()

        @pl.when(k + AHEAD < CHUNKS)
        def _():
            for copy in stage(k + AHEAD):
                copy.start()

        return 0

    @pl.when(second)
    def _():
        for d in range(1, 4):
            greet(device(x, y, (z + d) % 4, 1))
            greet(device(x, (y + d) % 4, z, 1))
            greet(device((x + d) % 4, y, z, 1))
        greet(chip_passer)
        greet(chip_giver)

    inner = remote(
        orb.at[:, pl.ds(2 * (1 - core), DEPTH)], ext.at[:, pl.ds(14 * core, DEPTH)],
        s_in, r_in, twin,
    )
    outer, passed = [], []
    for n in range(PIECES):
        some = pl.ds(n * (ORB // PIECES), ORB // PIECES)
        outer.append(
            remote(
                orb.at[some, pl.ds(2 * core, DEPTH)], relay.at[some],
                s_out.at[n], r_relay.at[n], relayer,
            )
        )
        passed.append(
            remote(
                relay.at[some], ext.at[some, pl.ds(14 * core, DEPTH)],
                s_fwd.at[n], r_out.at[n], forward,
            )
        )

    locals_ = [
        pltpu.make_async_copy(orb, ext.at[:, pl.ds(DEPTH, PLANES)], l0.at[0]),
        pltpu.make_async_copy(pot, potv, l0.at[1]),
    ]
    for copy in locals_:
        copy.start()
    lax.fori_loop(0, CHUNKS, fetch, 0)
    inner.start()

    band_z[...] = band_matrix(CZ, CZ, -1.5 * coeffs[0])
    band_y[...] = band_matrix(PLANES * CY, CY, 0.0)
    for copy in locals_:
        copy.wait()

    def near(o, _):
        cells = ext[o, DEPTH : DEPTH + PLANES].reshape(PLANES * CY, CZ)
        field = potv[...].reshape(PLANES * CY, CZ)
        total = field * cells + nn(cells, band_z[...], HIGH) + nn(band_y[...], cells, HIGH)
        applied[o] = total.reshape(PLANES, CY, CZ)
        return 0

    grams[...] = jnp.zeros_like(grams)
    flat_rows = rows.reshape(CHUNKS * ROWS * CHUNK_Y, CZ)

    def take(k, _):
        give(k).wait_recv()
        give(k).wait_send()

        @pl.when(k + AHEAD < CHUNKS)
        def _():
            for copy in stage(k + AHEAD):
                copy.wait()
            give(k + AHEAD).start()

        for copy in own(k):
            copy.wait()

        @pl.when(jnp.logical_and(k == 2, second))
        def _():
            pl.semaphore_wait(barrier, 11)
            tell(all_in)

        @pl.when(jnp.logical_and(k == 2, first))
        def _():
            pl.semaphore_wait(all_in, 1)

        @pl.when(jnp.logical_and(k == 2, early))
        def _():
            for copy in outer:
                copy.start()

        base = pl.multiple_of(k * CHUNK_Y, CHUNK_Y)
        start = pl.multiple_of(k * (ROWS * CHUNK_Y), ROWS * CHUNK_Y)
        for i in range(CHUNK_Y):
            at = pl.ds(pl.multiple_of((base + i) * CZ, CZ), CZ)
            for row, count, to in ORDER:
                hi, lo = split(
                    flat_rows[pl.ds(start + row * CHUNK_Y + i, count, stride=CHUNK_Y), :]
                )
                high[to : to + count, at] = hi
                low[to : to + count, at] = lo
        at = pl.ds(pl.multiple_of(base * CZ, CHUNK_Y * CZ), CHUNK_Y * CZ)
        hi, lo = high[:, at], low[:, at]
        grams[...] += nt(hi, hi) + nt(hi, lo) + nt(lo, hi)

        @pl.when(jnp.logical_and(k == CHUNKS - 2, jnp.logical_not(early)))
        def _():
            for copy in outer:
                copy.start()

        @pl.when(jnp.logical_and(k == CHUNKS - 2, early))
        def _():
            outer[0].wait_recv()
            passed[0].start()

        @pl.when(k < CHUNKS - 1)
        def _():
            lax.fori_loop(k * NEAR, jnp.minimum((k + 1) * NEAR, ORB), near, 0)

        return 0

    lax.fori_loop(0, CHUNKS, take, 0)

    red[0:ROWS, :] = grams[:, 0 : 2 * PREV]
    red[ROWS:, :] = jnp.zeros((2 * NEW, 2 * PREV), F32)
    red[ROWS:, 0 : 2 * NEW] = grams[2 * PREV :, 2 * PREV :]

    sent = []
    def quarter(size, index):
        return pl.ds(pl.multiple_of(size * index, size), size)

    copies = [
        remote(
            red.at[quarter(64, (z + d) % 4)], got_z.at[d - 1],
            sz.at[d - 1], rz.at[d - 1], z_peers[d - 1],
        )
        for d in range(1, 4)
    ]
    for copy in copies:
        copy.start()
    for copy in copies:
        copy.wait_recv()
    sent = sent + copies
    sum_z[...] = red[quarter(64, z)] + got_z[0] + got_z[1] + got_z[2]
    copies = [
        remote(
            sum_z.at[quarter(16, (y + d) % 4)], got_y.at[d - 1],
            sy.at[d - 1], ry.at[d - 1], y_peers[d - 1],
        )
        for d in range(1, 4)
    ]
    for copy in copies:
        copy.start()
    for copy in copies:
        copy.wait_recv()
    sent = sent + copies
    part[...] = sum_z[quarter(16, y)] + got_y[0] + got_y[1] + got_y[2]
    to_twin = remote(part, twin_part, s_twin, r_twin, twin)
    along_x = [
        remote(
            pair, got_x.at[x], sx.at[2 * d + c], rx.at[d],
            device((x + d + 1) % 4, y, z, c),
        )
        for d in range(3)
        for c in range(2)
    ]
    back = remote(pair, got_x.at[x], sx.at[6], rx.at[3], twin)

    @pl.when(jnp.logical_not(early))
    def _():
        to_twin.start()

    @pl.when(early)
    def _():
        to_twin.wait_recv()
        pair[...] = part[...] + twin_part[...]
        for copy in along_x:
            copy.start()
        back.start()
        for n in range(1, PIECES):
            outer[n].wait_recv()
            passed[n].start()
        got_x[x] = pair[...]

    @pl.when(jnp.logical_not(early))
    def _():
        back.wait_recv()

    for copy in along_x[::2]:
        copy.wait_recv()
    total = got_x[0]
    for d in range(1, 4):
        total = total + got_x[d]
    whole_y[quarter(16, y)] = total * (1.0 / TOTAL)
    copies = [
        remote(
            whole_y.at[quarter(16, y)], whole_y.at[quarter(16, y)],
            sgy.at[d - 1], rgy.at[d - 1], y_peers[d - 1],
        )
        for d in range(1, 4)
    ]
    for copy in copies:
        copy.start()
    for copy in copies:
        copy.wait_recv()
    sent = sent + copies
    whole[quarter(64, z)] = whole_y[...]
    copies = [
        remote(
            whole_y, whole.at[quarter(64, z)], sgz.at[d - 1], rgz.at[d - 1], z_peers[d - 1]
        )
        for d in range(1, 4)
    ]
    for copy in copies:
        copy.start()
    for copy in copies:
        copy.wait_recv()
    sent = sent + copies

    corr_t = whole[2 * PREV : 2 * PREV + 2 * NEW]
    i = lax.broadcasted_iota(jnp.int32, (128, 128), 0)
    j = lax.broadcasted_iota(jnp.int32, (128, 128), 1)
    middle = whole[0 : 2 * PREV] - jnp.where(i == j, 2.0, 0.0)
    gram = whole[ROWS:, 0 : 2 * NEW] + nt(nn(corr_t, middle, HIGH), corr_t, HIGH)
    i = lax.broadcasted_iota(jnp.int32, (64, 128), 0)
    j = lax.broadcasted_iota(jnp.int32, (64, 128), 1)
    factor[...] = jnp.where(j == i + 64, 1.0, 0.0)
    factor[:, 0:64] = gram

    both = factor[...]
    for first in range(0, 64, 4):
        columns = [
            jnp.broadcast_to(both[:, first + n : first + n + 1], (64, 128)) for n in range(4)
        ]
        for n in range(4):
            step = first + n
            pivot = 1.0 / columns[n][step : step + 1]
            below = jnp.where(i > step, columns[n] * pivot, 0.0)
            both = both - below * both[step : step + 1]
            for m in range(n + 1, 4):
                columns[m] = columns[m] - below * columns[m][step : step + 1]
    pivots = jnp.sum(jnp.where(i == j, both, 0.0), axis=1, keepdims=True)
    root = lax.rsqrt(pivots)
    root = root * (1.5 - 0.5 * pivots * root * root)
    factor[...] = both * root
    inverse = factor[:, 64:128]
    inverse_hi, inverse_lo = split(inverse)
    corr_hi, corr_lo = split(corr_t)
    work[0:64] = -(
        nn(inverse_hi, corr_hi) + (nn(inverse_hi, corr_lo) + nn(inverse_lo, corr_hi))
    )
    theirs, own = pl.ds(NEW * other, NEW), pl.ds(NEW * band, NEW)
    prev_hi, prev_lo = split(jnp.concatenate([work[theirs], work[own]], axis=0))
    new_hi, new_lo = split(
        jnp.concatenate([factor[theirs, 64:128], factor[own, 64:128]], axis=0)
    )
    hi = jnp.concatenate([prev_hi, new_hi], axis=1)
    lo = jnp.concatenate([prev_lo, new_lo], axis=1)
    stacked = jnp.concatenate([hi, lo], axis=0)

    flat_outs = outs.reshape(NEW * KEPT * CY, CZ)
    flat_ortho = ortho.reshape(NEW * PLANES * CY, CZ)
    kept = pl.multiple_of(band * (KEPT * CY), KEPT * CY)

    def tile(k):
        return k // (CY // TILE_Y), pl.ds(
            pl.multiple_of((k % (CY // TILE_Y)) * TILE_Y, TILE_Y), TILE_Y
        )

    def send_new(k):
        plane, at = tile(k)
        return remote(
            outs.at[:, plane, at],
            ortho.at[:, KEPT * band + plane, at],
            s2.at[k], r2.at[k], partner,
        )

    def make(k, _):
        base = pl.multiple_of(k * TILE_Y, TILE_Y)
        at = pl.ds(pl.multiple_of(base * CZ, TILE_Y * CZ), TILE_Y * CZ)
        both = nn(stacked, high[:, at])
        total = both[0:64] + both[64:128] + nn(hi, low[:, at])
        for n in range(TILE_Y):
            at = slice(n * CZ, (n + 1) * CZ)
            flat_outs[pl.ds(base + n, NEW, stride=KEPT * CY), :] = total[:NEW, at]
            flat_ortho[pl.ds(kept + base + n, NEW, stride=PLANES * CY), :] = total[NEW:, at]
        send_new(k).start()

        @pl.when(jnp.logical_and(k == 3, jnp.logical_not(early)))
        def _():
            for n in range(PIECES):
                outer[n].wait_recv()
                passed[n].start()

        return 0

    lax.fori_loop(0, TILES, make, 0)

    work[...] = whole[2 * PREV :].T
    corr[...] = work[pl.ds(pl.multiple_of(PREV * band, PREV), PREV), 0 : 2 * NEW]

    inner.wait()
    for copy in passed:
        copy.wait_recv()

    def far(o, _):
        for p in range(PLANES):
            total = applied[o, p]
            for step in range(1, DEPTH + 1):
                total = total - (0.5 * coeffs[step]) * (
                    ext[o, p + DEPTH + step] + ext[o, p + DEPTH - step]
                )
            applied[o, p] = total
        return 0

    lax.fori_loop(0, ORB, far, 0)
    for copy in sent + outer + passed:
        copy.wait_send()

    @pl.when(early)
    def _():
        for copy in along_x + [back]:
            copy.wait_send()

    @pl.when(jnp.logical_not(early))
    def _():
        to_twin.wait_send()


    def finish(k, _):
        send_new(k).wait()
        return 0

    lax.fori_loop(0, TILES, finish, 0)


def hand_over(a, b, c, a_out, b_out, c_out, sems):
    copies = []
    for n in range(2):
        part = pl.ds(n * (ORB // 2), ORB // 2)
        copies.append(pltpu.make_async_copy(a.at[part], a_out.at[part], sems.at[n]))
    for n in range(4):
        part = pl.ds(n * (NEW // 4), NEW // 4)
        copies.append(pltpu.make_async_copy(c.at[part], c_out.at[part], sems.at[2 + n]))
    copies.append(pltpu.make_async_copy(b, b_out, sems.at[6]))
    for copy in copies:
        copy.start()
    for copy in copies:
        copy.wait()


def on_device(orbitals, potential, earlier, incoming):
    dma = pltpu.SemaphoreType.DMA
    any_ = pl.BlockSpec(memory_space=pl.ANY)
    shapes = (
        jax.ShapeDtypeStruct(orbitals.shape, F32),
        jax.ShapeDtypeStruct((PREV, 2 * NEW), F32),
        jax.ShapeDtypeStruct(incoming.shape, F32),
    )
    held = tuple(pltpu.VMEM(shape.shape, shape.dtype) for shape in shapes)
    in_vmem = pl.BlockSpec(memory_space=pltpu.VMEM)
    arguments = [
        pltpu.with_memory_space_constraint(a, pltpu.HBM)
        for a in (orbitals, potential, earlier, incoming)
    ]
    results = pl.pallas_call(
        kernel,
        out_shape=held,
        in_specs=[any_] * 4,
        out_specs=(in_vmem,) * 3,
        scratch_shapes=[
            pltpu.VMEM((CHUNKS, HALF_ROWS, CHUNK_Y, CZ), F32),
            pltpu.VMEM((CHUNKS, ROWS, CHUNK_Y, CZ), F32),
            pltpu.VMEM((ROWS, CELLS), BF16),
            pltpu.VMEM((ROWS, CELLS), BF16),
            pltpu.VMEM((ORB, PLANES + 2 * DEPTH, CY, CZ), F32),
            pltpu.VMEM((PLANES, CY, CZ), F32),
            pltpu.VMEM((ORB, DEPTH, CY, CZ), F32),
            pltpu.VMEM((ROWS, ROWS), F32),
            pltpu.VMEM((256, 128), F32),
            pltpu.VMEM((3, 64, 128), F32),
            pltpu.VMEM((64, 128), F32),
            pltpu.VMEM((3, 16, 128), F32),
            pltpu.VMEM((16, 128), F32),
            pltpu.VMEM((16, 128), F32),
            pltpu.VMEM((16, 128), F32),
            pltpu.VMEM((4, 16, 128), F32),
            pltpu.VMEM((64, 128), F32),
            pltpu.VMEM((256, 128), F32),
            pltpu.VMEM((128, 128), F32),
            pltpu.VMEM((64, 128), F32),
            pltpu.VMEM((NEW, KEPT, CY, CZ), F32),
            pltpu.VMEM((CZ, CZ), F32),
            pltpu.VMEM((PLANES * CY, PLANES * CY), F32),
            dma((CHUNKS,)), dma((CHUNKS,)), dma((CHUNKS, 2)), dma((CHUNKS, 2)), dma((2,)),
            dma, dma, dma((PIECES,)), dma((PIECES,)), dma((PIECES,)), dma((PIECES,)),
            dma((3,)), dma((3,)), dma((3,)), dma((3,)), dma, dma, dma((7,)), dma((4,)),
            dma((3,)), dma((3,)), dma((3,)), dma((3,)),
            dma((TILES,)), dma((TILES,)),
            pltpu.SemaphoreType.REGULAR, pltpu.SemaphoreType.REGULAR,
        ],
        compiler_params=pltpu.CompilerParams(
            collective_id=0, has_side_effects=True, vmem_limit_bytes=50 * 2**20
        ),
        cost_estimate=pl.CostEstimate(
            flops=6 * 10**9, bytes_accessed=22 * 10**6, transcendentals=0
        ),
    )(*arguments)
    return pl.pallas_call(
        hand_over,
        out_shape=shapes,
        in_specs=[any_] * 3,
        out_specs=(any_,) * 3,
        scratch_shapes=[dma((7,))],
        compiler_params=pltpu.CompilerParams(vmem_limit_bytes=50 * 2**20),
        cost_estimate=pl.CostEstimate(flops=0, bytes_accessed=13 * 10**6, transcendentals=0),
    )(*[pltpu.with_memory_space_constraint(a, pltpu.VMEM) for a in results])


def solution(mesh):
    in_specs = (
        P("band", "domain", None, None),
        P("domain", None, None),
        P("band", "domain", None, None),
        P("band", "domain", None, None),
    )
    out_specs = (P("band", "domain", None, None), P("band", None), P("band", "domain", None, None))
    return jax.shard_map(
        on_device, mesh=mesh, in_specs=in_specs, out_specs=out_specs, check_vma=False
    )
```

```python
import jax
import jax.numpy as jnp
from jax import lax
from jax.experimental import pallas as pl
from jax.experimental.pallas import tpu as pltpu
from jax.sharding import PartitionSpec as P

coeffs = (
    -5369.0 / 1800.0,
    12.0 / 7.0,
    -15.0 / 56.0,
    10.0 / 189.0,
    -1.0 / 112.0,
    2.0 / 1925.0,
    -1.0 / 16632.0,
)

MESH = pl.DeviceIdType.MESH
HIGH = lax.Precision.HIGHEST
F32 = jnp.float32
BF16 = jnp.bfloat16

ORB = 16
PREV = 64
NEW = 32
PLANES = 8
KEPT = 4
CY = 32
CZ = 128
DEPTH = 6
ROWS = 2 * PREV + 2 * NEW
HALF_ROWS = PREV + NEW
ORDER = (
    (0, PREV, 0),
    (HALF_ROWS, PREV, PREV),
    (PREV, NEW, 2 * PREV),
    (HALF_ROWS + PREV, NEW, 2 * PREV + NEW),
)
CELLS = KEPT * CY * CZ
TOTAL = 512 * CY * CZ

CHUNKS = 16
CHUNK_Y = KEPT * CY // CHUNKS
AHEAD = 2
NEAR = -(-ORB // (CHUNKS - 1))
PIECES = 4
TILES = 16
TILE_Y = KEPT * CY // TILES


def nt(a, b, precision=None):
    return lax.dot_general(
        a, b, (((1,), (1,)), ((), ())), precision=precision, preferred_element_type=F32
    )


def nn(a, b, precision=None):
    return lax.dot_general(
        a, b, (((1,), (0,)), ((), ())), precision=precision, preferred_element_type=F32
    )


def split(a):
    hi = a.astype(BF16)
    return hi, (a - hi.astype(F32)).astype(BF16)


def band_matrix(size, block, diagonal):
    i = lax.broadcasted_iota(jnp.int32, (size, size), 0)
    j = lax.broadcasted_iota(jnp.int32, (size, size), 1)
    gap = jnp.abs(i - j)
    out = jnp.where(gap == 0, diagonal, 0.0).astype(F32)
    for step in range(1, DEPTH + 1):
        out = jnp.where(gap == step, -0.5 * coeffs[step], out)
    if block != size:
        out = jnp.where(i // block == j // block, out, 0.0)
    return out


def kernel(
    orb, pot, earl, inc,
    applied, corr, ortho,
    to_give, rows, high, low, ext, potv, relay, grams, red,
    got_z, sum_z, got_y, part, twin_part, pair, got_x, whole_y, whole, work, factor, outs, band_z, band_y,
    s1, r1, l1, l2, l0,
    s_in, r_in, s_out, r_relay, s_fwd, r_out,
    sz, rz, sy, ry, s_twin, r_twin, sx, rx, sgy, rgy, sgz, rgz,
    s2, r2, go, all_in,
):
    band = lax.axis_index("band")
    domain = lax.axis_index("domain")
    core = domain % 2
    other = 1 - band
    partner = (other, domain)
    twin = (band, domain + 1 - 2 * core)

    def piece(planes, k):
        plane = planes + k // (CY // CHUNK_Y)
        at = pl.multiple_of((k % (CY // CHUNK_Y)) * CHUNK_Y, CHUNK_Y)
        return plane, pl.ds(at, CHUNK_Y)

    def stage(k):
        plane, at = piece(KEPT * other, k)
        return (
            pltpu.make_async_copy(earl.at[:, plane, at], to_give.at[k, 0:PREV], l1.at[k, 0]),
            pltpu.make_async_copy(inc.at[:, plane, at], to_give.at[k, PREV:], l1.at[k, 1]),
        )

    def own(k):
        plane, at = piece(KEPT * band, k)
        return (
            pltpu.make_async_copy(
                earl.at[:, plane, at], rows.at[k, pl.ds(HALF_ROWS * band, PREV)], l2.at[k, 0]
            ),
            pltpu.make_async_copy(
                inc.at[:, plane, at], rows.at[k, pl.ds(HALF_ROWS * band + PREV, NEW)], l2.at[k, 1]
            ),
        )

    barrier = pltpu.get_barrier_semaphore()
    first, second = core == 0, core == 1

    def greet(peer):
        pl.semaphore_signal(barrier, inc=1, device_id=peer, device_id_type=MESH)

    def tell(semaphore):
        pl.semaphore_signal(semaphore, inc=1, device_id=twin, device_id_type=MESH)

    @pl.when(second)
    def _():
        greet(twin)
        greet((other, domain - 1))

    @pl.when(first)
    def _():
        greet(partner)

    for k in range(AHEAD):
        for copy in stage(k):
            copy.start()

    @pl.when(first)
    def _():
        pl.semaphore_wait(barrier, 3)
        tell(go)

    @pl.when(second)
    def _():
        pl.semaphore_wait(go, 1)

    def remote(src, dst, send, recv, peer):
        return pltpu.make_async_remote_copy(
            src_ref=src, dst_ref=dst, send_sem=send, recv_sem=recv,
            device_id=peer, device_id_type=MESH,
        )

    def give(k):
        return remote(
            to_give.at[k], rows.at[k, pl.ds(HALF_ROWS * band, HALF_ROWS)],
            s1.at[k], r1.at[k], partner,
        )

    for k in range(AHEAD):
        for copy in stage(k):
            copy.wait()
        give(k).start()

    def fetch(k, _):
        for copy in own(k):
            copy.start()

        @pl.when(k + AHEAD < CHUNKS)
        def _():
            for copy in stage(k + AHEAD):
                copy.start()

        return 0

    x = ((domain // 2) % 2) * 2 + band
    y = (domain // 4) % 4
    z = domain // 16

    def device(xx, yy, zz, cc):
        return (xx % 2, ((zz * 4 + yy) * 2 + xx // 2) * 2 + cc)

    z_peers = [device(x, y, (z + d) % 4, core) for d in range(1, 4)]
    y_peers = [device(x, (y + d) % 4, z, core) for d in range(1, 4)]
    toward = 2 * core - 1
    early = (band + core + 1) % 2
    next_domain = (domain + toward + 64) % 64
    via_y = early * ((next_domain // 4) % 4) + (1 - early) * y
    via_z = early * (next_domain // 16) + (1 - early) * z
    relayer = device((x + toward + 4) % 4, via_y, via_z, 1 - core)
    from_domain = ((z * 4 + y) * 2 + ((x + toward + 4) % 4) // 2) * 2 + 1 - core
    straight = ((z * 4 + y) * 2 + ((x - toward + 4) % 4) // 2) * 2 + core
    to_domain = (early * straight + (1 - early) * (from_domain - toward) + 64) % 64
    forward = (other, to_domain)
    way = 2 * band - 1
    chip = (z * 4 + y) * 2
    to = (chip + x // 2) * 2 + band + way + 64
    to = to % 64
    chip_passer = device(
        (((to // 2) % 2) * 2 + band - way + 4) % 4, (to // 4) % 4, to // 16, 1
    )
    giver_domain = ((chip + ((x - way + 4) % 4) // 2) * 2 + band + way + 64) % 64
    chip_giver = (other, giver_domain - giver_domain % 2 + 1)
    early = early == 1

    @pl.when(second)
    def _():
        for d in range(1, 4):
            greet(device(x, y, (z + d) % 4, 1))
            greet(device(x, (y + d) % 4, z, 1))
            greet(device((x + d) % 4, y, z, 1))
        greet(chip_passer)
        greet(chip_giver)

    inner = remote(
        orb.at[:, pl.ds(2 * (1 - core), DEPTH)], ext.at[:, pl.ds(14 * core, DEPTH)],
        s_in, r_in, twin,
    )
    outer, passed = [], []
    for n in range(PIECES):
        some = pl.ds(n * (ORB // PIECES), ORB // PIECES)
        outer.append(
            remote(
                orb.at[some, pl.ds(2 * core, DEPTH)], relay.at[some],
                s_out.at[n], r_relay.at[n], relayer,
            )
        )
        passed.append(
            remote(
                relay.at[some], ext.at[some, pl.ds(14 * core, DEPTH)],
                s_fwd.at[n], r_out.at[n], forward,
            )
        )

    locals_ = [
        pltpu.make_async_copy(orb, ext.at[:, pl.ds(DEPTH, PLANES)], l0.at[0]),
        pltpu.make_async_copy(pot, potv, l0.at[1]),
    ]
    for copy in locals_:
        copy.start()
    lax.fori_loop(0, CHUNKS, fetch, 0)
    inner.start()

    band_z[...] = band_matrix(CZ, CZ, -1.5 * coeffs[0])
    band_y[...] = band_matrix(PLANES * CY, CY, 0.0)
    for copy in locals_:
        copy.wait()

    def near(o, _):
        cells = ext[o, DEPTH : DEPTH + PLANES].reshape(PLANES * CY, CZ)
        field = potv[...].reshape(PLANES * CY, CZ)
        total = field * cells + nn(cells, band_z[...], HIGH) + nn(band_y[...], cells, HIGH)
        applied[o] = total.reshape(PLANES, CY, CZ)
        return 0

    grams[...] = jnp.zeros_like(grams)
    flat_rows = rows.reshape(CHUNKS * ROWS * CHUNK_Y, CZ)

    def take(k, _):
        give(k).wait_recv()
        give(k).wait_send()

        @pl.when(k + AHEAD < CHUNKS)
        def _():
            for copy in stage(k + AHEAD):
                copy.wait()
            give(k + AHEAD).start()

        for copy in own(k):
            copy.wait()

        @pl.when(jnp.logical_and(k == 2, second))
        def _():
            pl.semaphore_wait(barrier, 11)
            tell(all_in)

        @pl.when(jnp.logical_and(k == 2, first))
        def _():
            pl.semaphore_wait(all_in, 1)

        @pl.when(jnp.logical_and(k == 2, early))
        def _():
            for copy in outer:
                copy.start()

        @pl.when(jnp.logical_and(k == CHUNKS - 1, early))
        def _():
            outer[0].wait_recv()
            passed[0].start()

        base = pl.multiple_of(k * CHUNK_Y, CHUNK_Y)
        start = pl.multiple_of(k * (ROWS * CHUNK_Y), ROWS * CHUNK_Y)
        for i in range(CHUNK_Y):
            at = pl.ds(pl.multiple_of((base + i) * CZ, CZ), CZ)
            for row, count, to in ORDER:
                hi, lo = split(
                    flat_rows[pl.ds(start + row * CHUNK_Y + i, count, stride=CHUNK_Y), :]
                )
                high[to : to + count, at] = hi
                low[to : to + count, at] = lo
        at = pl.ds(pl.multiple_of(base * CZ, CHUNK_Y * CZ), CHUNK_Y * CZ)
        hi, lo = high[:, at], low[:, at]
        grams[...] += nt(hi, hi) + nt(hi, lo) + nt(lo, hi)

        @pl.when(jnp.logical_and(k == CHUNKS - 2, jnp.logical_not(early)))
        def _():
            for copy in outer:
                copy.start()

        @pl.when(k < CHUNKS - 1)
        def _():
            lax.fori_loop(k * NEAR, jnp.minimum((k + 1) * NEAR, ORB), near, 0)

        return 0

    lax.fori_loop(0, CHUNKS, take, 0)

    red[0:ROWS, :] = grams[:, 0 : 2 * PREV]
    red[ROWS:, :] = jnp.zeros((2 * NEW, 2 * PREV), F32)
    red[ROWS:, 0 : 2 * NEW] = grams[2 * PREV :, 2 * PREV :]

    sent = []
    def quarter(size, index):
        return pl.ds(pl.multiple_of(size * index, size), size)

    copies = [
        remote(
            red.at[quarter(64, (z + d) % 4)], got_z.at[d - 1],
            sz.at[d - 1], rz.at[d - 1], z_peers[d - 1],
        )
        for d in range(1, 4)
    ]
    for copy in copies:
        copy.start()
    for copy in copies:
        copy.wait_recv()
    sent = sent + copies
    sum_z[...] = red[quarter(64, z)] + got_z[0] + got_z[1] + got_z[2]
    copies = [
        remote(
            sum_z.at[quarter(16, (y + d) % 4)], got_y.at[d - 1],
            sy.at[d - 1], ry.at[d - 1], y_peers[d - 1],
        )
        for d in range(1, 4)
    ]
    for copy in copies:
        copy.start()
    for copy in copies:
        copy.wait_recv()
    sent = sent + copies
    part[...] = sum_z[quarter(16, y)] + got_y[0] + got_y[1] + got_y[2]
    to_twin = remote(part, twin_part, s_twin, r_twin, twin)
    along_x = [
        remote(
            pair, got_x.at[x], sx.at[2 * d + c], rx.at[d],
            device((x + d + 1) % 4, y, z, c),
        )
        for d in range(3)
        for c in range(2)
    ]
    back = remote(pair, got_x.at[x], sx.at[6], rx.at[3], twin)

    @pl.when(jnp.logical_not(early))
    def _():
        to_twin.start()

    @pl.when(early)
    def _():
        to_twin.wait_recv()
        pair[...] = part[...] + twin_part[...]
        for copy in along_x:
            copy.start()
        back.start()
        for n in range(1, PIECES):
            outer[n].wait_recv()
            passed[n].start()
        got_x[x] = pair[...]

    @pl.when(jnp.logical_not(early))
    def _():
        back.wait_recv()

    for copy in along_x[::2]:
        copy.wait_recv()
    total = got_x[0]
    for d in range(1, 4):
        total = total + got_x[d]
    whole_y[quarter(16, y)] = total * (1.0 / TOTAL)
    copies = [
        remote(
            whole_y.at[quarter(16, y)], whole_y.at[quarter(16, y)],
            sgy.at[d - 1], rgy.at[d - 1], y_peers[d - 1],
        )
        for d in range(1, 4)
    ]
    for copy in copies:
        copy.start()
    for copy in copies:
        copy.wait_recv()
    sent = sent + copies
    whole[quarter(64, z)] = whole_y[...]
    copies = [
        remote(
            whole_y, whole.at[quarter(64, z)], sgz.at[d - 1], rgz.at[d - 1], z_peers[d - 1]
        )
        for d in range(1, 4)
    ]
    for copy in copies:
        copy.start()
    for copy in copies:
        copy.wait_recv()
    sent = sent + copies

    corr_t = whole[2 * PREV : 2 * PREV + 2 * NEW]
    i = lax.broadcasted_iota(jnp.int32, (128, 128), 0)
    j = lax.broadcasted_iota(jnp.int32, (128, 128), 1)
    middle = whole[0 : 2 * PREV] - jnp.where(i == j, 2.0, 0.0)
    gram = whole[ROWS:, 0 : 2 * NEW] + nt(nn(corr_t, middle, HIGH), corr_t, HIGH)
    i = lax.broadcasted_iota(jnp.int32, (64, 128), 0)
    j = lax.broadcasted_iota(jnp.int32, (64, 128), 1)
    factor[...] = jnp.where(j == i + 64, 1.0, 0.0)
    factor[:, 0:64] = gram

    both = factor[...]
    for first in range(0, 64, 4):
        columns = [
            jnp.broadcast_to(both[:, first + n : first + n + 1], (64, 128)) for n in range(4)
        ]
        for n in range(4):
            step = first + n
            pivot = 1.0 / columns[n][step : step + 1]
            below = jnp.where(i > step, columns[n] * pivot, 0.0)
            both = both - below * both[step : step + 1]
            for m in range(n + 1, 4):
                columns[m] = columns[m] - below * columns[m][step : step + 1]
    pivots = jnp.sum(jnp.where(i == j, both, 0.0), axis=1, keepdims=True)
    root = lax.rsqrt(pivots)
    root = root * (1.5 - 0.5 * pivots * root * root)
    factor[...] = both * root
    inverse = factor[:, 64:128]
    inverse_hi, inverse_lo = split(inverse)
    corr_hi, corr_lo = split(corr_t)
    work[0:64] = -(
        nn(inverse_hi, corr_hi) + (nn(inverse_hi, corr_lo) + nn(inverse_lo, corr_hi))
    )
    theirs, own = pl.ds(NEW * other, NEW), pl.ds(NEW * band, NEW)
    prev_hi, prev_lo = split(jnp.concatenate([work[theirs], work[own]], axis=0))
    new_hi, new_lo = split(
        jnp.concatenate([factor[theirs, 64:128], factor[own, 64:128]], axis=0)
    )
    hi = jnp.concatenate([prev_hi, new_hi], axis=1)
    lo = jnp.concatenate([prev_lo, new_lo], axis=1)
    stacked = jnp.concatenate([hi, lo], axis=0)

    flat_outs = outs.reshape(NEW * KEPT * CY, CZ)
    flat_ortho = ortho.reshape(NEW * PLANES * CY, CZ)
    kept = pl.multiple_of(band * (KEPT * CY), KEPT * CY)

    def tile(k):
        return k // (CY // TILE_Y), pl.ds(
            pl.multiple_of((k % (CY // TILE_Y)) * TILE_Y, TILE_Y), TILE_Y
        )

    def send_new(k):
        plane, at = tile(k)
        return remote(
            outs.at[:, plane, at],
            ortho.at[:, KEPT * band + plane, at],
            s2.at[k], r2.at[k], partner,
        )

    def make(k, _):
        base = pl.multiple_of(k * TILE_Y, TILE_Y)
        at = pl.ds(pl.multiple_of(base * CZ, TILE_Y * CZ), TILE_Y * CZ)
        both = nn(stacked, high[:, at])
        total = both[0:64] + both[64:128] + nn(hi, low[:, at])
        for n in range(TILE_Y):
            at = slice(n * CZ, (n + 1) * CZ)
            flat_outs[pl.ds(base + n, NEW, stride=KEPT * CY), :] = total[:NEW, at]
            flat_ortho[pl.ds(kept + base + n, NEW, stride=PLANES * CY), :] = total[NEW:, at]
        send_new(k).start()

        @pl.when(jnp.logical_and(k == 3, jnp.logical_not(early)))
        def _():
            for n in range(PIECES):
                outer[n].wait_recv()
                passed[n].start()

        return 0

    lax.fori_loop(0, TILES, make, 0)

    work[...] = whole[2 * PREV :].T
    corr[...] = work[pl.ds(pl.multiple_of(PREV * band, PREV), PREV), 0 : 2 * NEW]

    inner.wait()
    for copy in passed:
        copy.wait_recv()

    def far(o, _):
        for p in range(PLANES):
            total = applied[o, p]
            for step in range(1, DEPTH + 1):
                total = total - (0.5 * coeffs[step]) * (
                    ext[o, p + DEPTH + step] + ext[o, p + DEPTH - step]
                )
            applied[o, p] = total
        return 0

    lax.fori_loop(0, ORB, far, 0)
    for copy in sent + outer + passed:
        copy.wait_send()

    @pl.when(early)
    def _():
        for copy in along_x + [back]:
            copy.wait_send()

    @pl.when(jnp.logical_not(early))
    def _():
        to_twin.wait_send()


    def finish(k, _):
        send_new(k).wait()
        return 0

    lax.fori_loop(0, TILES, finish, 0)


def hand_over(a, b, c, a_out, b_out, c_out, sems):
    copies = []
    for n in range(2):
        part = pl.ds(n * (ORB // 2), ORB // 2)
        copies.append(pltpu.make_async_copy(a.at[part], a_out.at[part], sems.at[n]))
    for n in range(4):
        part = pl.ds(n * (NEW // 4), NEW // 4)
        copies.append(pltpu.make_async_copy(c.at[part], c_out.at[part], sems.at[2 + n]))
    copies.append(pltpu.make_async_copy(b, b_out, sems.at[6]))
    for copy in copies:
        copy.start()
    for copy in copies:
        copy.wait()


def on_device(orbitals, potential, earlier, incoming):
    dma = pltpu.SemaphoreType.DMA
    any_ = pl.BlockSpec(memory_space=pl.ANY)
    shapes = (
        jax.ShapeDtypeStruct(orbitals.shape, F32),
        jax.ShapeDtypeStruct((PREV, 2 * NEW), F32),
        jax.ShapeDtypeStruct(incoming.shape, F32),
    )
    held = tuple(pltpu.VMEM(shape.shape, shape.dtype) for shape in shapes)
    in_vmem = pl.BlockSpec(memory_space=pltpu.VMEM)
    arguments = [
        pltpu.with_memory_space_constraint(a, pltpu.HBM)
        for a in (orbitals, potential, earlier, incoming)
    ]
    results = pl.pallas_call(
        kernel,
        out_shape=held,
        in_specs=[any_] * 4,
        out_specs=(in_vmem,) * 3,
        scratch_shapes=[
            pltpu.VMEM((CHUNKS, HALF_ROWS, CHUNK_Y, CZ), F32),
            pltpu.VMEM((CHUNKS, ROWS, CHUNK_Y, CZ), F32),
            pltpu.VMEM((ROWS, CELLS), BF16),
            pltpu.VMEM((ROWS, CELLS), BF16),
            pltpu.VMEM((ORB, PLANES + 2 * DEPTH, CY, CZ), F32),
            pltpu.VMEM((PLANES, CY, CZ), F32),
            pltpu.VMEM((ORB, DEPTH, CY, CZ), F32),
            pltpu.VMEM((ROWS, ROWS), F32),
            pltpu.VMEM((256, 128), F32),
            pltpu.VMEM((3, 64, 128), F32),
            pltpu.VMEM((64, 128), F32),
            pltpu.VMEM((3, 16, 128), F32),
            pltpu.VMEM((16, 128), F32),
            pltpu.VMEM((16, 128), F32),
            pltpu.VMEM((16, 128), F32),
            pltpu.VMEM((4, 16, 128), F32),
            pltpu.VMEM((64, 128), F32),
            pltpu.VMEM((256, 128), F32),
            pltpu.VMEM((128, 128), F32),
            pltpu.VMEM((64, 128), F32),
            pltpu.VMEM((NEW, KEPT, CY, CZ), F32),
            pltpu.VMEM((CZ, CZ), F32),
            pltpu.VMEM((PLANES * CY, PLANES * CY), F32),
            dma((CHUNKS,)), dma((CHUNKS,)), dma((CHUNKS, 2)), dma((CHUNKS, 2)), dma((2,)),
            dma, dma, dma((PIECES,)), dma((PIECES,)), dma((PIECES,)), dma((PIECES,)),
            dma((3,)), dma((3,)), dma((3,)), dma((3,)), dma, dma, dma((7,)), dma((4,)),
            dma((3,)), dma((3,)), dma((3,)), dma((3,)),
            dma((TILES,)), dma((TILES,)),
            pltpu.SemaphoreType.REGULAR, pltpu.SemaphoreType.REGULAR,
        ],
        compiler_params=pltpu.CompilerParams(
            collective_id=0, has_side_effects=True, vmem_limit_bytes=50 * 2**20
        ),
        cost_estimate=pl.CostEstimate(
            flops=6 * 10**9, bytes_accessed=22 * 10**6, transcendentals=0
        ),
    )(*arguments)
    return pl.pallas_call(
        hand_over,
        out_shape=shapes,
        in_specs=[any_] * 3,
        out_specs=(any_,) * 3,
        scratch_shapes=[dma((7,))],
        compiler_params=pltpu.CompilerParams(vmem_limit_bytes=50 * 2**20),
        cost_estimate=pl.CostEstimate(flops=0, bytes_accessed=13 * 10**6, transcendentals=0),
    )(*[pltpu.with_memory_space_constraint(a, pltpu.VMEM) for a in results])


def solution(mesh):
    in_specs = (
        P("band", "domain", None, None),
        P("domain", None, None),
        P("band", "domain", None, None),
        P("band", "domain", None, None),
    )
    out_specs = (P("band", "domain", None, None), P("band", None), P("band", "domain", None, None))
    return jax.shard_map(
        on_device, mesh=mesh, in_specs=in_specs, out_specs=out_specs, check_vma=False
    )
```

```python
import jax
import jax.numpy as jnp
from jax import lax
from jax.experimental import pallas as pl
from jax.experimental.pallas import tpu as pltpu
from jax.sharding import PartitionSpec as P

coeffs = (
    -5369.0 / 1800.0,
    12.0 / 7.0,
    -15.0 / 56.0,
    10.0 / 189.0,
    -1.0 / 112.0,
    2.0 / 1925.0,
    -1.0 / 16632.0,
)

MESH = pl.DeviceIdType.MESH
HIGH = lax.Precision.HIGHEST
F32 = jnp.float32
BF16 = jnp.bfloat16

ORB = 16
PREV = 64
NEW = 32
PLANES = 8
KEPT = 4
CY = 32
CZ = 128
DEPTH = 6
ROWS = 2 * PREV + 2 * NEW
HALF_ROWS = PREV + NEW
ORDER = (
    (0, PREV, 0),
    (HALF_ROWS, PREV, PREV),
    (PREV, NEW, 2 * PREV),
    (HALF_ROWS + PREV, NEW, 2 * PREV + NEW),
)
CELLS = KEPT * CY * CZ
TOTAL = 512 * CY * CZ

CHUNKS = 16
CHUNK_Y = KEPT * CY // CHUNKS
AHEAD = 2
NEAR = -(-ORB // (CHUNKS - 1))
PIECES = 4
TILES = 16
TILE_Y = KEPT * CY // TILES


def nt(a, b, precision=None):
    return lax.dot_general(
        a, b, (((1,), (1,)), ((), ())), precision=precision, preferred_element_type=F32
    )


def nn(a, b, precision=None):
    return lax.dot_general(
        a, b, (((1,), (0,)), ((), ())), precision=precision, preferred_element_type=F32
    )


def split(a):
    hi = a.astype(BF16)
    return hi, (a - hi.astype(F32)).astype(BF16)


def band_matrix(size, block, diagonal):
    i = lax.broadcasted_iota(jnp.int32, (size, size), 0)
    j = lax.broadcasted_iota(jnp.int32, (size, size), 1)
    gap = jnp.abs(i - j)
    out = jnp.where(gap == 0, diagonal, 0.0).astype(F32)
    for step in range(1, DEPTH + 1):
        out = jnp.where(gap == step, -0.5 * coeffs[step], out)
    if block != size:
        out = jnp.where(i // block == j // block, out, 0.0)
    return out


def kernel(
    orb, pot, earl, inc,
    applied, corr, ortho,
    to_give, rows, high, low, ext, potv, relay, grams, red,
    got_z, sum_z, got_y, part, twin_part, pair, got_x, whole_y, whole, work, factor, outs, band_z, band_y,
    s1, r1, l1, l2, l0,
    s_in, r_in, s_out, r_relay, s_fwd, r_out,
    sz, rz, sy, ry, s_twin, r_twin, sx, rx, sgy, rgy, sgz, rgz,
    s2, r2, go, all_in,
):
    band = lax.axis_index("band")
    domain = lax.axis_index("domain")
    core = domain % 2
    x = ((domain // 2) % 2) * 2 + band
    y = (domain // 4) % 4
    z = domain // 16
    other = 1 - band

    def device(xx, yy, zz, cc):
        return (xx % 2, ((zz * 4 + yy) * 2 + xx // 2) * 2 + cc)

    z_peers = [device(x, y, (z + d) % 4, core) for d in range(1, 4)]
    y_peers = [device(x, (y + d) % 4, z, core) for d in range(1, 4)]
    partner = (other, domain)
    twin = (band, domain + 1 - 2 * core)
    toward = 2 * core - 1
    early = (band + core + 1) % 2
    next_domain = (domain + toward + 64) % 64
    via_y = early * ((next_domain // 4) % 4) + (1 - early) * y
    via_z = early * (next_domain // 16) + (1 - early) * z
    relayer = device((x + toward + 4) % 4, via_y, via_z, 1 - core)
    from_domain = ((z * 4 + y) * 2 + ((x + toward + 4) % 4) // 2) * 2 + 1 - core
    straight = ((z * 4 + y) * 2 + ((x - toward + 4) % 4) // 2) * 2 + core
    to_domain = (early * straight + (1 - early) * (from_domain - toward) + 64) % 64
    forward = (other, to_domain)
    way = 2 * band - 1
    chip = (z * 4 + y) * 2
    to = (chip + x // 2) * 2 + band + way + 64
    to = to % 64
    chip_passer = device(
        (((to // 2) % 2) * 2 + band - way + 4) % 4, (to // 4) % 4, to // 16, 1
    )
    giver_domain = ((chip + ((x - way + 4) % 4) // 2) * 2 + band + way + 64) % 64
    chip_giver = (other, giver_domain - giver_domain % 2 + 1)
    early = early == 1

    def piece(planes, k):
        plane = planes + k // (CY // CHUNK_Y)
        at = pl.multiple_of((k % (CY // CHUNK_Y)) * CHUNK_Y, CHUNK_Y)
        return plane, pl.ds(at, CHUNK_Y)

    def stage(k):
        plane, at = piece(KEPT * other, k)
        return (
            pltpu.make_async_copy(earl.at[:, plane, at], to_give.at[k, 0:PREV], l1.at[k, 0]),
            pltpu.make_async_copy(inc.at[:, plane, at], to_give.at[k, PREV:], l1.at[k, 1]),
        )

    def own(k):
        plane, at = piece(KEPT * band, k)
        return (
            pltpu.make_async_copy(
                earl.at[:, plane, at], rows.at[k, pl.ds(HALF_ROWS * band, PREV)], l2.at[k, 0]
            ),
            pltpu.make_async_copy(
                inc.at[:, plane, at], rows.at[k, pl.ds(HALF_ROWS * band + PREV, NEW)], l2.at[k, 1]
            ),
        )

    for k in range(AHEAD):
        for copy in stage(k):
            copy.start()

    barrier = pltpu.get_barrier_semaphore()
    first, second = core == 0, core == 1

    def greet(peer):
        pl.semaphore_signal(barrier, inc=1, device_id=peer, device_id_type=MESH)

    def tell(semaphore):
        pl.semaphore_signal(semaphore, inc=1, device_id=twin, device_id_type=MESH)

    @pl.when(second)
    def _():
        greet(twin)
        greet((other, domain - 1))

    @pl.when(first)
    def _():
        greet(partner)

    @pl.when(first)
    def _():
        pl.semaphore_wait(barrier, 3)
        tell(go)

    @pl.when(second)
    def _():
        pl.semaphore_wait(go, 1)

    def remote(src, dst, send, recv, peer):
        return pltpu.make_async_remote_copy(
            src_ref=src, dst_ref=dst, send_sem=send, recv_sem=recv,
            device_id=peer, device_id_type=MESH,
        )

    def give(k):
        return remote(
            to_give.at[k], rows.at[k, pl.ds(HALF_ROWS * band, HALF_ROWS)],
            s1.at[k], r1.at[k], partner,
        )

    for k in range(AHEAD):
        for copy in stage(k):
            copy.wait()
        give(k).start()

    def fetch(k, _):
        for copy in own(k):
            copy.start()

        @pl.when(k + AHEAD < CHUNKS)
        def _():
            for copy in stage(k + AHEAD):
                copy.start()

        return 0

    @pl.when(second)
    def _():
        for d in range(1, 4):
            greet(device(x, y, (z + d) % 4, 1))
            greet(device(x, (y + d) % 4, z, 1))
            greet(device((x + d) % 4, y, z, 1))
        greet(chip_passer)
        greet(chip_giver)

    inner = remote(
        orb.at[:, pl.ds(2 * (1 - core), DEPTH)], ext.at[:, pl.ds(14 * core, DEPTH)],
        s_in, r_in, twin,
    )
    outer, passed = [], []
    for n in range(PIECES):
        some = pl.ds(n * (ORB // PIECES), ORB // PIECES)
        outer.append(
            remote(
                orb.at[some, pl.ds(2 * core, DEPTH)], relay.at[some],
                s_out.at[n], r_relay.at[n], relayer,
            )
        )
        passed.append(
            remote(
                relay.at[some], ext.at[some, pl.ds(14 * core, DEPTH)],
                s_fwd.at[n], r_out.at[n], forward,
            )
        )

    locals_ = [
        pltpu.make_async_copy(orb, ext.at[:, pl.ds(DEPTH, PLANES)], l0.at[0]),
        pltpu.make_async_copy(pot, potv, l0.at[1]),
    ]
    for copy in locals_:
        copy.start()
    lax.fori_loop(0, CHUNKS, fetch, 0)
    inner.start()

    band_z[...] = band_matrix(CZ, CZ, -1.5 * coeffs[0])
    band_y[...] = band_matrix(PLANES * CY, CY, 0.0)
    for copy in locals_:
        copy.wait()

    def near(o, _):
        cells = ext[o, DEPTH : DEPTH + PLANES].reshape(PLANES * CY, CZ)
        field = potv[...].reshape(PLANES * CY, CZ)
        total = field * cells + nn(cells, band_z[...], HIGH) + nn(band_y[...], cells, HIGH)
        applied[o] = total.reshape(PLANES, CY, CZ)
        return 0

    grams[...] = jnp.zeros_like(grams)
    flat_rows = rows.reshape(CHUNKS * ROWS * CHUNK_Y, CZ)

    def take(k, _):
        give(k).wait_recv()
        give(k).wait_send()

        @pl.when(k + AHEAD < CHUNKS)
        def _():
            for copy in stage(k + AHEAD):
                copy.wait()
            give(k + AHEAD).start()

        for copy in own(k):
            copy.wait()

        @pl.when(jnp.logical_and(k == 2, second))
        def _():
            pl.semaphore_wait(barrier, 11)
            tell(all_in)

        @pl.when(jnp.logical_and(k == 2, first))
        def _():
            pl.semaphore_wait(all_in, 1)

        @pl.when(jnp.logical_and(k == 2, early))
        def _():
            for copy in outer:
                copy.start()

        @pl.when(jnp.logical_and(k == CHUNKS - 1, jnp.logical_not(early)))
        def _():
            for copy in outer[1:]:
                copy.start()

        @pl.when(jnp.logical_and(k == CHUNKS - 1, early))
        def _():
            outer[0].wait_recv()
            passed[0].start()

        base = pl.multiple_of(k * CHUNK_Y, CHUNK_Y)
        start = pl.multiple_of(k * (ROWS * CHUNK_Y), ROWS * CHUNK_Y)
        for i in range(CHUNK_Y):
            at = pl.ds(pl.multiple_of((base + i) * CZ, CZ), CZ)
            for row, count, to in ORDER:
                hi, lo = split(
                    flat_rows[pl.ds(start + row * CHUNK_Y + i, count, stride=CHUNK_Y), :]
                )
                high[to : to + count, at] = hi
                low[to : to + count, at] = lo
        at = pl.ds(pl.multiple_of(base * CZ, CHUNK_Y * CZ), CHUNK_Y * CZ)
        hi, lo = high[:, at], low[:, at]
        grams[...] += nt(hi, hi) + nt(hi, lo) + nt(lo, hi)

        @pl.when(jnp.logical_and(k == CHUNKS - 2, jnp.logical_not(early)))
        def _():
            outer[0].start()

        @pl.when(k < CHUNKS - 1)
        def _():
            lax.fori_loop(k * NEAR, jnp.minimum((k + 1) * NEAR, ORB), near, 0)

        return 0

    lax.fori_loop(0, CHUNKS, take, 0)

    red[0:ROWS, :] = grams[:, 0 : 2 * PREV]
    red[ROWS:, :] = jnp.zeros((2 * NEW, 2 * PREV), F32)
    red[ROWS:, 0 : 2 * NEW] = grams[2 * PREV :, 2 * PREV :]

    sent = []
    def quarter(size, index):
        return pl.ds(pl.multiple_of(size * index, size), size)

    copies = [
        remote(
            red.at[quarter(64, (z + d) % 4)], got_z.at[d - 1],
            sz.at[d - 1], rz.at[d - 1], z_peers[d - 1],
        )
        for d in range(1, 4)
    ]
    for copy in copies:
        copy.start()
    for copy in copies:
        copy.wait_recv()
    sent = sent + copies
    sum_z[...] = red[quarter(64, z)] + got_z[0] + got_z[1] + got_z[2]
    copies = [
        remote(
            sum_z.at[quarter(16, (y + d) % 4)], got_y.at[d - 1],
            sy.at[d - 1], ry.at[d - 1], y_peers[d - 1],
        )
        for d in range(1, 4)
    ]
    for copy in copies:
        copy.start()
    for copy in copies:
        copy.wait_recv()
    sent = sent + copies
    part[...] = sum_z[quarter(16, y)] + got_y[0] + got_y[1] + got_y[2]
    to_twin = remote(part, twin_part, s_twin, r_twin, twin)
    along_x = [
        remote(
            pair, got_x.at[x], sx.at[2 * d + c], rx.at[d],
            device((x + d + 1) % 4, y, z, c),
        )
        for d in range(3)
        for c in range(2)
    ]
    back = remote(pair, got_x.at[x], sx.at[6], rx.at[3], twin)

    @pl.when(jnp.logical_not(early))
    def _():
        to_twin.start()

    @pl.when(early)
    def _():
        to_twin.wait_recv()
        pair[...] = part[...] + twin_part[...]
        for copy in along_x:
            copy.start()
        back.start()
        for n in range(1, PIECES):
            outer[n].wait_recv()
            passed[n].start()
        got_x[x] = pair[...]

    @pl.when(jnp.logical_not(early))
    def _():
        back.wait_recv()

    for copy in along_x[::2]:
        copy.wait_recv()
    total = got_x[0]
    for d in range(1, 4):
        total = total + got_x[d]
    whole_y[quarter(16, y)] = total * (1.0 / TOTAL)
    copies = [
        remote(
            whole_y.at[quarter(16, y)], whole_y.at[quarter(16, y)],
            sgy.at[d - 1], rgy.at[d - 1], y_peers[d - 1],
        )
        for d in range(1, 4)
    ]
    for copy in copies:
        copy.start()
    for copy in copies:
        copy.wait_recv()
    sent = sent + copies
    whole[quarter(64, z)] = whole_y[...]
    copies = [
        remote(
            whole_y, whole.at[quarter(64, z)], sgz.at[d - 1], rgz.at[d - 1], z_peers[d - 1]
        )
        for d in range(1, 4)
    ]
    for copy in copies:
        copy.start()
    for copy in copies:
        copy.wait_recv()
    sent = sent + copies

    corr_t = whole[2 * PREV : 2 * PREV + 2 * NEW]
    i = lax.broadcasted_iota(jnp.int32, (128, 128), 0)
    j = lax.broadcasted_iota(jnp.int32, (128, 128), 1)
    middle = whole[0 : 2 * PREV] - jnp.where(i == j, 2.0, 0.0)
    gram = whole[ROWS:, 0 : 2 * NEW] + nt(nn(corr_t, middle, HIGH), corr_t, HIGH)
    i = lax.broadcasted_iota(jnp.int32, (64, 128), 0)
    j = lax.broadcasted_iota(jnp.int32, (64, 128), 1)
    factor[...] = jnp.where(j == i + 64, 1.0, 0.0)
    factor[:, 0:64] = gram

    both = factor[...]
    for first in range(0, 64, 4):
        columns = [
            jnp.broadcast_to(both[:, first + n : first + n + 1], (64, 128)) for n in range(4)
        ]
        for n in range(4):
            step = first + n
            pivot = 1.0 / columns[n][step : step + 1]
            below = jnp.where(i > step, columns[n] * pivot, 0.0)
            both = both - below * both[step : step + 1]
            for m in range(n + 1, 4):
                columns[m] = columns[m] - below * columns[m][step : step + 1]
    pivots = jnp.sum(jnp.where(i == j, both, 0.0), axis=1, keepdims=True)
    root = lax.rsqrt(pivots)
    root = root * (1.5 - 0.5 * pivots * root * root)
    factor[...] = both * root
    inverse = factor[:, 64:128]
    inverse_hi, inverse_lo = split(inverse)
    corr_hi, corr_lo = split(corr_t)
    work[0:64] = -(
        nn(inverse_hi, corr_hi) + (nn(inverse_hi, corr_lo) + nn(inverse_lo, corr_hi))
    )
    theirs, own = pl.ds(NEW * other, NEW), pl.ds(NEW * band, NEW)
    prev_hi, prev_lo = split(jnp.concatenate([work[theirs], work[own]], axis=0))
    new_hi, new_lo = split(
        jnp.concatenate([factor[theirs, 64:128], factor[own, 64:128]], axis=0)
    )
    hi = jnp.concatenate([prev_hi, new_hi], axis=1)
    lo = jnp.concatenate([prev_lo, new_lo], axis=1)
    stacked = jnp.concatenate([hi, lo], axis=0)

    flat_outs = outs.reshape(NEW * KEPT * CY, CZ)
    flat_ortho = ortho.reshape(NEW * PLANES * CY, CZ)
    kept = pl.multiple_of(band * (KEPT * CY), KEPT * CY)

    def tile(k):
        return k // (CY // TILE_Y), pl.ds(
            pl.multiple_of((k % (CY // TILE_Y)) * TILE_Y, TILE_Y), TILE_Y
        )

    def send_new(k):
        plane, at = tile(k)
        return remote(
            outs.at[:, plane, at],
            ortho.at[:, KEPT * band + plane, at],
            s2.at[k], r2.at[k], partner,
        )

    def make(k, _):
        base = pl.multiple_of(k * TILE_Y, TILE_Y)
        at = pl.ds(pl.multiple_of(base * CZ, TILE_Y * CZ), TILE_Y * CZ)
        both = nn(stacked, high[:, at])
        total = both[0:64] + both[64:128] + nn(hi, low[:, at])
        for n in range(TILE_Y):
            at = slice(n * CZ, (n + 1) * CZ)
            flat_outs[pl.ds(base + n, NEW, stride=KEPT * CY), :] = total[:NEW, at]
            flat_ortho[pl.ds(kept + base + n, NEW, stride=PLANES * CY), :] = total[NEW:, at]
        send_new(k).start()

        @pl.when(jnp.logical_and(k == 3, jnp.logical_not(early)))
        def _():
            for n in range(PIECES):
                outer[n].wait_recv()
                passed[n].start()

        return 0

    lax.fori_loop(0, TILES, make, 0)

    work[...] = whole[2 * PREV :].T
    corr[...] = work[pl.ds(pl.multiple_of(PREV * band, PREV), PREV), 0 : 2 * NEW]

    inner.wait()
    for copy in passed:
        copy.wait_recv()

    def far(o, _):
        for p in range(PLANES):
            total = applied[o, p]
            for step in range(1, DEPTH + 1):
                total = total - (0.5 * coeffs[step]) * (
                    ext[o, p + DEPTH + step] + ext[o, p + DEPTH - step]
                )
            applied[o, p] = total
        return 0

    lax.fori_loop(0, ORB, far, 0)
    for copy in sent + outer + passed:
        copy.wait_send()

    @pl.when(early)
    def _():
        for copy in along_x + [back]:
            copy.wait_send()

    @pl.when(jnp.logical_not(early))
    def _():
        to_twin.wait_send()


    def finish(k, _):
        send_new(k).wait()
        return 0

    lax.fori_loop(0, TILES, finish, 0)


def hand_over(a, b, c, a_out, b_out, c_out, sems):
    copies = []
    for n in range(2):
        part = pl.ds(n * (ORB // 2), ORB // 2)
        copies.append(pltpu.make_async_copy(a.at[part], a_out.at[part], sems.at[n]))
    for n in range(4):
        part = pl.ds(n * (NEW // 4), NEW // 4)
        copies.append(pltpu.make_async_copy(c.at[part], c_out.at[part], sems.at[2 + n]))
    copies.append(pltpu.make_async_copy(b, b_out, sems.at[6]))
    for copy in copies:
        copy.start()
    for copy in copies:
        copy.wait()


def on_device(orbitals, potential, earlier, incoming):
    dma = pltpu.SemaphoreType.DMA
    any_ = pl.BlockSpec(memory_space=pl.ANY)
    shapes = (
        jax.ShapeDtypeStruct(orbitals.shape, F32),
        jax.ShapeDtypeStruct((PREV, 2 * NEW), F32),
        jax.ShapeDtypeStruct(incoming.shape, F32),
    )
    held = tuple(pltpu.VMEM(shape.shape, shape.dtype) for shape in shapes)
    in_vmem = pl.BlockSpec(memory_space=pltpu.VMEM)
    arguments = [
        pltpu.with_memory_space_constraint(a, pltpu.HBM)
        for a in (orbitals, potential, earlier, incoming)
    ]
    results = pl.pallas_call(
        kernel,
        out_shape=held,
        in_specs=[any_] * 4,
        out_specs=(in_vmem,) * 3,
        scratch_shapes=[
            pltpu.VMEM((CHUNKS, HALF_ROWS, CHUNK_Y, CZ), F32),
            pltpu.VMEM((CHUNKS, ROWS, CHUNK_Y, CZ), F32),
            pltpu.VMEM((ROWS, CELLS), BF16),
            pltpu.VMEM((ROWS, CELLS), BF16),
            pltpu.VMEM((ORB, PLANES + 2 * DEPTH, CY, CZ), F32),
            pltpu.VMEM((PLANES, CY, CZ), F32),
            pltpu.VMEM((ORB, DEPTH, CY, CZ), F32),
            pltpu.VMEM((ROWS, ROWS), F32),
            pltpu.VMEM((256, 128), F32),
            pltpu.VMEM((3, 64, 128), F32),
            pltpu.VMEM((64, 128), F32),
            pltpu.VMEM((3, 16, 128), F32),
            pltpu.VMEM((16, 128), F32),
            pltpu.VMEM((16, 128), F32),
            pltpu.VMEM((16, 128), F32),
            pltpu.VMEM((4, 16, 128), F32),
            pltpu.VMEM((64, 128), F32),
            pltpu.VMEM((256, 128), F32),
            pltpu.VMEM((128, 128), F32),
            pltpu.VMEM((64, 128), F32),
            pltpu.VMEM((NEW, KEPT, CY, CZ), F32),
            pltpu.VMEM((CZ, CZ), F32),
            pltpu.VMEM((PLANES * CY, PLANES * CY), F32),
            dma((CHUNKS,)), dma((CHUNKS,)), dma((CHUNKS, 2)), dma((CHUNKS, 2)), dma((2,)),
            dma, dma, dma((PIECES,)), dma((PIECES,)), dma((PIECES,)), dma((PIECES,)),
            dma((3,)), dma((3,)), dma((3,)), dma((3,)), dma, dma, dma((7,)), dma((4,)),
            dma((3,)), dma((3,)), dma((3,)), dma((3,)),
            dma((TILES,)), dma((TILES,)),
            pltpu.SemaphoreType.REGULAR, pltpu.SemaphoreType.REGULAR,
        ],
        compiler_params=pltpu.CompilerParams(
            collective_id=0, has_side_effects=True, vmem_limit_bytes=50 * 2**20
        ),
        cost_estimate=pl.CostEstimate(
            flops=6 * 10**9, bytes_accessed=22 * 10**6, transcendentals=0
        ),
    )(*arguments)
    return pl.pallas_call(
        hand_over,
        out_shape=shapes,
        in_specs=[any_] * 3,
        out_specs=(any_,) * 3,
        scratch_shapes=[dma((7,))],
        compiler_params=pltpu.CompilerParams(vmem_limit_bytes=50 * 2**20),
        cost_estimate=pl.CostEstimate(flops=0, bytes_accessed=13 * 10**6, transcendentals=0),
    )(*[pltpu.with_memory_space_constraint(a, pltpu.VMEM) for a in results])


def solution(mesh):
    in_specs = (
        P("band", "domain", None, None),
        P("domain", None, None),
        P("band", "domain", None, None),
        P("band", "domain", None, None),
    )
    out_specs = (P("band", "domain", None, None), P("band", None), P("band", "domain", None, None))
    return jax.shard_map(
        on_device, mesh=mesh, in_specs=in_specs, out_specs=out_specs, check_vma=False
    )
```

```python
import jax
import jax.numpy as jnp
from jax import lax
from jax.experimental import pallas as pl
from jax.experimental.pallas import tpu as pltpu
from jax.sharding import PartitionSpec as P

coeffs = (
    -5369.0 / 1800.0,
    12.0 / 7.0,
    -15.0 / 56.0,
    10.0 / 189.0,
    -1.0 / 112.0,
    2.0 / 1925.0,
    -1.0 / 16632.0,
)

MESH = pl.DeviceIdType.MESH
HIGH = lax.Precision.HIGHEST
F32 = jnp.float32
BF16 = jnp.bfloat16

ORB = 16
PREV = 64
NEW = 32
PLANES = 8
KEPT = 4
CY = 32
CZ = 128
DEPTH = 6
ROWS = 2 * PREV + 2 * NEW
HALF_ROWS = PREV + NEW
ORDER = (
    (0, PREV, 0),
    (HALF_ROWS, PREV, PREV),
    (PREV, NEW, 2 * PREV),
    (HALF_ROWS + PREV, NEW, 2 * PREV + NEW),
)
CELLS = KEPT * CY * CZ
TOTAL = 512 * CY * CZ

CHUNKS = 16
CHUNK_Y = KEPT * CY // CHUNKS
AHEAD = 3
NEAR = -(-ORB // (CHUNKS - 1))
PIECES = 4
TILES = 16
TILE_Y = KEPT * CY // TILES


def nt(a, b, precision=None):
    return lax.dot_general(
        a, b, (((1,), (1,)), ((), ())), precision=precision, preferred_element_type=F32
    )


def nn(a, b, precision=None):
    return lax.dot_general(
        a, b, (((1,), (0,)), ((), ())), precision=precision, preferred_element_type=F32
    )


def split(a):
    hi = a.astype(BF16)
    return hi, (a - hi.astype(F32)).astype(BF16)


def band_matrix(size, block, diagonal):
    i = lax.broadcasted_iota(jnp.int32, (size, size), 0)
    j = lax.broadcasted_iota(jnp.int32, (size, size), 1)
    gap = jnp.abs(i - j)
    out = jnp.where(gap == 0, diagonal, 0.0).astype(F32)
    for step in range(1, DEPTH + 1):
        out = jnp.where(gap == step, -0.5 * coeffs[step], out)
    if block != size:
        out = jnp.where(i // block == j // block, out, 0.0)
    return out


def kernel(
    orb, pot, earl, inc,
    applied, corr, ortho,
    to_give, rows, high, low, ext, potv, relay, grams, red,
    got_z, sum_z, got_y, part, twin_part, pair, got_x, whole_y, whole, work, factor, outs, band_z, band_y,
    s1, r1, l1, l2, l0,
    s_in, r_in, s_out, r_relay, s_fwd, r_out,
    sz, rz, sy, ry, s_twin, r_twin, sx, rx, sgy, rgy, sgz, rgz,
    s2, r2, go, all_in,
):
    band = lax.axis_index("band")
    domain = lax.axis_index("domain")
    core = domain % 2
    x = ((domain // 2) % 2) * 2 + band
    y = (domain // 4) % 4
    z = domain // 16
    other = 1 - band

    def device(xx, yy, zz, cc):
        return (xx % 2, ((zz * 4 + yy) * 2 + xx // 2) * 2 + cc)

    z_peers = [device(x, y, (z + d) % 4, core) for d in range(1, 4)]
    y_peers = [device(x, (y + d) % 4, z, core) for d in range(1, 4)]
    partner = (other, domain)
    twin = (band, domain + 1 - 2 * core)
    toward = 2 * core - 1
    early = (band + core + 1) % 2
    next_domain = (domain + toward + 64) % 64
    via_y = early * ((next_domain // 4) % 4) + (1 - early) * y
    via_z = early * (next_domain // 16) + (1 - early) * z
    relayer = device((x + toward + 4) % 4, via_y, via_z, 1 - core)
    from_domain = ((z * 4 + y) * 2 + ((x + toward + 4) % 4) // 2) * 2 + 1 - core
    straight = ((z * 4 + y) * 2 + ((x - toward + 4) % 4) // 2) * 2 + core
    to_domain = (early * straight + (1 - early) * (from_domain - toward) + 64) % 64
    forward = (other, to_domain)
    way = 2 * band - 1
    chip = (z * 4 + y) * 2
    to = (chip + x // 2) * 2 + band + way + 64
    to = to % 64
    chip_passer = device(
        (((to // 2) % 2) * 2 + band - way + 4) % 4, (to // 4) % 4, to // 16, 1
    )
    giver_domain = ((chip + ((x - way + 4) % 4) // 2) * 2 + band + way + 64) % 64
    chip_giver = (other, giver_domain - giver_domain % 2 + 1)
    early = early == 1

    def piece(planes, k):
        plane = planes + k // (CY // CHUNK_Y)
        at = pl.multiple_of((k % (CY // CHUNK_Y)) * CHUNK_Y, CHUNK_Y)
        return plane, pl.ds(at, CHUNK_Y)

    def stage(k):
        plane, at = piece(KEPT * other, k)
        return (
            pltpu.make_async_copy(earl.at[:, plane, at], to_give.at[k, 0:PREV], l1.at[k, 0]),
            pltpu.make_async_copy(inc.at[:, plane, at], to_give.at[k, PREV:], l1.at[k, 1]),
        )

    def own(k):
        plane, at = piece(KEPT * band, k)
        return (
            pltpu.make_async_copy(
                earl.at[:, plane, at], rows.at[k, pl.ds(HALF_ROWS * band, PREV)], l2.at[k, 0]
            ),
            pltpu.make_async_copy(
                inc.at[:, plane, at], rows.at[k, pl.ds(HALF_ROWS * band + PREV, NEW)], l2.at[k, 1]
            ),
        )

    for k in range(AHEAD):
        for copy in stage(k):
            copy.start()

    barrier = pltpu.get_barrier_semaphore()
    first, second = core == 0, core == 1

    def greet(peer):
        pl.semaphore_signal(barrier, inc=1, device_id=peer, device_id_type=MESH)

    def tell(semaphore):
        pl.semaphore_signal(semaphore, inc=1, device_id=twin, device_id_type=MESH)

    @pl.when(second)
    def _():
        greet(twin)
        greet((other, domain - 1))

    @pl.when(first)
    def _():
        greet(partner)

    @pl.when(first)
    def _():
        pl.semaphore_wait(barrier, 3)
        tell(go)

    @pl.when(second)
    def _():
        pl.semaphore_wait(go, 1)

    def remote(src, dst, send, recv, peer):
        return pltpu.make_async_remote_copy(
            src_ref=src, dst_ref=dst, send_sem=send, recv_sem=recv,
            device_id=peer, device_id_type=MESH,
        )

    def give(k):
        return remote(
            to_give.at[k], rows.at[k, pl.ds(HALF_ROWS * band, HALF_ROWS)],
            s1.at[k], r1.at[k], partner,
        )

    for k in range(AHEAD):
        for copy in stage(k):
            copy.wait()
        give(k).start()

    def fetch(k, _):
        for copy in own(k):
            copy.start()

        @pl.when(k + AHEAD < CHUNKS)
        def _():
            for copy in stage(k + AHEAD):
                copy.start()

        return 0

    @pl.when(second)
    def _():
        for d in range(1, 4):
            greet(device(x, y, (z + d) % 4, 1))
            greet(device(x, (y + d) % 4, z, 1))
            greet(device((x + d) % 4, y, z, 1))
        greet(chip_passer)
        greet(chip_giver)

    inner = remote(
        orb.at[:, pl.ds(2 * (1 - core), DEPTH)], ext.at[:, pl.ds(14 * core, DEPTH)],
        s_in, r_in, twin,
    )
    outer, passed = [], []
    for n in range(PIECES):
        some = pl.ds(n * (ORB // PIECES), ORB // PIECES)
        outer.append(
            remote(
                orb.at[some, pl.ds(2 * core, DEPTH)], relay.at[some],
                s_out.at[n], r_relay.at[n], relayer,
            )
        )
        passed.append(
            remote(
                relay.at[some], ext.at[some, pl.ds(14 * core, DEPTH)],
                s_fwd.at[n], r_out.at[n], forward,
            )
        )

    locals_ = [
        pltpu.make_async_copy(orb, ext.at[:, pl.ds(DEPTH, PLANES)], l0.at[0]),
        pltpu.make_async_copy(pot, potv, l0.at[1]),
    ]
    for copy in locals_:
        copy.start()
    lax.fori_loop(0, CHUNKS, fetch, 0)
    inner.start()

    band_z[...] = band_matrix(CZ, CZ, -1.5 * coeffs[0])
    band_y[...] = band_matrix(PLANES * CY, CY, 0.0)
    for copy in locals_:
        copy.wait()

    def near(o, _):
        cells = ext[o, DEPTH : DEPTH + PLANES].reshape(PLANES * CY, CZ)
        field = potv[...].reshape(PLANES * CY, CZ)
        total = field * cells + nn(cells, band_z[...], HIGH) + nn(band_y[...], cells, HIGH)
        applied[o] = total.reshape(PLANES, CY, CZ)
        return 0

    grams[...] = jnp.zeros_like(grams)
    flat_rows = rows.reshape(CHUNKS * ROWS * CHUNK_Y, CZ)

    def take(k, _):
        give(k).wait_recv()
        give(k).wait_send()

        @pl.when(k + AHEAD < CHUNKS)
        def _():
            for copy in stage(k + AHEAD):
                copy.wait()
            give(k + AHEAD).start()

        for copy in own(k):
            copy.wait()

        @pl.when(jnp.logical_and(k == 2, second))
        def _():
            pl.semaphore_wait(barrier, 11)
            tell(all_in)

        @pl.when(jnp.logical_and(k == 2, first))
        def _():
            pl.semaphore_wait(all_in, 1)

        @pl.when(jnp.logical_and(k == 2, early))
        def _():
            for copy in outer:
                copy.start()

        @pl.when(jnp.logical_and(k == CHUNKS - 1, early))
        def _():
            outer[0].wait_recv()
            passed[0].start()

        base = pl.multiple_of(k * CHUNK_Y, CHUNK_Y)
        start = pl.multiple_of(k * (ROWS * CHUNK_Y), ROWS * CHUNK_Y)
        for i in range(CHUNK_Y):
            at = pl.ds(pl.multiple_of((base + i) * CZ, CZ), CZ)
            for row, count, to in ORDER:
                hi, lo = split(
                    flat_rows[pl.ds(start + row * CHUNK_Y + i, count, stride=CHUNK_Y), :]
                )
                high[to : to + count, at] = hi
                low[to : to + count, at] = lo
        at = pl.ds(pl.multiple_of(base * CZ, CHUNK_Y * CZ), CHUNK_Y * CZ)
        hi, lo = high[:, at], low[:, at]
        grams[...] += nt(hi, hi) + nt(hi, lo) + nt(lo, hi)

        @pl.when(jnp.logical_and(k == CHUNKS - 2, jnp.logical_not(early)))
        def _():
            for copy in outer:
                copy.start()

        @pl.when(k < CHUNKS - 1)
        def _():
            lax.fori_loop(k * NEAR, jnp.minimum((k + 1) * NEAR, ORB), near, 0)

        return 0

    lax.fori_loop(0, CHUNKS, take, 0)

    red[0:ROWS, :] = grams[:, 0 : 2 * PREV]
    red[ROWS:, :] = jnp.zeros((2 * NEW, 2 * PREV), F32)
    red[ROWS:, 0 : 2 * NEW] = grams[2 * PREV :, 2 * PREV :]

    sent = []
    def quarter(size, index):
        return pl.ds(pl.multiple_of(size * index, size), size)

    copies = [
        remote(
            red.at[quarter(64, (z + d) % 4)], got_z.at[d - 1],
            sz.at[d - 1], rz.at[d - 1], z_peers[d - 1],
        )
        for d in range(1, 4)
    ]
    for copy in copies:
        copy.start()
    for copy in copies:
        copy.wait_recv()
    sent = sent + copies
    sum_z[...] = red[quarter(64, z)] + got_z[0] + got_z[1] + got_z[2]
    copies = [
        remote(
            sum_z.at[quarter(16, (y + d) % 4)], got_y.at[d - 1],
            sy.at[d - 1], ry.at[d - 1], y_peers[d - 1],
        )
        for d in range(1, 4)
    ]
    for copy in copies:
        copy.start()
    for copy in copies:
        copy.wait_recv()
    sent = sent + copies
    part[...] = sum_z[quarter(16, y)] + got_y[0] + got_y[1] + got_y[2]
    to_twin = remote(part, twin_part, s_twin, r_twin, twin)
    along_x = [
        remote(
            pair, got_x.at[x], sx.at[2 * d + c], rx.at[d],
            device((x + d + 1) % 4, y, z, c),
        )
        for d in range(3)
        for c in range(2)
    ]
    back = remote(pair, got_x.at[x], sx.at[6], rx.at[3], twin)

    @pl.when(jnp.logical_not(early))
    def _():
        to_twin.start()

    @pl.when(early)
    def _():
        to_twin.wait_recv()
        pair[...] = part[...] + twin_part[...]
        for copy in along_x:
            copy.start()
        back.start()
        for n in range(1, PIECES):
            outer[n].wait_recv()
            passed[n].start()
        got_x[x] = pair[...]

    @pl.when(jnp.logical_not(early))
    def _():
        back.wait_recv()

    for copy in along_x[::2]:
        copy.wait_recv()
    total = got_x[0]
    for d in range(1, 4):
        total = total + got_x[d]
    whole_y[quarter(16, y)] = total * (1.0 / TOTAL)
    copies = [
        remote(
            whole_y.at[quarter(16, y)], whole_y.at[quarter(16, y)],
            sgy.at[d - 1], rgy.at[d - 1], y_peers[d - 1],
        )
        for d in range(1, 4)
    ]
    for copy in copies:
        copy.start()
    for copy in copies:
        copy.wait_recv()
    sent = sent + copies
    whole[quarter(64, z)] = whole_y[...]
    copies = [
        remote(
            whole_y, whole.at[quarter(64, z)], sgz.at[d - 1], rgz.at[d - 1], z_peers[d - 1]
        )
        for d in range(1, 4)
    ]
    for copy in copies:
        copy.start()
    for copy in copies:
        copy.wait_recv()
    sent = sent + copies

    corr_t = whole[2 * PREV : 2 * PREV + 2 * NEW]
    i = lax.broadcasted_iota(jnp.int32, (128, 128), 0)
    j = lax.broadcasted_iota(jnp.int32, (128, 128), 1)
    middle = whole[0 : 2 * PREV] - jnp.where(i == j, 2.0, 0.0)
    gram = whole[ROWS:, 0 : 2 * NEW] + nt(nn(corr_t, middle, HIGH), corr_t, HIGH)
    i = lax.broadcasted_iota(jnp.int32, (64, 128), 0)
    j = lax.broadcasted_iota(jnp.int32, (64, 128), 1)
    factor[...] = jnp.where(j == i + 64, 1.0, 0.0)
    factor[:, 0:64] = gram

    both = factor[...]
    for first in range(0, 64, 4):
        columns = [
            jnp.broadcast_to(both[:, first + n : first + n + 1], (64, 128)) for n in range(4)
        ]
        for n in range(4):
            step = first + n
            pivot = 1.0 / columns[n][step : step + 1]
            below = jnp.where(i > step, columns[n] * pivot, 0.0)
            both = both - below * both[step : step + 1]
            for m in range(n + 1, 4):
                columns[m] = columns[m] - below * columns[m][step : step + 1]
    pivots = jnp.sum(jnp.where(i == j, both, 0.0), axis=1, keepdims=True)
    root = lax.rsqrt(pivots)
    root = root * (1.5 - 0.5 * pivots * root * root)
    factor[...] = both * root
    inverse = factor[:, 64:128]
    inverse_hi, inverse_lo = split(inverse)
    corr_hi, corr_lo = split(corr_t)
    work[0:64] = -(
        nn(inverse_hi, corr_hi) + (nn(inverse_hi, corr_lo) + nn(inverse_lo, corr_hi))
    )
    theirs, own = pl.ds(NEW * other, NEW), pl.ds(NEW * band, NEW)
    prev_hi, prev_lo = split(jnp.concatenate([work[theirs], work[own]], axis=0))
    new_hi, new_lo = split(
        jnp.concatenate([factor[theirs, 64:128], factor[own, 64:128]], axis=0)
    )
    hi = jnp.concatenate([prev_hi, new_hi], axis=1)
    lo = jnp.concatenate([prev_lo, new_lo], axis=1)
    stacked = jnp.concatenate([hi, lo], axis=0)

    flat_outs = outs.reshape(NEW * KEPT * CY, CZ)
    flat_ortho = ortho.reshape(NEW * PLANES * CY, CZ)
    kept = pl.multiple_of(band * (KEPT * CY), KEPT * CY)

    def tile(k):
        return k // (CY // TILE_Y), pl.ds(
            pl.multiple_of((k % (CY // TILE_Y)) * TILE_Y, TILE_Y), TILE_Y
        )

    def send_new(k):
        plane, at = tile(k)
        return remote(
            outs.at[:, plane, at],
            ortho.at[:, KEPT * band + plane, at],
            s2.at[k], r2.at[k], partner,
        )

    def make(k, _):
        base = pl.multiple_of(k * TILE_Y, TILE_Y)
        at = pl.ds(pl.multiple_of(base * CZ, TILE_Y * CZ), TILE_Y * CZ)
        both = nn(stacked, high[:, at])
        total = both[0:64] + both[64:128] + nn(hi, low[:, at])
        for n in range(TILE_Y):
            at = slice(n * CZ, (n + 1) * CZ)
            flat_outs[pl.ds(base + n, NEW, stride=KEPT * CY), :] = total[:NEW, at]
            flat_ortho[pl.ds(kept + base + n, NEW, stride=PLANES * CY), :] = total[NEW:, at]
        send_new(k).start()

        @pl.when(jnp.logical_and(k == 3, jnp.logical_not(early)))
        def _():
            for n in range(PIECES):
                outer[n].wait_recv()
                passed[n].start()

        return 0

    lax.fori_loop(0, TILES, make, 0)

    work[...] = whole[2 * PREV :].T
    corr[...] = work[pl.ds(pl.multiple_of(PREV * band, PREV), PREV), 0 : 2 * NEW]

    inner.wait()
    for copy in passed:
        copy.wait_recv()

    def far(o, _):
        for p in range(PLANES):
            total = applied[o, p]
            for step in range(1, DEPTH + 1):
                total = total - (0.5 * coeffs[step]) * (
                    ext[o, p + DEPTH + step] + ext[o, p + DEPTH - step]
                )
            applied[o, p] = total
        return 0

    lax.fori_loop(0, ORB, far, 0)
    for copy in sent + outer + passed:
        copy.wait_send()

    @pl.when(early)
    def _():
        for copy in along_x + [back]:
            copy.wait_send()

    @pl.when(jnp.logical_not(early))
    def _():
        to_twin.wait_send()


    def finish(k, _):
        send_new(k).wait()
        return 0

    lax.fori_loop(0, TILES, finish, 0)


def hand_over(a, b, c, a_out, b_out, c_out, sems):
    copies = []
    for n in range(2):
        part = pl.ds(n * (ORB // 2), ORB // 2)
        copies.append(pltpu.make_async_copy(a.at[part], a_out.at[part], sems.at[n]))
    for n in range(4):
        part = pl.ds(n * (NEW // 4), NEW // 4)
        copies.append(pltpu.make_async_copy(c.at[part], c_out.at[part], sems.at[2 + n]))
    copies.append(pltpu.make_async_copy(b, b_out, sems.at[6]))
    for copy in copies:
        copy.start()
    for copy in copies:
        copy.wait()


def on_device(orbitals, potential, earlier, incoming):
    dma = pltpu.SemaphoreType.DMA
    any_ = pl.BlockSpec(memory_space=pl.ANY)
    shapes = (
        jax.ShapeDtypeStruct(orbitals.shape, F32),
        jax.ShapeDtypeStruct((PREV, 2 * NEW), F32),
        jax.ShapeDtypeStruct(incoming.shape, F32),
    )
    held = tuple(pltpu.VMEM(shape.shape, shape.dtype) for shape in shapes)
    in_vmem = pl.BlockSpec(memory_space=pltpu.VMEM)
    arguments = [
        pltpu.with_memory_space_constraint(a, pltpu.HBM)
        for a in (orbitals, potential, earlier, incoming)
    ]
    results = pl.pallas_call(
        kernel,
        out_shape=held,
        in_specs=[any_] * 4,
        out_specs=(in_vmem,) * 3,
        scratch_shapes=[
            pltpu.VMEM((CHUNKS, HALF_ROWS, CHUNK_Y, CZ), F32),
            pltpu.VMEM((CHUNKS, ROWS, CHUNK_Y, CZ), F32),
            pltpu.VMEM((ROWS, CELLS), BF16),
            pltpu.VMEM((ROWS, CELLS), BF16),
            pltpu.VMEM((ORB, PLANES + 2 * DEPTH, CY, CZ), F32),
            pltpu.VMEM((PLANES, CY, CZ), F32),
            pltpu.VMEM((ORB, DEPTH, CY, CZ), F32),
            pltpu.VMEM((ROWS, ROWS), F32),
            pltpu.VMEM((256, 128), F32),
            pltpu.VMEM((3, 64, 128), F32),
            pltpu.VMEM((64, 128), F32),
            pltpu.VMEM((3, 16, 128), F32),
            pltpu.VMEM((16, 128), F32),
            pltpu.VMEM((16, 128), F32),
            pltpu.VMEM((16, 128), F32),
            pltpu.VMEM((4, 16, 128), F32),
            pltpu.VMEM((64, 128), F32),
            pltpu.VMEM((256, 128), F32),
            pltpu.VMEM((128, 128), F32),
            pltpu.VMEM((64, 128), F32),
            pltpu.VMEM((NEW, KEPT, CY, CZ), F32),
            pltpu.VMEM((CZ, CZ), F32),
            pltpu.VMEM((PLANES * CY, PLANES * CY), F32),
            dma((CHUNKS,)), dma((CHUNKS,)), dma((CHUNKS, 2)), dma((CHUNKS, 2)), dma((2,)),
            dma, dma, dma((PIECES,)), dma((PIECES,)), dma((PIECES,)), dma((PIECES,)),
            dma((3,)), dma((3,)), dma((3,)), dma((3,)), dma, dma, dma((7,)), dma((4,)),
            dma((3,)), dma((3,)), dma((3,)), dma((3,)),
            dma((TILES,)), dma((TILES,)),
            pltpu.SemaphoreType.REGULAR, pltpu.SemaphoreType.REGULAR,
        ],
        compiler_params=pltpu.CompilerParams(
            collective_id=0, has_side_effects=True, vmem_limit_bytes=50 * 2**20
        ),
        cost_estimate=pl.CostEstimate(
            flops=6 * 10**9, bytes_accessed=22 * 10**6, transcendentals=0
        ),
    )(*arguments)
    return pl.pallas_call(
        hand_over,
        out_shape=shapes,
        in_specs=[any_] * 3,
        out_specs=(any_,) * 3,
        scratch_shapes=[dma((7,))],
        compiler_params=pltpu.CompilerParams(vmem_limit_bytes=50 * 2**20),
        cost_estimate=pl.CostEstimate(flops=0, bytes_accessed=13 * 10**6, transcendentals=0),
    )(*[pltpu.with_memory_space_constraint(a, pltpu.VMEM) for a in results])


def solution(mesh):
    in_specs = (
        P("band", "domain", None, None),
        P("domain", None, None),
        P("band", "domain", None, None),
        P("band", "domain", None, None),
    )
    out_specs = (P("band", "domain", None, None), P("band", None), P("band", "domain", None, None))
    return jax.shard_map(
        on_device, mesh=mesh, in_specs=in_specs, out_specs=out_specs, check_vma=False
    )
```
